128 devices in a mesh: dp: 16 (over x, y), expert: 8 (over z, core).
Axes of the slice: x: 4, y: 4, z: 4, core: 2. Of those that a mesh axis runs over, the one named last changes fastest.
Arguments:
- block_input: bfloat16 [16384, 512], P(('dp', 'expert')), may hold values from -6 to 6
- gain_one: float32 [512], replicated, may hold values from 0.5 to 1.5
- gain_two: float32 [512], replicated, may hold values from 0.5 to 1.5
- moa_router: bfloat16 [512, 8], replicated, may hold values from -0.125 to 0.125
- key_proj: bfloat16 [512, 512], replicated, may hold values from -0.25 to 0.25
- value_proj: bfloat16 [512, 512], replicated, may hold values from -0.25 to 0.25
- query_proj: bfloat16 [8, 512, 512], P('expert'), may hold values from -0.25 to 0.25
- out_proj: bfloat16 [8, 512, 512], P('expert'), may hold values from -1.5 to 1.5
- moe_router: bfloat16 [512, 8], replicated, may hold values from -0.25 to 0.25
- ffn_in: bfloat16 [8, 512, 2048], P('expert'), may hold values from -0.25 to 0.25
- ffn_out: bfloat16 [8, 2048, 512], P('expert'), may hold values from -0.1875 to 0.1875
- halt_weight: float32 [512], replicated, may hold values from -0.25 to 0.25
- depths: int32 [16384], P(('dp', 'expert')), may hold values from 1 to 3, as said below
- moa_choice: int32 [3, 16384, 4], P(None, 'dp'), may hold values from 0 to 7, all different within a row
- moe_choice: int32 [3, 16384, 2], P(None, ('dp', 'expert')), may hold values from 0 to 7, all different within a row; in each aligned block of 128 rows (0 to 127, 128 to 255, ..., all dimensions but the last counted through in order) at most 40 rows name the same one
- cotangent: bfloat16 [16384, 512], P(('dp', 'expert')), may hold values from -6 to 6
Outputs:
- block_output: float32 [16384, 512], P(('dp', 'expert'))
- grad_input: float32 [16384, 512], P(('dp', 'expert'))
- grad_gain_one: float32 [512], P(('dp', 'expert'))
- grad_gain_two: float32 [512], P(('dp', 'expert'))
- grad_moa_router: float32 [512, 8], P(('dp', 'expert'))
- grad_key_proj: float32 [512, 512], P(('dp', 'expert'))
- grad_value_proj: float32 [512, 512], P(('dp', 'expert'))
- grad_query_proj: float32 [8, 512, 512], P('expert', 'dp')
- grad_out_proj: float32 [8, 512, 512], P('expert', 'dp')
- grad_moe_router: float32 [512, 8], P(('dp', 'expert'))
- grad_ffn_in: float32 [8, 512, 2048], P('expert', 'dp')
- grad_ffn_out: float32 [8, 2048, 512], P('expert', 'dp')
- grad_halt_weight: float32 [512], P(('dp', 'expert'))
The draws below stay inside these ranges and needn't reach their ends.
Inputs may be any that keep to these rules, and one draw needn't show every extreme that they name: `depths`: at least one token has 3 steps and one has 1. `moa_choice`: each row names 4 different experts. `moe_choice`: each row names 2 different experts; in every step, among the rows of one device no expert is named by more than 40 rows, and some device reaches 40.
All inputs are finite; a program needn't handle non-finite values.
Results may differ from the reference program's by a relative error of at most 0.035.
Values may be sent and summed in bfloat16 or wider, within the bound.
No kernel may reach another device: no remote copies, remote signals or barrier semaphores. Data moves between devices by JAX's collectives and lax.ppermute only.
A program may use at most 384 MiB of HBM per device.

```python
import math
import jax
import jax.numpy as jnp
import numpy as np
from jax import lax

D = 512
HEADS = 8
HEAD = 64
FF = 2048
HD = 512
MOA_TOP = 4
MOE_TOP = 2
EXPERTS_A = 8
EXPERTS_M = 8
STEPS = 3
TOK_DEV = 128
SEQ = 1024
TOKENS = 16384
CAP = 40
N_DP = 16
N_EXPERT = 8


def draw_depths(key, part):
    key = jax.random.fold_in(key, 11)
    first_key, second_key, third_key = jax.random.split(key, 3)
    base_depths = jax.random.randint(first_key, (TOKENS,), 1, STEPS + 1)
    high_spot = jax.random.randint(second_key, (), 0, TOKENS)
    offset = jax.random.randint(third_key, (), 1, TOKENS)
    low_spot = (high_spot + offset) % TOKENS
    return base_depths.at[high_spot].set(STEPS).at[low_spot].set(1).astype(jnp.int32)


def shard_levels(stream_key, shape, cuts, least, largest):
    loudness = 1.0
    for dim, blocks in cuts:
        steps = jax.random.uniform(jax.random.fold_in(jax.random.fold_in(stream_key, 6), dim), (blocks,), jnp.float32, least / len(cuts), largest / len(cuts))
        loudness = loudness * jnp.repeat(jnp.exp(steps), shape[dim] // blocks).reshape((-1,) + (1,) * (len(shape) - 1 - dim))
    return loudness


def picks_of(own_key, rows, count, top, lift):
    ranking = jax.random.permutation(jax.random.fold_in(own_key, 1), count)
    favour = ranking
    for power in range(3):
        favour = favour * favour // count
    favour = favour * lift // count
    chance = jax.random.randint(jax.random.fold_in(own_key, 2), (rows, count), 0, 4096) + favour
    fixed_rows = jax.random.permutation(jax.random.fold_in(own_key, 3), rows)[jnp.arange(count) % rows]
    chance = jnp.where(jnp.arange(rows)[:, None] == fixed_rows[None, :], 1 << 14, chance)
    merit = chance * count + jnp.arange(count)
    return lax.top_k(merit.astype(jnp.int32), top)[1].astype(jnp.int32)


def routed_block(rng, own, number, rows, amount, top, limit, skew):
    ranking = jax.random.permutation(rng, amount)
    packed, usual = portions_of(amount, rows * top, limit, skew, True), portions_of(amount, rows * top, limit, skew, False)
    places = jnp.arange(amount)

    def named(sizes, rotation):
        used = int((sizes > 0).sum())
        fixed = max(1, used // 4)
        shifted = fixed + (places - fixed + rotation * (used - fixed)) % max(1, amount - fixed)
        return jnp.zeros((amount,), jnp.int32).at[ranking[jnp.where(places < fixed, places, shifted)]].set(jnp.asarray(sizes, jnp.int32))

    sizes = jnp.where(number % 4 == 0, named(packed, number // 4), named(usual, number - number // 4 - 1))
    mixed = jax.random.permutation(jax.random.fold_in(own, 3), amount)
    source_of, taker = mixed[0:amount // 2 * 2:2], mixed[1:amount // 2 * 2:2]
    slack = jnp.minimum(sizes[source_of] - 1, limit - sizes[taker]) // 2
    slack = jnp.where((source_of == ranking[0]) | (taker == ranking[0]) | (sizes[taker] == 0), 0, jnp.maximum(slack, 0))
    shifted = jax.random.randint(jax.random.fold_in(own, 4), (amount // 2,), 0, 1 << 20) % (slack + 1)
    sizes = sizes.at[source_of].add(-shifted).at[taker].add(shifted)
    members = jnp.searchsorted(jnp.cumsum(sizes), jnp.arange(rows * top), side="right").astype(jnp.int32)
    grid = members.reshape(top, rows).T
    grid = grid[jax.random.permutation(jax.random.fold_in(own, 1), rows)]
    rotation = jax.random.randint(jax.random.fold_in(own, 2), (rows, 1), 0, top)
    return jnp.take_along_axis(grid, (jnp.arange(top)[None, :] + rotation) % top, axis=1)


def portions_of(number_of, total, most, lean, full):
    portions = [(1 << 20) // math.isqrt(rank ** lean) + 1 for rank in range(1, number_of + 1)]
    largest = most if full else min(most, max(-(-total // number_of), total * portions[0] // sum(portions)))
    least = 1 if total - largest >= number_of - 1 else 0
    holding, spare = [largest] + [least] * (number_of - 1), total - largest - least * (number_of - 1)
    while spare > 0:
        candidates = [i for i in range(1, number_of) if holding[i] < largest] or [i for i in range(1, number_of) if holding[i] < most]
        whole, remaining = sum([portions[i] for i in candidates]), spare
        for i in candidates:
            extra = min(most - holding[i], max(1, remaining * portions[i] // whole), spare)
            holding[i] = holding[i] + extra
            spare = spare - extra
    return np.array(holding)


def noise(rng, extent, scale, most, pieces=(), kind=jnp.bfloat16):
    entries = scale * jax.random.normal(rng, extent, jnp.float32)
    if pieces:
        entries = entries * shard_levels(rng, extent, pieces, -0.22, 0.18)
    return jnp.clip(entries, -most, most).astype(kind)


def setup_inputs(seed: int = 0) -> dict:
    key_of = jax.random.split(jax.random.key(seed), 17)
    block_input = noise(key_of[0], (TOKENS, D), 1.0, 6.0, ((0, 128),))
    gain_one = jnp.clip(1.0 + 0.1 * jax.random.normal(key_of[1], (D,), jnp.float32), 0.5, 1.5)
    gain_two = jnp.clip(1.0 + 0.1 * jax.random.normal(key_of[2], (D,), jnp.float32), 0.5, 1.5)
    moa_router = noise(key_of[3], (D, EXPERTS_A), (4 * D) ** -0.5, 0.125)
    key_proj = noise(key_of[4], (D, HD), D ** -0.5, 0.25)
    value_proj = noise(key_of[5], (D, HD), D ** -0.5, 0.25)
    query_proj = noise(key_of[6], (EXPERTS_A, D, HD), D ** -0.5, 0.25, ((0, 8),))
    out_proj = noise(key_of[7], (EXPERTS_A, HD, D), (HEAD // 4) ** -0.5, 1.5, ((0, 8),))
    moe_router = noise(key_of[8], (D, EXPERTS_M), D ** -0.5, 0.25)
    ffn_in = noise(key_of[9], (EXPERTS_M, D, FF), D ** -0.5, 0.25, ((0, 8),))
    ffn_out = noise(key_of[10], (EXPERTS_M, FF, D), (FF // 2) ** -0.5, 0.1875, ((0, 8),))
    halt_weight = noise(key_of[11], (D,), D ** -0.5, 0.25, (), jnp.float32)
    depths = draw_depths(jax.random.fold_in(key_of[16], 71), 0)
    moa_choice = picks_of(key_of[13], STEPS * TOKENS, EXPERTS_A, MOA_TOP, 0).reshape((STEPS, TOKENS, MOA_TOP))
    moe_choice_keys = jax.random.split(jax.random.fold_in(key_of[14], 1), STEPS * TOKENS // TOK_DEV)
    moe_choice_turns = jax.random.permutation(jax.random.fold_in(key_of[14], 3), STEPS * TOKENS // TOK_DEV)
    moe_choice = jax.vmap(lambda own, number: routed_block(jax.random.fold_in(key_of[14], 2), own, number, TOK_DEV, EXPERTS_M, MOE_TOP, CAP, 2))(moe_choice_keys, moe_choice_turns).reshape((STEPS, TOKENS, MOE_TOP))
    cotangent = noise(key_of[15], (TOKENS, D), 1.0, 6.0, ((0, 128),))
    return {"block_input": block_input, "gain_one": gain_one, "gain_two": gain_two, "moa_router": moa_router, "key_proj": key_proj, "value_proj": value_proj, "query_proj": query_proj, "out_proj": out_proj, "moe_router": moe_router, "ffn_in": ffn_in, "ffn_out": ffn_out, "halt_weight": halt_weight, "depths": depths, "moa_choice": moa_choice, "moe_choice": moe_choice, "cotangent": cotangent}


highest = lax.Precision.HIGHEST

@jax.custom_vjp
def low(v):
    return lax.optimization_barrier(v.astype(jnp.bfloat16)).astype(jnp.float32)

@jax.custom_vjp
def low_back(v):
    return v

def low_keep(v):
    return (low(v), None)

def low_pass(kept, grad):
    return (grad,)

def back_keep(v):
    return (v, None)

def back_low(kept, grad):
    return (low(grad),)
low.defvjp(low_keep, low_pass)
low_back.defvjp(back_keep, back_low)

def rounded_both(inputs):
    return low(low_back(inputs))

def layer_norm(inputs, norm_gain):
    average = lax.optimization_barrier(jnp.mean(inputs, -1, keepdims=True))
    centred = inputs - average
    spread = lax.optimization_barrier(jnp.mean(centred * centred, -1, keepdims=True))
    return centred * lax.rsqrt(spread + 1e-05) * norm_gain

def slot_index(chosen, running, experts, capacity):
    flat_ids = chosen.reshape(-1).astype(jnp.int32)
    live_rows = jnp.repeat(running, chosen.shape[1])
    onehot = (flat_ids[:, None] == jnp.arange(experts, dtype=jnp.int32)[None, :]).astype(jnp.int32) * live_rows[:, None]
    earlier = jnp.cumsum(onehot, 0) - onehot
    position = lax.optimization_barrier(jnp.sum(earlier * onehot, -1))
    target = jnp.where(live_rows > 0, flat_ids * capacity + position, experts * capacity)
    return (target.astype(jnp.int32), live_rows)

def combine(stacked, halt_vec, depth_rows):
    remain = jnp.ones(depth_rows.shape, jnp.float32)
    output = jnp.zeros(stacked.shape[1:], jnp.float32)
    for section_index in range(stacked.shape[0]):
        halt_prob = jax.nn.sigmoid(jnp.dot(stacked[section_index], halt_vec, precision=highest))
        continues = depth_rows > section_index + 1
        stops_here = depth_rows == section_index + 1
        weight_now = jnp.where(continues, halt_prob * remain, jnp.where(stops_here, remain, 0.0))
        output = output + weight_now[:, None] * stacked[section_index]
        remain = remain * (1.0 - halt_prob)
    return output

def group_mix(items, key_proj, value_proj, query_proj, out_proj):
    row_values, moa_gates = items
    key_rows = low(jnp.dot(row_values, key_proj, precision=highest)).reshape(SEQ, HEADS, HEAD)
    value_rows = low(jnp.dot(row_values, value_proj, precision=highest)).reshape(SEQ, HEADS, HEAD)
    queries = rounded_both(jnp.einsum('sd,edf->esf', row_values, query_proj, precision=highest))
    queries = queries.reshape(EXPERTS_A, SEQ, HEADS, HEAD)
    scores = jnp.einsum('eqhd,khd->ehqk', queries, key_rows, precision=highest) * HEAD ** (-0.5)
    allowed = jnp.arange(SEQ)[None, :] <= jnp.arange(SEQ)[:, None]
    scores = low_back(jnp.where(allowed, scores, -jnp.inf))
    weights_low = low(jax.nn.softmax(scores, axis=-1))
    attended = rounded_both(jnp.einsum('ehqk,khd->eqhd', weights_low, value_rows, precision=highest))
    attended = attended.reshape(EXPERTS_A, SEQ, HD)
    projected = low_back(jnp.einsum('esf,efd->esd', attended, out_proj, precision=highest))
    return jnp.einsum('se,esd->sd', moa_gates, projected, precision=highest)

def expert_mix(row_values, chosen, running, ffn_in, ffn_out):
    room = N_DP * N_EXPERT * CAP
    target, live_rows = slot_index(chosen, running, EXPERTS_M, room)
    spread_rows = jnp.repeat(row_values, MOE_TOP, axis=0)
    buffer_rows = jnp.zeros((EXPERTS_M * room, D), jnp.float32).at[target].set(spread_rows, mode='drop')
    pre_act = low_back(jnp.einsum('ecd,edf->ecf', buffer_rows.reshape(EXPERTS_M, room, D), ffn_in, precision=highest))
    activated = low(jax.nn.gelu(pre_act, approximate=True))
    result = rounded_both(jnp.einsum('ecf,efd->ecd', activated, ffn_out, precision=highest))
    result = result.reshape(EXPERTS_M * room, D)
    picked_rows = result[jnp.minimum(target, EXPERTS_M * room - 1)]
    return (picked_rows * live_rows[:, None].astype(jnp.float32)).reshape(TOKENS, MOE_TOP, D)

def forward(block_input, gain_one, gain_two, moa_router, key_proj, value_proj, query_proj, out_proj, moe_router, ffn_in, ffn_out, halt_weight, depths, moa_choice, moe_choice):
    current = block_input
    history = []
    moa_ids = jnp.arange(EXPERTS_A, dtype=jnp.int32)
    moe_ids = jnp.arange(EXPERTS_M, dtype=jnp.int32)

    def mixer_fn(items):
        return group_mix(items, key_proj, value_proj, query_proj, out_proj)
    mixer = jax.checkpoint(mixer_fn)
    experts_fn = jax.checkpoint(expert_mix)
    for section_index in range(STEPS):
        running = (depths > section_index).astype(jnp.int32)
        normed = low(layer_norm(current, gain_one))
        chosen_moa = jnp.any(moa_choice[section_index][:, :, None] == moa_ids, axis=1)
        moa_logits = jnp.dot(normed, moa_router, precision=highest)
        moa_gates = jax.nn.softmax(jnp.where(chosen_moa, moa_logits, -jnp.inf), axis=-1)
        attention = lax.map(mixer, (normed.reshape(N_DP, SEQ, D), moa_gates.reshape(N_DP, SEQ, EXPERTS_A)))
        mixed_state = current + attention.reshape(TOKENS, D)
        normed_two = low(layer_norm(mixed_state, gain_two))
        onehot_moe = (moe_choice[section_index][:, :, None] == moe_ids).astype(jnp.float32)
        moe_logits = jnp.dot(normed_two, moe_router, precision=highest)
        moe_gates = jax.nn.softmax(lax.optimization_barrier(jnp.sum(onehot_moe * moe_logits[:, None, :], -1)), axis=-1)
        moe_rows = experts_fn(normed_two, moe_choice[section_index], running, ffn_in, ffn_out)
        moe_part = lax.optimization_barrier(jnp.sum(moe_gates[:, :, None] * moe_rows, 1))
        current = jnp.where(running[:, None] > 0, mixed_state + moe_part, current)
        history.append(current)
    return combine(jnp.stack(history), halt_weight, depths)

def reference(block_input, gain_one, gain_two, moa_router, key_proj, value_proj, query_proj, out_proj, moe_router, ffn_in, ffn_out, halt_weight, depths, moa_choice, moe_choice, cotangent):
    floats = [item.astype(jnp.float32) for item in (block_input, gain_one, gain_two, moa_router, key_proj, value_proj, query_proj, out_proj, moe_router, ffn_in, ffn_out, halt_weight)]

    def apply_block(*weights):
        return forward(*weights, depths, moa_choice, moe_choice)
    output, pullback = jax.vjp(apply_block, *floats)
    grads = pullback(cotangent.astype(jnp.float32))
    return (output, grads[0], grads[1], grads[2], grads[3], grads[4], grads[5], grads[6], grads[7], grads[8], grads[9], grads[10], grads[11])
```

```python
import functools

import jax
import jax.numpy as jnp
from jax import lax
from jax.experimental import pallas as pl
from jax.experimental.pallas import tpu as pltpu
from jax.sharding import PartitionSpec as P

F32 = jnp.float32
BF16 = jnp.bfloat16
I32 = jnp.int32

WIDTH = 512
SEQ = 1024
TOK = 128
HALF = 512
CHIPS = 4
PAIRS = 4
SLOTS = 40
SPAN = 256
FFN = 2048
UNROLL = 4
PART = 512
LANES = 128


def nn(a, b):
    return lax.dot_general(a, b, (((1,), (0,)), ((), ())), preferred_element_type=F32)


def nt(a, b):
    return lax.dot_general(a, b, (((1,), (1,)), ((), ())), preferred_element_type=F32)


def tn(a, b):
    return lax.dot_general(a, b, (((0,), (0,)), ((), ())), preferred_element_type=F32)


def iota(shape, dim):
    return lax.broadcasted_iota(I32, shape, dim)


def onehot(mask):
    return jnp.where(mask, 1.0, 0.0).astype(BF16)


def row_sum(x):
    return jnp.sum(x, -1, keepdims=True)


def norm_parts(x):
    centred = x - jnp.mean(x, -1, keepdims=True)
    rstd = lax.rsqrt(jnp.mean(centred * centred, -1, keepdims=True) + 1e-05)
    return centred * rstd, rstd


def norm_back(grad, x, gain):
    hat, rstd = norm_parts(x)
    inner = grad * gain
    out = rstd * (
        inner
        - jnp.mean(inner, -1, keepdims=True)
        - hat * jnp.mean(inner * hat, -1, keepdims=True)
    )
    return out, jnp.sum(grad * hat, 0, keepdims=True)


def column(table, index):
    return row_sum(jnp.where(iota(table.shape, 1) == index, table, 0.0))


def masked_softmax(logits, chosen):
    peak = jnp.max(jnp.where(chosen, logits, -jnp.inf), -1, keepdims=True)
    weights = jnp.where(chosen, jnp.exp(logits - peak), 0.0)
    return weights / row_sum(weights)


def named(choice, count):
    lanes = iota((choice.shape[0], LANES), 1)
    mask = lanes == choice[:, 0:1]
    for k in range(1, count):
        mask = mask | (lanes == choice[:, k : k + 1])
    return mask


def lane_of(row, lane):
    return jnp.where(iota((LANES, WIDTH), 0) == lane, row, 0.0).T


def rows_at(block):
    return pl.ds(pl.multiple_of(block * TOK, TOK), TOK)


def split_heads(pair):
    lanes = iota((1, LANES), 1)
    low = jnp.where(lanes < 64, 1.0, 0.0).astype(BF16)
    high = jnp.where(lanes < 64, 0.0, 1.0).astype(BF16)
    return jnp.concatenate([pair * low, pair * high], 0)


def join_heads(both):
    return jnp.where(iota((TOK, LANES), 1) < 64, both[:TOK], both[TOK:])


def call(name, kernel, outs, args, scratch=(), smem=(), flops=0, vmem=60, aliases=None):
    specs = [
        pl.BlockSpec(memory_space=pltpu.SMEM if i in smem else pltpu.VMEM)
        for i in range(len(args))
    ]
    moved = sum(a.size * a.dtype.itemsize for a in args) + sum(
        o.size * o.dtype.itemsize for o in outs
    )
    return pl.pallas_call(
        kernel,
        out_shape=tuple(outs),
        in_specs=specs,
        out_specs=tuple(pl.BlockSpec(memory_space=pltpu.VMEM) for _ in outs),
        scratch_shapes=list(scratch),
        input_output_aliases=aliases or {},
        compiler_params=pltpu.CompilerParams(vmem_limit_bytes=vmem * 2**20),
        cost_estimate=pl.CostEstimate(flops=flops, bytes_accessed=moved, transcendentals=0),
        name=name,
    )(*args)


def like(shape, dtype):
    return jax.ShapeDtypeStruct(shape, dtype)


ANY = pl.BlockSpec(memory_space=pl.ANY)


def copy_in(src, dst, sem):
    moving = pltpu.make_async_copy(src, dst, sem)
    moving.start()
    return moving


def call_any(name, kernel, outs, args, scratch, flops, vmem):
    moved = sum(a.size * a.dtype.itemsize for a in args) + sum(
        o.size * o.dtype.itemsize for o in outs
    )
    return pl.pallas_call(
        kernel,
        out_shape=tuple(outs),
        in_specs=[pl.BlockSpec(memory_space=pltpu.SMEM)] + [ANY] * (len(args) - 1),
        out_specs=tuple(ANY for _ in outs),
        scratch_shapes=list(scratch),
        compiler_params=pltpu.CompilerParams(vmem_limit_bytes=vmem * 2**20),
        cost_estimate=pl.CostEstimate(flops=flops, bytes_accessed=moved, transcendentals=0),
        name=name,
    )(*args)


def allowed_keys(key_pos, span, start):
    number = lax.rem(iota((span, 2 * TOK), 1), TOK) + start
    column_pos = key_pos[0:span, :]
    return jnp.concatenate([column_pos, column_pos], 1) <= number


def attend_level(span, start, keys, value_x, key_row, q_pairs, o_held, logs):
    @pl.loop(0, PAIRS, unroll=UNROLL)
    def _(i):
        pair = pl.ds(pl.multiple_of(i * LANES, LANES), LANES)
        part = nt(q_pairs[i], keys[0:span, pair])
        number = lax.rem(iota((2 * TOK, span), 0), TOK) + start
        part = jnp.where(key_row[0:1, 0:span] <= number, part, -jnp.inf)
        top = jnp.max(part, -1, keepdims=True)
        mixed = nn(jnp.exp(part - top).astype(BF16), value_x[i, 0:span, :])
        total = mixed[:, LANES : 2 * LANES]
        o_held[pl.ds(pl.multiple_of(start, TOK), TOK), pair] = join_heads(
            mixed[:, 0:LANES] / total
        ).astype(BF16)
        lanes = iota((2 * TOK, LANES), 1)
        logs[...] = jnp.where(lanes == i, top + jnp.log(total), logs[...])


def attend_kernel(*refs):
    scal = refs[0]
    same, other = refs[1:5], refs[5:9]
    sources = refs[9:19]
    outs = refs[20:24]
    rows_out, keys_out, values_out, q_out, o_out, spread_0, spread_1, lse_out, gates_out = refs[24:33]
    rows, own, keys, values, value_t = refs[33:38]
    held = refs[38:48]
    key_w, value_w, query_0, query_1, out_0, out_1, router, chosen, pos_row, pos_col = held[:10]
    key_pos = refs[48]
    queries, q_held, o_held, spread, o_spread, staged, lse, gates = refs[49:57]
    q_pairs, key_row, logs = refs[57:60]
    in_sems, row_sems, out_sems, block_sems = refs[60:64]
    query_w, out_w = (query_0, query_1), (out_0, out_1)
    blocks, chip, core = scal[0, 8], scal[0, 9], scal[0, 10]

    row_copies = []
    for hop in range(CHIPS):
        source = lax.rem(chip - hop + CHIPS, CHIPS)
        row_copies.append(
            copy_in(same[hop].at[0:TOK], rows.at[rows_at(source * 2 + core)], row_sems.at[2 * hop])
        )
        row_copies.append(
            copy_in(
                other[hop].at[0:TOK], rows.at[rows_at(source * 2 + 1 - core)], row_sems.at[2 * hop + 1]
            )
        )
    order = (0, 1, 2, 3, 6, 7, 8, 9, 4, 5)
    copies = {i: copy_in(sources[i], held[i], in_sems.at[i]) for i in order}
    key_copy = copy_in(refs[19], key_pos, in_sems.at[10])
    for moving in row_copies:
        moving.wait()
    rows_copy = copy_in(rows, rows_out, out_sems.at[0])
    for source in range(CHIPS):
        own[source * TOK : (source + 1) * TOK, :] = rows[rows_at(2 * source + core), :]
    copies[0].wait()
    copies[1].wait()

    @pl.loop(0, 4)
    def _(tile):
        at = pl.ds(pl.multiple_of(tile * 256, 256), 256)
        block = rows[at, :]
        keys[at, :] = nn(block, key_w[...]).astype(BF16)
        low = nn(block, value_w[...]).astype(BF16)
        values[at, :] = low
        for i in range(PAIRS):
            value_t[i, at, 0:LANES] = low[:, i * LANES : (i + 1) * LANES]
            value_t[i, at, LANES : 2 * LANES] = jnp.ones((256, LANES), BF16)

    keys_copy = copy_in(keys, keys_out, out_sems.at[1])
    values_copy = copy_in(values, values_out, out_sems.at[2])
    mine = own[...]
    for r in range(2):
        copies[2 + r].wait()
        full = nn(mine, query_w[r][...]).astype(BF16)
        queries[r] = full * jnp.asarray(0.125, BF16)
    copies[6].wait()
    copies[7].wait()
    weights = masked_softmax(nt(mine, router[...]), chosen[...] > 0.0)
    gates[...] = weights
    gates_copy = copy_in(gates, gates_out, out_sems.at[3])
    spread[...] = jnp.zeros_like(spread)
    copies[8].wait()
    copies[9].wait()
    key_copy.wait()
    for part in range(8):
        at = slice(part * TOK, (part + 1) * TOK)
        key_row[:, at] = key_pos[at, :].astype(F32).T[:8].astype(I32)

    @pl.loop(0, blocks)
    def _(j):
        start = j * TOK
        here = pl.ds(pl.multiple_of(start, TOK), TOK)
        take = iota((TOK, HALF), 0) + start
        packed = sum(
            nn(onehot(pos_row[r : r + 1, :] == take), queries[r]) for r in range(2)
        ).astype(BF16)
        q_held[here, :] = packed
        copy_in(q_held.at[here], q_out.at[here], block_sems.at[0, j])
        for i in range(PAIRS):
            q_pairs[i] = split_heads(packed[:, i * LANES : (i + 1) * LANES])
        for level in range(1, 5):
            pl.when(scal[0, j] == level)(
                functools.partial(
                    attend_level, level * SPAN, start, keys, value_t, key_row, q_pairs, o_held, logs
                )
            )
        lse[j] = logs[...].T[:8]
        copy_in(o_held.at[here], o_out.at[here], block_sems.at[1, j])
        block = o_held[here, :]
        put = iota((HALF, TOK), 1) + start
        for r in range(2):
            spread[r] += nn(onehot(pos_col[:, r : r + 1] == put), block)

    lse_copy = copy_in(lse, lse_out, out_sems.at[4])
    copies[4].wait()
    copies[5].wait()
    mixture = jnp.zeros((HALF, WIDTH), F32)
    for r in range(2):
        full = spread[r].astype(BF16)
        o_spread[r] = full
        expert = 2 * chip + (core if r == 0 else 1 - core)
        mixture = mixture + column(gates[...], expert) * nn(full, out_w[r][...])
    staged[...] = mixture.astype(BF16)
    final = [
        copy_in(staged.at[rows_at(lax.rem(chip + hop, CHIPS))], outs[hop], row_sems.at[hop])
        for hop in range(CHIPS)
    ]
    final.append(copy_in(o_spread.at[0], spread_0, out_sems.at[5]))
    final.append(copy_in(o_spread.at[1], spread_1, out_sems.at[6]))

    @pl.loop(0, blocks)
    def _(j):
        here = rows_at(j)
        pltpu.make_async_copy(q_held.at[here], q_out.at[here], block_sems.at[0, j]).wait()
        pltpu.make_async_copy(o_held.at[here], o_out.at[here], block_sems.at[1, j]).wait()

    for moving in [rows_copy, keys_copy, values_copy, gates_copy, lse_copy, *final]:
        moving.wait()


def attend(table, same, other, key_w, value_w, query_w, out_w, router, plan):
    outs = [like((TOK, WIDTH), BF16)] * 4 + [
        like((SEQ, WIDTH), BF16),
        like((SEQ, WIDTH), BF16),
        like((SEQ, WIDTH), BF16),
        like((SEQ, WIDTH), BF16),
        like((SEQ, WIDTH), BF16),
        like((HALF, WIDTH), BF16),
        like((HALF, WIDTH), BF16),
        like((8, 8, 2 * TOK), F32),
        like((HALF, LANES), F32),
    ]
    square = pltpu.VMEM((WIDTH, WIDTH), BF16)
    scratch = [
        pltpu.VMEM((SEQ, WIDTH), BF16),
        pltpu.VMEM((HALF, WIDTH), BF16),
        pltpu.VMEM((SEQ, WIDTH), BF16),
        pltpu.VMEM((SEQ, WIDTH), BF16),
        pltpu.VMEM((PAIRS, SEQ, 2 * LANES), BF16),
        square,
        square,
        square,
        square,
        square,
        square,
        pltpu.VMEM((LANES, WIDTH), BF16),
        pltpu.VMEM((HALF, LANES), F32),
        pltpu.VMEM((8, HALF), I32),
        pltpu.VMEM((HALF, LANES), I32),
        pltpu.VMEM((SEQ, LANES), I32),
        pltpu.VMEM((2, HALF, WIDTH), BF16),
        pltpu.VMEM((SEQ, WIDTH), BF16),
        pltpu.VMEM((SEQ, WIDTH), BF16),
        pltpu.VMEM((2, HALF, WIDTH), F32),
        pltpu.VMEM((2, HALF, WIDTH), BF16),
        pltpu.VMEM((HALF, WIDTH), BF16),
        pltpu.VMEM((8, 8, 2 * TOK), F32),
        pltpu.VMEM((HALF, LANES), F32),
        pltpu.VMEM((PAIRS, 2 * TOK, LANES), BF16),
        pltpu.VMEM((8, SEQ), I32),
        pltpu.VMEM((2 * TOK, LANES), F32),
        pltpu.SemaphoreType.DMA((11,)),
        pltpu.SemaphoreType.DMA((8,)),
        pltpu.SemaphoreType.DMA((7,)),
        pltpu.SemaphoreType.DMA((2, 8)),
    ]
    args = [
        table, *same, *other, key_w, value_w, *query_w, *out_w, router,
        plan["chosen"], plan["pos_row"], plan["pos_col"], plan["key_pos"],
    ]
    return call_any("attend", attend_kernel, outs, args, scratch, 6 * 10**9, 60)


def back_level(
    span, start, keys, values, key_pos, q_pairs, o_pairs, logs, inner, sum_k, sum_v, part_q
):
    @pl.loop(0, PAIRS, unroll=UNROLL)
    def _(i):
        pair = pl.ds(pl.multiple_of(i * LANES, LANES), LANES)
        key_block = keys[0:span, pair]
        queries, grads = q_pairs[i], o_pairs[i]
        probs = jnp.exp(nt(key_block, queries) - logs[pl.ds(i, 1), :])
        probs = jnp.where(allowed_keys(key_pos, span, start), probs, 0.0)
        grad_probs = nt(values[0:span, pair], grads)
        grad_scores = (probs * (grad_probs - inner[pl.ds(i, 1), :])).astype(BF16)
        sum_k[0:span, pair] += nn(grad_scores, queries)
        sum_v[0:span, pair] += nn(probs.astype(BF16), grads)
        part_q[i] = tn(grad_scores, key_block)


def attend_back_kernel(*refs):
    scal = refs[0]
    arrived = refs[1:5]
    sources = refs[5:26]
    same, other = refs[26:30], refs[30]
    y_out, q_out, k_out, v_out, tiny_out = refs[31:33], refs[33:35], refs[35], refs[36], refs[37]
    upstream = refs[38]
    held = refs[39:60]
    (
        out_0, out_1, gates, spread_0, spread_1, pos_row, q_held, o_held, lse, keys, values,
        key_pos, pos_col, query_0, query_1, key_w, value_w, rows, router, gain, tiny,
    ) = held
    grad_o, sum_k, sum_v, sum_q, part_q, q_pairs, o_pairs, logs, inner, own, gate_low = refs[60:71]
    grad_y, grad_q, grad_k, grad_v, same_s, other_s = refs[71:77]
    in_sems, row_sems, out_sems = refs[77:80]
    o_spread = (spread_0, spread_1)
    query_w, out_w = (query_0, query_1), (out_0, out_1)
    blocks, chip, core = scal[0, 8], scal[0, 9], scal[0, 10]

    row_copies = [
        copy_in(
            arrived[hop],
            upstream.at[rows_at(lax.rem(chip - hop + CHIPS, CHIPS))],
            row_sems.at[hop],
        )
        for hop in range(CHIPS)
    ]
    copies = [copy_in(sources[i], held[i], in_sems.at[i]) for i in range(21)]
    sum_k[...] = jnp.zeros_like(sum_k)
    sum_v[...] = jnp.zeros_like(sum_v)
    sum_q[...] = jnp.zeros_like(sum_q)
    for moving in row_copies + copies[0:5]:
        moving.wait()
    lanes = iota((HALF, LANES), 1)
    gate_grads = jnp.zeros((HALF, LANES), F32)
    for r in range(2):
        expert = 2 * chip + (core if r == 0 else 1 - core)
        gate = column(gates[...], expert)
        raw = nt(upstream[...], out_w[r][...])
        gate_grads = jnp.where(
            lanes == expert, row_sum(o_spread[r][...].astype(F32) * raw), gate_grads
        )
        grad_o[r] = (gate * raw).astype(BF16)
        grad_y[r] = (gate * upstream[...].astype(F32)).astype(BF16)
    y_copies = [copy_in(grad_y.at[r], y_out[r], out_sems.at[r]) for r in range(2)]
    weights = gates[...]
    gate_low[...] = (weights * (gate_grads - row_sum(weights * gate_grads))).astype(BF16)
    for moving in copies[5:13]:
        moving.wait()

    @pl.loop(0, blocks)
    def _(j):
        start = j * TOK
        here = pl.ds(pl.multiple_of(start, TOK), TOK)
        take = iota((TOK, HALF), 0) + start
        packed = sum(
            nn(onehot(pos_row[r : r + 1, :] == take), grad_o[r]) for r in range(2)
        ).astype(BF16)
        pair_lanes = iota((2 * TOK, LANES), 1)
        inners = jnp.zeros((2 * TOK, LANES), F32)
        for i in range(PAIRS):
            at = slice(i * LANES, (i + 1) * LANES)
            q_pairs[i] = split_heads(q_held[here, at])
            grad_pair = split_heads(packed[:, at])
            o_pairs[i] = grad_pair
            block = o_held[here, at].astype(F32)
            product = row_sum(grad_pair.astype(F32) * jnp.concatenate([block, block], 0))
            inners = jnp.where(pair_lanes == i, product, inners)
        inner[...] = inners.T[:8]
        logs[...] = lse[j]
        for level in range(1, 5):
            pl.when(scal[0, j] == level)(
                functools.partial(
                    back_level, level * SPAN, start, keys, values, key_pos, q_pairs, o_pairs, logs,
                    inner, sum_k, sum_v, part_q,
                )
            )

        block = jnp.concatenate(
            [(join_heads(part_q[i]) * 0.125).astype(BF16) for i in range(PAIRS)], 1
        )
        put = iota((HALF, TOK), 1) + start
        for r in range(2):
            sum_q[r] += nn(onehot(pos_col[:, r : r + 1] == put), block)

    for r in range(2):
        grad_q[r] = sum_q[r].astype(BF16)
    q_copies = [copy_in(grad_q.at[r], q_out[r], out_sems.at[2 + r]) for r in range(2)]
    for moving in copies[13:21]:
        moving.wait()
    for source in range(CHIPS):
        own[source * TOK : (source + 1) * TOK, :] = rows[rows_at(2 * source + core), :]
    sum_q[0] = (
        nt(grad_q[0], query_w[0][...])
        + nt(grad_q[1], query_w[1][...])
        + nn(gate_low[...], router[...])
    )
    gain_part = jnp.sum(sum_q[0] * own[...].astype(F32), 0, keepdims=True)
    sum_q[1, 0:1, :] = gain_part

    @pl.loop(0, 4)
    def _(tile):
        at = pl.ds(pl.multiple_of(tile * 256, 256), 256)
        low_k, low_v = sum_k[at, :].astype(BF16), sum_v[at, :].astype(BF16)
        grad_k[at, :] = low_k
        grad_v[at, :] = low_v
        total = nt(low_k, key_w[...]) + nt(low_v, value_w[...])
        sum_k[at, :] = total
        sum_q[1, 0:1, :] += jnp.sum(total * rows[at, :].astype(F32), 0, keepdims=True)

    k_copy = copy_in(grad_k, k_out, out_sems.at[4])
    v_copy = copy_in(grad_v, v_out, out_sems.at[5])
    final = []
    for hop in range(CHIPS):
        target = lax.rem(chip + hop, CHIPS)
        other_s[hop] = sum_k[rows_at(target * 2 + 1 - core), :].astype(BF16)
    final.append(copy_in(other_s, other, out_sems.at[6]))
    for hop in range(CHIPS):
        target = lax.rem(chip + hop, CHIPS)
        same_s[hop] = (
            sum_k[rows_at(target * 2 + core), :] + sum_q[0, rows_at(target), :]
        ).astype(BF16)
        final.append(copy_in(same_s.at[hop], same[hop], row_sems.at[hop]))
    tiny[...] += tn(own[...], gate_low[...]) + lane_of(sum_q[1, 0:1, :] / gain[...], 8)
    final.append(copy_in(tiny, tiny_out, out_sems.at[7]))
    for moving in [*y_copies, *q_copies, k_copy, v_copy, *final]:
        moving.wait()


def attend_back(table, arrived, held, key_w, value_w, query_w, out_w, plan, rest):
    outs = [like((TOK, WIDTH), BF16)] * 4 + [
        like((CHIPS, TOK, WIDTH), BF16),
        like((HALF, WIDTH), BF16),
        like((HALF, WIDTH), BF16),
        like((HALF, WIDTH), BF16),
        like((HALF, WIDTH), BF16),
        like((SEQ, WIDTH), BF16),
        like((SEQ, WIDTH), BF16),
        like((WIDTH, LANES), F32),
    ]
    keys, values, q_held, o_held, spread_0, spread_1, lse, gates = held
    sources = [
        *out_w, gates, spread_0, spread_1, plan["pos_row"], q_held, o_held, lse, keys, values,
        plan["key_pos"], plan["pos_col"], *query_w, key_w, value_w, *rest,
    ]
    scratch = [pltpu.VMEM((HALF, WIDTH), BF16)]
    scratch += [pltpu.VMEM(a.shape, a.dtype) for a in sources]
    scratch += [
        pltpu.VMEM((2, HALF, WIDTH), BF16),
        pltpu.VMEM((SEQ, WIDTH), F32),
        pltpu.VMEM((SEQ, WIDTH), F32),
        pltpu.VMEM((2, HALF, WIDTH), F32),
        pltpu.VMEM((PAIRS, 2 * TOK, LANES), F32),
        pltpu.VMEM((PAIRS, 2 * TOK, LANES), BF16),
        pltpu.VMEM((PAIRS, 2 * TOK, LANES), BF16),
        pltpu.VMEM((8, 2 * TOK), F32),
        pltpu.VMEM((8, 2 * TOK), F32),
        pltpu.VMEM((HALF, WIDTH), BF16),
        pltpu.VMEM((HALF, LANES), BF16),
        pltpu.VMEM((2, HALF, WIDTH), BF16),
        pltpu.VMEM((2, HALF, WIDTH), BF16),
        pltpu.VMEM((SEQ, WIDTH), BF16),
        pltpu.VMEM((SEQ, WIDTH), BF16),
        pltpu.VMEM((CHIPS, TOK, WIDTH), BF16),
        pltpu.VMEM((CHIPS, TOK, WIDTH), BF16),
        pltpu.SemaphoreType.DMA((21,)),
        pltpu.SemaphoreType.DMA((4,)),
        pltpu.SemaphoreType.DMA((8,)),
    ]
    args = [table, *arrived, *sources]
    return call_any("attend_back", attend_back_kernel, outs, args, scratch, 10**11, 60)


def pair_sum_kernel(*refs):
    other, outs = refs[4], refs[5:]
    for hop in range(CHIPS):
        outs[hop][...] = (refs[hop][...].astype(F32) + other[hop].astype(F32)).astype(BF16)


def pair_sum(same, other):
    return call("pair_sum", pair_sum_kernel, [like((TOK, WIDTH), BF16)] * 4, [*same, other])


def expert_weights_kernel(first, *refs):
    scal, rows = refs[0:2]
    mixes, grad_y, grad_q = refs[2:4], refs[4:6], refs[6:8]
    before = None if first else refs[8]
    after, own = refs[8 if first else 9 :]
    core = scal[0, 10]
    for side in range(2):
        for source in range(CHIPS):
            own[side, source * TOK : (source + 1) * TOK, :] = rows[
                rows_at(2 * source + (core if side == 0 else 1 - core)), :
            ]
    halves = (
        tn(own[0], grad_q[0][...]) + tn(own[1], grad_q[1][...]),
        tn(mixes[0][...], grad_y[0][...]) + tn(mixes[1][...], grad_y[1][...]),
    )
    for half, value in enumerate(halves):
        at = slice(half * WIDTH, (half + 1) * WIDTH)
        if not first:
            value = value + before[:, at]
        after[:, at] = value.astype(after.dtype)


def expert_weights(table, rows, mixes, grad_y, grad_q, before, last):
    first = before is None
    args = [table, rows, *mixes, *grad_y, *grad_q, *(() if first else (before,))]
    outs = [like((WIDTH, 2 * WIDTH), BF16 if last else F32)]
    return call(
        "expert_weights",
        functools.partial(expert_weights_kernel, first),
        outs,
        args,
        [pltpu.VMEM((2, HALF, WIDTH), BF16)],
        smem=(0,),
        flops=3 * 10**9,
    )[0]


def shared_weights_kernel(first, rows, grad_k, grad_v, *refs):
    after = refs[-1]
    for half, grad in enumerate((grad_k, grad_v)):
        at = slice(half * WIDTH, (half + 1) * WIDTH)
        value = tn(rows[...], grad[...])
        if not first:
            value = value + refs[0][:, at]
        after[:, at] = value.astype(after.dtype)
    if after.shape[1] == SHARED:
        after[:, 2 * WIDTH :] = refs[1][...].astype(after.dtype)


SHARED = 2 * WIDTH + LANES


def shared_weights(rows, grad_k, grad_v, before, tiny):
    first, last = before is None, tiny is not None
    args = [rows, grad_k, grad_v, *(() if first else (before,)), *((tiny,) if last else ())]
    return call(
        "shared_weights",
        functools.partial(shared_weights_kernel, first),
        [like((WIDTH, SHARED), BF16) if last else like((WIDTH, 2 * WIDTH), F32)],
        args,
        flops=3 * 10**9,
    )[0]


def slot_pick(shape, r, row_dim):
    row, col = iota(shape, row_dim), iota(shape, 1 - row_dim)
    skip = SLOTS * r
    for source in range(1, CHIPS):
        skip = skip + jnp.where(row >= SLOTS * source, SLOTS, 0)
    return onehot(col == row + skip)


ROWS = CHIPS * SLOTS
BLOCK = 2 * SLOTS


def gelu_parts(x):
    scale = 0.7978845608028654
    inner = scale * (x + 0.044715 * x * x * x)
    return jnp.tanh(inner), scale * (1.0 + 3.0 * 0.044715 * x * x)


def store_blocks(results, outs):
    full = sum(
        nn(slot_pick((2 * ROWS, ROWS), r, 1), results[r].astype(BF16)) for r in range(2)
    ).astype(BF16)
    for hop in range(CHIPS):
        outs[hop][...] = full[hop * BLOCK : (hop + 1) * BLOCK]


def feed_kernel(*refs):
    blocks, win, wout = refs[0:4], refs[4:6], refs[6:8]
    outs, received = refs[8:12], refs[12:14]
    total, = refs[14:]
    step = pl.program_id(0)

    @pl.when(step == 0)
    def _():
        full = jnp.concatenate([b[...] for b in blocks], 0)
        for r in range(2):
            received[r][...] = nn(slot_pick((ROWS, 2 * ROWS), r, 0), full).astype(BF16)
        total[...] = jnp.zeros_like(total)

    for r in range(2):
        pre = nn(received[r][...], win[r][...])
        bend, _ = gelu_parts(pre)
        total[r] += nn((0.5 * pre * (1.0 + bend)).astype(BF16), wout[r][...])

    @pl.when(step == pl.num_programs(0) - 1)
    def _():
        store_blocks([total[0], total[1]], outs)


def whole(shape):
    return pl.BlockSpec(shape, lambda f: (0,) * len(shape))


def feed(blocks, win, wout):
    grid = FFN // PART
    return pl.pallas_call(
        feed_kernel,
        grid=(grid,),
        in_specs=[whole((BLOCK, WIDTH))] * 4
        + [pl.BlockSpec((WIDTH, PART), lambda f: (0, f))] * 2
        + [pl.BlockSpec((PART, WIDTH), lambda f: (f, 0))] * 2,
        out_specs=tuple([whole((BLOCK, WIDTH))] * 4 + [whole((ROWS, WIDTH))] * 2),
        out_shape=tuple([like((BLOCK, WIDTH), BF16)] * 4 + [like((ROWS, WIDTH), BF16)] * 2),
        scratch_shapes=[pltpu.VMEM((2, ROWS, WIDTH), F32)],
        compiler_params=pltpu.CompilerParams(vmem_limit_bytes=60 * 2**20),
        cost_estimate=pl.CostEstimate(flops=2 * 10**9, bytes_accessed=10**7, transcendentals=10**6),
        name="feed",
    )(*blocks, *win, *wout)


def feed_back_kernel(*refs):
    blocks, received, win, wout = refs[0:4], refs[4:6], refs[6:8], refs[8:10]
    outs, grad_rows, acts, grad_pre = refs[10:14], refs[14:16], refs[16:18], refs[18:20]
    total, = refs[20:]
    step = pl.program_id(0)

    @pl.when(step == 0)
    def _():
        full = jnp.concatenate([b[...] for b in blocks], 0)
        for r in range(2):
            grad_rows[r][...] = nn(slot_pick((ROWS, 2 * ROWS), r, 0), full).astype(BF16)
        total[...] = jnp.zeros_like(total)

    for r in range(2):
        pre = nn(received[r][...], win[r][...])
        bend, slope = gelu_parts(pre)
        acts[r][...] = (0.5 * pre * (1.0 + bend)).astype(BF16)
        grad_act = nt(grad_rows[r][...], wout[r][...])
        inner = 0.5 * (1.0 + bend) + 0.5 * pre * (1.0 - bend * bend) * slope
        low = (grad_act * inner).astype(BF16)
        grad_pre[r][...] = low
        total[r] += nt(low, win[r][...])

    @pl.when(step == pl.num_programs(0) - 1)
    def _():
        store_blocks([total[0], total[1]], outs)


HIDDEN = pl.BlockSpec((ROWS, PART), lambda f: (0, f))


def feed_back(blocks, received, win, wout):
    return pl.pallas_call(
        feed_back_kernel,
        grid=(FFN // PART,),
        in_specs=[whole((BLOCK, WIDTH))] * 4
        + [whole((ROWS, WIDTH))] * 2
        + [pl.BlockSpec((WIDTH, PART), lambda f: (0, f))] * 2
        + [pl.BlockSpec((PART, WIDTH), lambda f: (f, 0))] * 2,
        out_specs=tuple([whole((BLOCK, WIDTH))] * 4 + [whole((ROWS, WIDTH))] * 2 + [HIDDEN] * 4),
        out_shape=tuple(
            [like((BLOCK, WIDTH), BF16)] * 4
            + [like((ROWS, WIDTH), BF16)] * 2
            + [like((ROWS, FFN), BF16)] * 4
        ),
        scratch_shapes=[pltpu.VMEM((2, ROWS, WIDTH), F32)],
        compiler_params=pltpu.CompilerParams(vmem_limit_bytes=60 * 2**20),
        cost_estimate=pl.CostEstimate(flops=3 * 10**9, bytes_accessed=10**7, transcendentals=10**6),
        name="feed_back",
    )(*blocks, *received, *win, *wout)


def feed_weights_kernel(*refs):
    scal = refs[0]
    received, grad_rows, acts, grad_pre = refs[1:7], refs[7:13], refs[13:19], refs[19:25]
    out_in, outs_out, total = refs[25], refs[26:30], refs[30]
    out_in[...] = sum(tn(received[s][...], grad_pre[s][...]) for s in range(6)).astype(BF16)
    total[...] = sum(tn(acts[s][...], grad_rows[s][...]) for s in range(6))
    for hop in range(4):
        outs_out[hop][...] = total[rows_at(lax.rem(scal[0, 12] + hop, 4)), :].astype(BF16)


def feed_weights(table, received, grad_rows, acts, grad_pre):
    return pl.pallas_call(
        feed_weights_kernel,
        grid=(FFN // PART,),
        in_specs=[pl.BlockSpec(memory_space=pltpu.SMEM)]
        + [whole((ROWS, WIDTH))] * 12
        + [HIDDEN] * 12,
        out_specs=tuple(
            [pl.BlockSpec((WIDTH, PART), lambda f: (0, f))]
            + [pl.BlockSpec((TOK, WIDTH), lambda f: (f, 0))] * 4
        ),
        out_shape=tuple([like((WIDTH, FFN), BF16)] + [like((4 * TOK, WIDTH), BF16)] * 4),
        scratch_shapes=[pltpu.VMEM((WIDTH, PART), F32)],
        compiler_params=pltpu.CompilerParams(vmem_limit_bytes=60 * 2**20),
        cost_estimate=pl.CostEstimate(flops=8 * 10**9, bytes_accessed=2 * 10**7, transcendentals=0),
        name="feed_weights",
    )(table, *received, *grad_rows, *acts, *grad_pre)


def fold_kernel(axes, scal, *refs):
    count = len(axes)
    for n, axis in enumerate(axes):
        parts = refs[4 * n : 4 * n + 4]
        outs = refs[4 * (count + n) : 4 * (count + n) + 4]
        total = refs[8 * count + n]
        unit = total.shape[0] // 4
        total[...] = sum(p[...].astype(F32) for p in parts)
        place = scal[0, axis]
        for hop in range(4):
            at = pl.ds(pl.multiple_of(lax.rem(place + hop, 4) * unit, unit), unit)
            outs[hop][...] = total[at, :].astype(BF16)


def fold(table, groups, axes):
    outs = []
    for parts in groups:
        rows, cols = parts[0].shape
        outs += [like((rows // 4, cols), BF16)] * 4
    scratch = [pltpu.VMEM(parts[0].shape, F32) for parts in groups]
    args = [table] + [p for parts in groups for p in parts]
    places = tuple({"x": 11, "y": 12}[axis] for axis in axes)
    res = call("fold", functools.partial(fold_kernel, places), outs, args, scratch, smem=(0,))
    return [list(res[4 * n : 4 * n + 4]) for n in range(len(groups))]


def last_sum_kernel(count, *refs):
    for n in range(count):
        total = sum(p[...].astype(F32) for p in refs[4 * n : 4 * n + 4])
        refs[4 * count + n][...] = total.astype(refs[4 * count + n].dtype)


def last_sum(groups, dtypes):
    outs = [like(parts[0].shape, dtype) for parts, dtype in zip(groups, dtypes)]
    args = [p for parts in groups for p in parts]
    return call("last_sum", functools.partial(last_sum_kernel, len(groups)), outs, args)


def first_norm_kernel(block, gain, depth, wide, normed, payload, tail):
    value = block[...].astype(F32)
    wide[...] = value
    low = (norm_parts(value)[0] * gain[...]).astype(BF16)
    normed[...] = low
    payload[0:TOK, :] = low
    tail[...] = jnp.zeros_like(tail)
    tail[0:1, 0:TOK] = depth[...].astype(F32)
    payload[TOK : TOK + 16, :] = tail[...].astype(BF16)


def first_norm(block, gain, depth):
    outs = [
        like((TOK, WIDTH), F32),
        like((TOK, WIDTH), BF16),
        like((TOK + 16, WIDTH), BF16),
    ]
    scratch = [pltpu.VMEM((16, WIDTH), F32)]
    return call("first_norm", first_norm_kernel, outs, [block, gain, depth], scratch)


def attend_plan_kernel(steps, *refs):
    place, choices = refs[0], refs[1]
    blocks = refs[2:10] if 0 not in steps else ()
    outs = refs[2 + len(blocks) :]
    outs, (spots, named_all, depth_col) = outs[: 5 * len(steps)], outs[5 * len(steps) :]
    chip, core = place[0], place[1]
    dp_row, dp_col = place[2], place[3]
    token = iota((SEQ, LANES), 0)
    lanes = iota((SEQ, LANES), 1)
    held = ((token // TOK) % 2) == core
    if blocks:
        for hop in range(CHIPS):
            source = lax.rem(chip - hop + CHIPS, CHIPS)
            for side, ref in ((core, blocks[hop]), (1 - core, blocks[CHIPS + hop])):
                rows = ref[TOK : TOK + 16, 0:TOK].astype(F32)
                rows = jnp.concatenate([rows, jnp.zeros((TOK - 16, TOK), F32)], 0)
                depth_col[rows_at(source * 2 + side), :] = rows.T
    before = onehot(iota((SEQ, SEQ), 1) < iota((SEQ, SEQ), 0))
    for n, s in enumerate(steps):
        table, chosen_out, row_out, col_out, key_out = outs[5 * n : 5 * n + 5]
        turned = jnp.concatenate([choices[s].astype(F32), jnp.zeros((4, SEQ), F32)], 0).T
        named_here = named(turned.astype(I32), 4)
        named_all[...] = jnp.where(named_here, 1.0, 0.0)
        live = held[:, 0:1]
        if blocks:
            live = live & (depth_col[:, 0:1] > s + 0.5)
        live = jnp.where(live, 1.0, 0.0)
        hits = [
            row_sum(jnp.where(lanes == 2 * chip + side, named_all[...], 0.0)) * live
            for side in (core, 1 - core)
        ]
        count = hits[0] + hits[1]
        base = nn(before, jnp.broadcast_to(count, (SEQ, LANES)).astype(BF16))
        key_out[...] = base.astype(I32)
        spot = jnp.where(
            lanes == 0,
            jnp.where(hits[0] > 0, base, -1.0),
            jnp.where(hits[1] > 0, base + hits[0], -1.0),
        )
        spots[...] = jnp.where(lanes < 2, spot, -1.0)
        for source in range(CHIPS):
            at = slice(source * TOK, (source + 1) * TOK)
            chosen_out[at, :] = named_all[rows_at(2 * source + core), :]
            part = spots[rows_at(2 * source + core), :]
            col_out[at, :] = part.astype(I32)
            row_out[:, at] = part.T[:8].astype(I32)
        reach = jnp.sum(
            jnp.where(base <= (lanes * TOK + TOK - 1).astype(F32), 1.0, 0.0), 0, keepdims=True
        )
        total = jnp.sum(count, 0, keepdims=True).astype(I32)
        line = iota((8, LANES), 1)
        chunks = (reach.astype(I32) + (SPAN - 1)) // SPAN
        packed = (total + (TOK - 1)) // TOK
        table[...] = jnp.where(
            line < 8,
            chunks,
            packed,
        )
        for lane, value in ((9, chip), (10, core), (11, dp_row), (12, dp_col)):
            table[...] = jnp.where(line == lane, value, table[...])


def attend_plan(steps, place, choices, blocks):
    outs = [
        like((8, LANES), I32),
        like((HALF, LANES), F32),
        like((8, HALF), I32),
        like((HALF, LANES), I32),
        like((SEQ, LANES), I32),
    ] * len(steps)
    scratch = [pltpu.VMEM((SEQ, LANES), F32)] * 3
    res = call(
        "attend_plan", functools.partial(attend_plan_kernel, steps), outs,
        [place, choices, *blocks], scratch, smem=(0,), flops=10**9,
    )
    names = ("table", "chosen", "pos_row", "pos_col", "key_pos")
    return [dict(zip(names, res[5 * n : 5 * n + 5])) for n in range(len(steps))]


def slot_plan_kernel(place, choices, depth, *outs):
    chip, core = place[0], place[1]
    lanes = iota((TOK, LANES), 1)
    before = onehot(iota((TOK, TOK), 1) < iota((TOK, TOK), 0))
    hop = (lanes // 2 - chip + CHIPS) % CHIPS
    start = hop * BLOCK + jnp.where(lanes % 2 == core, 0, SLOTS)
    for s in range(3):
        turned = jnp.concatenate([choices[s].astype(F32), jnp.zeros((6, TOK), F32)], 0).T
        choice = turned.astype(I32)
        live = depth[...] > s
        names = [lanes == choice[:, k : k + 1] for k in range(2)]
        hits = jnp.where((names[0] | names[1]) & live, 1.0, 0.0)
        spot = nn(before, hits.astype(BF16)) + start.astype(F32)
        table = jnp.full((TOK, LANES), -1.0, F32)
        for k in range(2):
            slot = jnp.where(live, row_sum(jnp.where(names[k], spot, 0.0)), -1.0)
            table = jnp.where(lanes == k, slot, table)
            table = jnp.where(lanes == 2 + k, choice[:, k : k + 1].astype(F32), table)
        outs[2 * s][...] = table.astype(I32)
        outs[2 * s + 1][...] = table.T[:8].astype(I32)


def slot_plan(place, choices, depth):
    outs = [like((TOK, LANES), I32), like((8, TOK), I32)] * 3
    res = call("slot_plan", slot_plan_kernel, outs, [place, choices, depth], smem=(0,))
    return res[0::2], res[1::2]


def dispatch_kernel(*refs):
    state, parts = refs[0], refs[1:5]
    gain, router, slot_row, slot_col = refs[5:9]
    mixed_out, normed_out, gates_out = refs[9:12]
    sends = refs[12:16]
    mixed = state[...] + sum(p[...].astype(F32) for p in parts)
    mixed_out[...] = mixed
    normed = (norm_parts(mixed)[0] * gain[...]).astype(BF16)
    normed_out[...] = normed
    logits = nt(normed, router[...])
    picked = [column(logits, slot_col[:, 2 + k : 3 + k]) for k in range(2)]
    peak = jnp.maximum(picked[0], picked[1])
    weights = [jnp.exp(p - peak) for p in picked]
    total = weights[0] + weights[1]
    lanes = iota((TOK, LANES), 1)
    gates_out[...] = jnp.where(
        lanes == 0, weights[0] / total, jnp.where(lanes == 1, weights[1] / total, 0.0)
    )
    slots = iota((2 * ROWS, TOK), 0)
    hit = (slot_row[0:1, :] == slots) | (slot_row[1:2, :] == slots)
    full = nn(onehot(hit), normed).astype(BF16)
    for hop in range(CHIPS):
        sends[hop][...] = full[hop * BLOCK : (hop + 1) * BLOCK]


def dispatch(state, parts, gain, router, slot_row, slot_col):
    outs = [
        like((TOK, WIDTH), F32),
        like((TOK, WIDTH), BF16),
        like((TOK, LANES), F32),
    ] + [like((BLOCK, WIDTH), BF16)] * 4
    return call("dispatch", dispatch_kernel, outs, [state, *parts, gain, router, slot_row, slot_col])


def picked_rows(slot_col, returned):
    full = jnp.concatenate([b[...] for b in returned], 0)
    slots = iota((TOK, 2 * ROWS), 1)
    return [nn(onehot(slot_col[:, k : k + 1] == slots), full) for k in range(2)]


def next_state(mixed, state, gates, slot_col, rows):
    part = gates[:, 0:1] * rows[0] + gates[:, 1:2] * rows[1]
    return jnp.where(slot_col[:, 0:1] >= 0, mixed + part, state)


def advance_kernel(*refs):
    mixed, state, gates, slot_col = refs[0:4]
    returned, gain = refs[4:8], refs[8]
    state_out, normed_out = refs[9:11]
    rows = picked_rows(slot_col[...], returned)
    new = next_state(mixed[...], state[...], gates[...], slot_col[...], rows)
    state_out[...] = new
    normed_out[...] = (norm_parts(new)[0] * gain[...]).astype(BF16)


def advance(mixed, state, gates, slot_col, returned, gain):
    outs = [like((TOK, WIDTH), F32), like((TOK, WIDTH), BF16)]
    return call("advance", advance_kernel, outs, [mixed, state, gates, slot_col, *returned, gain])


def send_grads(upstream, rows, gates, slot_row, slot_col, grad_z_out, gate_grads_out, sends):
    grad_z = jnp.where(slot_col[:, 0:1] >= 0, upstream, 0.0)
    grad_z_out[...] = grad_z
    lanes = iota((TOK, LANES), 1)
    gate_grads_out[...] = jnp.where(
        lanes == 0,
        row_sum(rows[0] * grad_z),
        jnp.where(lanes == 1, row_sum(rows[1] * grad_z), 0.0),
    )
    slots = iota((2 * ROWS, TOK), 0)
    full = sum(
        nn(onehot(slot_row[k : k + 1, :] == slots), (gates[:, k : k + 1] * grad_z).astype(BF16))
        for k in range(2)
    ).astype(BF16)
    for hop in range(CHIPS):
        sends[hop][...] = full[hop * BLOCK : (hop + 1) * BLOCK]


SEND_OUTS = [
    like((TOK, WIDTH), F32),
    like((TOK, LANES), F32),
] + [like((BLOCK, WIDTH), BF16)] * 4


def turn_kernel(*refs):
    mixed, state, gates, slot_col, slot_row = refs[0:5]
    returned = refs[5:9]
    first_state, halt, depth, cotangent = refs[9:13]
    output, coefs, tiny, upstream_out, grad_z, gate_grads = refs[13:19]
    sends = refs[19:23]
    rows = picked_rows(slot_col[...], returned)
    second = state[...]
    third = next_state(mixed[...], second, gates[...], slot_col[...], rows)
    first = first_state[...]
    vector = halt[...]
    grad = cotangent[...].astype(F32)
    p1 = jax.nn.sigmoid(row_sum(first * vector))
    p2 = jax.nn.sigmoid(row_sum(second * vector))
    a1, a2, a3 = row_sum(first * grad), row_sum(second * grad), row_sum(third * grad)
    steps = depth[...]
    one, two, three = steps == 1, steps == 2, steps == 3
    c1 = jnp.where(one, 1.0, p1)
    c2 = jnp.where(one, 0.0, jnp.where(two, 1.0 - p1, p2 * (1.0 - p1)))
    c3 = jnp.where(three, (1.0 - p1) * (1.0 - p2), 0.0)
    output[...] = c1 * first + c2 * second + c3 * third
    d1 = jnp.where(
        two, a1 - a2, jnp.where(three, a1 - p2 * a2 - (1.0 - p2) * a3, 0.0)
    ) * (p1 * (1.0 - p1))
    d2 = jnp.where(three, (1.0 - p1) * (a2 - a3), 0.0) * (p2 * (1.0 - p2))
    tiny[...] = lane_of(jnp.sum(d1 * first + d2 * second, 0, keepdims=True), 25)
    lanes = iota((TOK, LANES), 1)
    table = jnp.zeros((TOK, LANES), F32)
    for lane, value in enumerate((c1, c2, c3, d1, d2)):
        table = jnp.where(lanes == lane, value, table)
    coefs[...] = table
    upstream = c3 * grad
    upstream_out[...] = upstream
    send_grads(upstream, rows, gates[...], slot_row[...], slot_col[...], grad_z, gate_grads, sends)


def turn(mixed, state, gates, slot_col, slot_row, returned, first_state, halt, depth, cotangent):
    outs = [
        like((TOK, WIDTH), F32),
        like((TOK, LANES), F32),
        like((WIDTH, LANES), F32),
        like((TOK, WIDTH), F32),
    ] + SEND_OUTS
    args = [mixed, state, gates, slot_col, slot_row, *returned, first_state, halt, depth, cotangent]
    return call("turn", turn_kernel, outs, args)


def moe_back_kernel(*refs):
    returned, slot_col, gates, gate_grads = refs[0:4], refs[4], refs[5], refs[6]
    normed, router, mixed, gain, grad_z, tiny = refs[7:13]
    grad_mixed, grad_low, tiny_out = refs[13:]
    full = jnp.concatenate([b[...] for b in returned], 0)
    slots = iota((TOK, 2 * ROWS), 1)
    hit = (slot_col[:, 0:1] == slots) | (slot_col[:, 1:2] == slots)
    grad_normed = nn(onehot(hit), full)
    weights, grads = gates[...], gate_grads[...]
    inner = row_sum(weights * grads)
    lanes = iota((TOK, LANES), 1)
    grad_logits = jnp.zeros((TOK, LANES), F32)
    for k in range(2):
        value = weights[:, k : k + 1] * (grads[:, k : k + 1] - inner)
        grad_logits = grad_logits + jnp.where(lanes == slot_col[:, 2 + k : 3 + k], value, 0.0)
    low = grad_logits.astype(BF16)
    grad_normed = grad_normed + nn(low, router[...])
    out, gain_part = norm_back(grad_normed, mixed[...], gain[...])
    out = out + grad_z[...]
    turned = jnp.concatenate([low[:, LANES - 16 :], low[:, : LANES - 16]], 1)
    tiny_out[...] = tiny[...] + tn(normed[...], turned) + lane_of(gain_part, 24)
    grad_mixed[...] = out
    grad_low[...] = out.astype(BF16)


def moe_back(returned, slot_col, gates, gate_grads, normed, router, mixed, gain, grad_z, tiny):
    outs = [
        like((TOK, WIDTH), F32),
        like((TOK, WIDTH), BF16),
        like((WIDTH, LANES), F32),
    ]
    args = [*returned, slot_col, gates, gate_grads, normed, router, mixed, gain, grad_z, tiny]
    return call("moe_back", moe_back_kernel, outs, args)


def retreat_kernel(step, *refs):
    parts = refs[0:4]
    state, gain, slot_col, upstream, grad_mixed = refs[4:9]
    rest = refs[9:]
    total = sum(p[...].astype(F32) for p in parts)
    out, _ = norm_back(total, state[...], gain[...])
    kept = jnp.where(slot_col[:, 0:1] >= 0, 0.0, upstream[...])
    carry = kept + grad_mixed[...] + out
    if step == 0:
        rest[0][...] = carry
        return
    cotangent, halt, coefs, gates, before_col, before_row = rest[0:6]
    returned = rest[6:10]
    upstream_out, grad_z, gate_grads_out = rest[10:13]
    sends = rest[13:17]
    table = coefs[...]
    carry = carry + column(table, step - 1) * cotangent[...].astype(F32)
    carry = carry + column(table, step + 2) * halt[...]
    upstream_out[...] = carry
    rows = picked_rows(before_col[...], returned)
    send_grads(
        carry, rows, gates[...], before_row[...], before_col[...], grad_z, gate_grads_out, sends
    )


def retreat(step, parts, args, extra):
    outs = [like((TOK, WIDTH), F32)] + (SEND_OUTS if step else [])
    return call("retreat", functools.partial(retreat_kernel, step), outs, [*parts, *args, *extra])


def swap_core(rows):
    return lax.ppermute(rows, "expert", [(i, i ^ 1) for i in range(2 * CHIPS)])


def shift_chip(rows, hops):
    count = 2 * CHIPS
    return lax.ppermute(rows, "expert", [(i, (i + 2 * hops) % count) for i in range(count)])


def send_blocks(blocks):
    return [blocks[0]] + [shift_chip(blocks[d], d) for d in (1, 2, 3)]


def return_blocks(blocks):
    return [blocks[0]] + [shift_chip(blocks[d], CHIPS - d) for d in (1, 2, 3)]


def spread_rows(rows):
    return [rows] + [shift_chip(rows, d) for d in (1, 2, 3)]


def shift_x(rows, hops):
    return lax.ppermute(rows, "dp", [(i, (i + 4 * hops) % 16) for i in range(16)])


def shift_y(rows, hops):
    return lax.ppermute(rows, "dp", [(i, i // 4 * 4 + (i + hops) % 4) for i in range(16)])


def go(shift, blocks):
    return [blocks[0]] + [shift(blocks[d], d) for d in (1, 2, 3)]


def block_sum(blocks):
    return jnp.sum(blocks.astype(F32), 0)


def local(
    block_input,
    gain_one,
    gain_two,
    moa_router,
    key_proj,
    value_proj,
    query_proj,
    out_proj,
    moe_router,
    ffn_in,
    ffn_out,
    halt_weight,
    depths,
    moa_choice,
    moe_choice,
    cotangent,
):
    member = lax.axis_index("expert")
    spot = lax.axis_index("dp")
    place = jnp.stack([member // 2, member % 2, spot // 4, spot % 4]).astype(I32)
    gain_a, gain_b = gain_one[None, :], gain_two[None, :]
    halt = halt_weight[None, :]
    router_a = jnp.pad(moa_router.T, ((0, LANES - 8), (0, 0)))
    router_b = jnp.pad(moe_router.T, ((0, LANES - 8), (0, 0)))
    depth = depths[:, None]
    moa_rows, moe_rows = moa_choice.swapaxes(1, 2), moe_choice.swapaxes(1, 2)

    state, normed, payload = first_norm(block_input, gain_a, depths[None, :])
    same = spread_rows(payload)
    query_w = [query_proj[0], swap_core(query_proj[0])]
    out_w = [out_proj[0], swap_core(out_proj[0])]
    plan = attend_plan((0,), place, moa_rows, ())
    same[1], plan[0]["table"] = lax.optimization_barrier((same[1], plan[0]["table"]))
    other = [swap_core(rows) for rows in same]
    slot_cols, slot_rows = slot_plan(place, moe_rows, depth)
    win = wout = None

    kept = []
    states = [state]
    for s in range(3):
        if s:
            same = spread_rows(normed)
            other = [swap_core(rows) for rows in same]
        p = plan[s]
        res = attend(
            p["table"], same, other, key_proj, value_proj, query_w, out_w, router_a, p
        )
        parts = send_blocks(res[:4])
        if s == 0:
            win = [ffn_in[0], swap_core(ffn_in[0])]
            wout = [ffn_out[0], swap_core(ffn_out[0])]
            plan = plan + attend_plan((1, 2), place, moa_rows, (*same, *other))
            parts[1], plan[1]["table"] = lax.optimization_barrier((parts[1], plan[1]["table"]))
        mixed, normed_b, gates, *sends = dispatch(
            state, parts, gain_b, router_b, slot_rows[s], slot_cols[s]
        )
        *sends, mine, others = feed(send_blocks(sends), win, wout)
        returned = return_blocks(sends)
        *saved, spread_0, spread_1, lse, weights = res[4:]
        kept.append(
            dict(
                normed=normed, rows=saved[0], mixed=mixed, normed_b=normed_b, gates=gates,
                attend=(*saved[1:], spread_0, spread_1, lse, weights),
                mixes=(spread_0, swap_core(spread_1)),
                received=(mine, others), returned=returned, state=state,
                received_all=(mine, swap_core(others)),
            )
        )
        if s < 2:
            state, normed = advance(mixed, state, gates, slot_cols[s], returned, gain_a)
            states.append(state)

    output, coefs, tiny, upstream, grad_z, gate_grads, *sends = turn(
        mixed, state, gates, slot_cols[2], slot_rows[2], returned, states[1], halt, depth, cotangent
    )
    expert_acc = shared_acc = None
    received, acts, grad_pres, grad_rows = [], [], [], []
    for s in (2, 1, 0):
        k, p = kept[s], plan[s]
        table = p["table"]
        *sends, rows_0, rows_1, act_0, act_1, pre_0, pre_1 = feed_back(
            send_blocks(sends), k["received"], win, wout
        )
        back = return_blocks(sends)
        received += k["received_all"]
        acts += [act_0, swap_core(act_1)]
        grad_pres += [pre_0, swap_core(pre_1)]
        grad_rows += [rows_0, swap_core(rows_1)]
        grad_mixed, grad_low, tiny = moe_back(
            back, slot_cols[s], k["gates"], gate_grads, k["normed_b"], router_b, k["mixed"],
            gain_b, grad_z, tiny,
        )
        if s == 0:
            grad_in, *blocks = feed_weights(table, received, grad_rows, acts, grad_pres)
            grad_low, grad_in, *blocks = lax.optimization_barrier((grad_low, grad_in, *blocks))
            grads_out = go(shift_y, blocks)
            grad_in = lax.psum_scatter(grad_in, "dp", scatter_dimension=0, tiled=True)
        *same, other, y_0, y_1, q_0, q_1, grad_k, grad_v, tiny = attend_back(
            table, spread_rows(grad_low), k["attend"], key_proj, value_proj, query_w, out_w, p,
            (k["rows"], router_a, gain_a, tiny),
        )
        other = swap_core(other)
        if s == 0:
            other, *arrived = lax.optimization_barrier((other, *grads_out[1:]))
            grads_out[1:] = arrived
        parts = pair_sum(same, other)
        q_0, grad_k, *parts = lax.optimization_barrier((q_0, grad_k, *parts))
        parts = send_blocks(parts)
        expert_acc = expert_weights(
            table, k["rows"], k["mixes"], (y_0, swap_core(y_1)), (q_0, swap_core(q_1)),
            expert_acc, s == 0,
        )
        shared_acc = shared_weights(
            k["rows"], grad_k, grad_v, shared_acc, None if s else tiny
        )
        parts[1], shared_acc, expert_acc = lax.optimization_barrier(
            (parts[1], shared_acc, expert_acc)
        )
        args = (k["state"], gain_a, slot_cols[s], upstream, grad_mixed)
        if s:
            b = kept[s - 1]
            extra = (
                cotangent, halt, coefs, b["gates"], slot_cols[s - 1], slot_rows[s - 1],
                *b["returned"],
            )
            upstream, grad_z, gate_grads, *sends = retreat(s, parts, args, extra)
        else:
            (grad_input,) = retreat(s, parts, args, ())

    (grads_out,) = fold(table, (grads_out,), "x")
    grads_out = go(shift_x, grads_out)
    grad_qo = block_sum(
        lax.all_to_all(
            expert_acc.reshape(16, 32, 2 * WIDTH), "dp", split_axis=0, concat_axis=0, tiled=True
        )
    )
    shared = block_sum(
        lax.all_to_all(
            shared_acc.reshape(128, 4, SHARED), ("dp", "expert"), split_axis=0, concat_axis=0,
            tiled=True,
        )
    )
    tiny = shared[:, 2 * WIDTH :]
    (grad_out,) = last_sum((grads_out,), (F32,))
    return (
        output,
        grad_input,
        tiny[:, 8],
        tiny[:, 24],
        tiny[:, :8],
        shared[:, :WIDTH],
        shared[:, WIDTH : 2 * WIDTH],
        grad_qo[:, :WIDTH][None],
        grad_qo[:, WIDTH:][None],
        tiny[:, 16:24],
        grad_in.astype(F32)[None],
        grad_out[None],
        tiny[:, 25],
    )


def solution(mesh):
    in_specs = (
        P(("dp", "expert"), None),
        P(),
        P(),
        P(),
        P(),
        P(),
        P("expert", None, None),
        P("expert", None, None),
        P(),
        P("expert", None, None),
        P("expert", None, None),
        P(),
        P(("dp", "expert")),
        P(None, "dp", None),
        P(None, ("dp", "expert"), None),
        P(("dp", "expert"), None),
    )
    out_specs = (
        P(("dp", "expert"), None),
        P(("dp", "expert"), None),
        P(("dp", "expert")),
        P(("dp", "expert")),
        P(("dp", "expert"), None),
        P(("dp", "expert"), None),
        P(("dp", "expert"), None),
        P("expert", "dp", None),
        P("expert", "dp", None),
        P(("dp", "expert"), None),
        P("expert", "dp", None),
        P("expert", "dp", None),
        P(("dp", "expert")),
    )
    return jax.shard_map(local, mesh=mesh, in_specs=in_specs, out_specs=out_specs, check_vma=False)
```

```python
import functools

import jax
import jax.numpy as jnp
from jax import lax
from jax.experimental import pallas as pl
from jax.experimental.pallas import tpu as pltpu
from jax.sharding import PartitionSpec as P

F32 = jnp.float32
BF16 = jnp.bfloat16
I32 = jnp.int32

WIDTH = 512
SEQ = 1024
TOK = 128
HALF = 512
CHIPS = 4
PAIRS = 4
SLOTS = 40
SPAN = 256
FFN = 2048
UNROLL = 4
PART = 512
LANES = 128


def nn(a, b):
    return lax.dot_general(a, b, (((1,), (0,)), ((), ())), preferred_element_type=F32)


def nt(a, b):
    return lax.dot_general(a, b, (((1,), (1,)), ((), ())), preferred_element_type=F32)


def tn(a, b):
    return lax.dot_general(a, b, (((0,), (0,)), ((), ())), preferred_element_type=F32)


def iota(shape, dim):
    return lax.broadcasted_iota(I32, shape, dim)


def onehot(mask):
    return jnp.where(mask, 1.0, 0.0).astype(BF16)


def row_sum(x):
    return jnp.sum(x, -1, keepdims=True)


def norm_parts(x):
    centred = x - jnp.mean(x, -1, keepdims=True)
    rstd = lax.rsqrt(jnp.mean(centred * centred, -1, keepdims=True) + 1e-05)
    return centred * rstd, rstd


def norm_back(grad, x, gain):
    hat, rstd = norm_parts(x)
    inner = grad * gain
    out = rstd * (
        inner
        - jnp.mean(inner, -1, keepdims=True)
        - hat * jnp.mean(inner * hat, -1, keepdims=True)
    )
    return out, jnp.sum(grad * hat, 0, keepdims=True)


def column(table, index):
    return row_sum(jnp.where(iota(table.shape, 1) == index, table, 0.0))


def masked_softmax(logits, chosen):
    peak = jnp.max(jnp.where(chosen, logits, -jnp.inf), -1, keepdims=True)
    weights = jnp.where(chosen, jnp.exp(logits - peak), 0.0)
    return weights / row_sum(weights)


def named(choice, count):
    lanes = iota((choice.shape[0], LANES), 1)
    mask = lanes == choice[:, 0:1]
    for k in range(1, count):
        mask = mask | (lanes == choice[:, k : k + 1])
    return mask


def lane_of(row, lane):
    return jnp.where(iota((LANES, WIDTH), 0) == lane, row, 0.0).T


def rows_at(block):
    return pl.ds(pl.multiple_of(block * TOK, TOK), TOK)


def split_heads(pair):
    lanes = iota((1, LANES), 1)
    low = jnp.where(lanes < 64, 1.0, 0.0).astype(BF16)
    high = jnp.where(lanes < 64, 0.0, 1.0).astype(BF16)
    return jnp.concatenate([pair * low, pair * high], 0)


def join_heads(both):
    return jnp.where(iota((TOK, LANES), 1) < 64, both[:TOK], both[TOK:])


def call(name, kernel, outs, args, scratch=(), smem=(), near=(), near_out=(), raw=(), flops=0, vmem=20):
    far = [i for i in range(len(args)) if i not in smem and i not in near and i not in raw]
    far_out = [i for i in range(len(outs)) if i not in near_out]
    count, total = len(args), len(args) + len(outs)

    def body(*refs):
        held = refs[total : total + len(far) + len(far_out)]
        in_sems, out_sems = refs[-2:]
        given, results = list(refs[:count]), list(refs[count:total])
        moving = []
        for n, i in enumerate(far):
            moving.append(pltpu.make_async_copy(given[i], held[n], in_sems.at[n]))
            moving[-1].start()
            given[i] = held[n]
        for n, i in enumerate(far_out):
            results[i] = held[len(far) + n]
        for copy in moving:
            copy.wait()
        kernel(*given, *results, *refs[total + len(far) + len(far_out) : -2])
        leaving = []
        for n, i in enumerate(far_out):
            leaving.append(pltpu.make_async_copy(results[i], refs[count + i], out_sems.at[n]))
            leaving[-1].start()
        for copy in leaving:
            copy.wait()

    def spec(i, places, nearby):
        if i in places:
            return pl.BlockSpec(memory_space=pltpu.SMEM)
        return pl.BlockSpec(memory_space=pltpu.VMEM if i in nearby else pltpu.HBM)

    moved = sum(a.size * a.dtype.itemsize for a in args) + sum(
        o.size * o.dtype.itemsize for o in outs
    )
    return pl.pallas_call(
        body,
        out_shape=tuple(outs),
        in_specs=[spec(i, smem, near) for i in range(count)],
        out_specs=tuple(spec(i, (), near_out) for i in range(len(outs))),
        scratch_shapes=[pltpu.VMEM(args[i].shape, args[i].dtype) for i in far]
        + [pltpu.VMEM(outs[i].shape, outs[i].dtype) for i in far_out]
        + list(scratch)
        + [pltpu.SemaphoreType.DMA((max(1, len(far)),)), pltpu.SemaphoreType.DMA((max(1, len(far_out)),))],
        compiler_params=pltpu.CompilerParams(vmem_limit_bytes=vmem * 2**20),
        cost_estimate=pl.CostEstimate(flops=flops, bytes_accessed=moved, transcendentals=0),
        name=name,
    )(*args)


def like(shape, dtype):
    return jax.ShapeDtypeStruct(shape, dtype)


ANY = pl.BlockSpec(memory_space=pl.ANY)
FAR = pl.BlockSpec(memory_space=pltpu.HBM)


def copy_in(src, dst, sem):
    moving = pltpu.make_async_copy(src, dst, sem)
    moving.start()
    return moving


def call_any(name, kernel, outs, args, scratch, flops, vmem, near, near_out):
    moved = sum(a.size * a.dtype.itemsize for a in args) + sum(
        o.size * o.dtype.itemsize for o in outs
    )
    return pl.pallas_call(
        kernel,
        out_shape=tuple(outs),
        in_specs=[pl.BlockSpec(memory_space=pltpu.SMEM)]
        + [ANY if i in near else FAR for i in range(1, len(args))],
        out_specs=tuple(ANY if i in near_out else FAR for i in range(len(outs))),
        scratch_shapes=list(scratch),
        compiler_params=pltpu.CompilerParams(vmem_limit_bytes=vmem * 2**20),
        cost_estimate=pl.CostEstimate(flops=flops, bytes_accessed=moved, transcendentals=0),
        name=name,
    )(*args)


def allowed_keys(key_pos, span, start):
    number = lax.rem(iota((span, 2 * TOK), 1), TOK) + start
    column_pos = key_pos[0:span, :]
    return jnp.concatenate([column_pos, column_pos], 1) <= number


def attend_level(span, start, keys, value_x, key_row, q_pairs, o_held, logs):
    @pl.loop(0, PAIRS, unroll=UNROLL)
    def _(i):
        pair = pl.ds(pl.multiple_of(i * LANES, LANES), LANES)
        part = nt(q_pairs[i], keys[0:span, pair])
        number = lax.rem(iota((2 * TOK, span), 0), TOK) + start
        part = jnp.where(key_row[0:1, 0:span] <= number, part, -jnp.inf)
        top = jnp.max(part, -1, keepdims=True)
        mixed = nn(jnp.exp(part - top).astype(BF16), value_x[i, 0:span, :])
        total = mixed[:, LANES : 2 * LANES]
        o_held[pl.ds(pl.multiple_of(start, TOK), TOK), pair] = join_heads(
            mixed[:, 0:LANES] / total
        ).astype(BF16)
        lanes = iota((2 * TOK, LANES), 1)
        logs[...] = jnp.where(lanes == i, top + jnp.log(total), logs[...])


def attend_kernel(*refs):
    scal = refs[0]
    same, other = refs[1:5], refs[5:9]
    sources = refs[9:19]
    outs = refs[20:24]
    rows_out, keys_out, values_out, q_out, o_out, spread_0, spread_1, lse_out, gates_out = refs[24:33]
    rows, own, keys, values, value_t = refs[33:38]
    held = refs[38:48]
    key_w, value_w, query_0, query_1, out_0, out_1, router, chosen, pos_row, pos_col = held[:10]
    key_pos = refs[48]
    queries, q_held, o_held, spread, o_spread, staged, lse, gates = refs[49:57]
    q_pairs, key_row, logs = refs[57:60]
    in_sems, row_sems, out_sems, block_sems = refs[60:64]
    query_w, out_w = (query_0, query_1), (out_0, out_1)
    blocks, chip, core = scal[0, 8], scal[0, 9], scal[0, 10]

    row_copies = []
    for hop in range(CHIPS):
        source = lax.rem(chip - hop + CHIPS, CHIPS)
        row_copies.append(
            copy_in(same[hop].at[0:TOK], rows.at[rows_at(source * 2 + core)], row_sems.at[2 * hop])
        )
        row_copies.append(
            copy_in(
                other[hop].at[0:TOK], rows.at[rows_at(source * 2 + 1 - core)], row_sems.at[2 * hop + 1]
            )
        )
    order = (0, 1, 2, 3, 6, 7, 8, 9, 4, 5)
    copies = {i: copy_in(sources[i], held[i], in_sems.at[i]) for i in order}
    key_copy = copy_in(refs[19], key_pos, in_sems.at[10])
    for moving in row_copies:
        moving.wait()
    rows_copy = copy_in(rows, rows_out, out_sems.at[0])
    for source in range(CHIPS):
        own[source * TOK : (source + 1) * TOK, :] = rows[rows_at(2 * source + core), :]
    copies[0].wait()
    copies[1].wait()

    @pl.loop(0, 4)
    def _(tile):
        at = pl.ds(pl.multiple_of(tile * 256, 256), 256)
        block = rows[at, :]
        keys[at, :] = nn(block, key_w[...]).astype(BF16)
        low = nn(block, value_w[...]).astype(BF16)
        values[at, :] = low
        for i in range(PAIRS):
            value_t[i, at, 0:LANES] = low[:, i * LANES : (i + 1) * LANES]
            value_t[i, at, LANES : 2 * LANES] = jnp.ones((256, LANES), BF16)

    keys_copy = copy_in(keys, keys_out, out_sems.at[1])
    values_copy = copy_in(values, values_out, out_sems.at[2])
    mine = own[...]
    for r in range(2):
        copies[2 + r].wait()
        full = nn(mine, query_w[r][...]).astype(BF16)
        queries[r] = full * jnp.asarray(0.125, BF16)
    copies[6].wait()
    copies[7].wait()
    weights = masked_softmax(nt(mine, router[...]), chosen[...] > 0.0)
    gates[...] = weights
    gates_copy = copy_in(gates, gates_out, out_sems.at[3])
    spread[...] = jnp.zeros_like(spread)
    copies[8].wait()
    copies[9].wait()
    key_copy.wait()
    for part in range(8):
        at = slice(part * TOK, (part + 1) * TOK)
        key_row[:, at] = key_pos[at, :].astype(F32).T[:8].astype(I32)

    @pl.loop(0, blocks)
    def _(j):
        start = j * TOK
        here = pl.ds(pl.multiple_of(start, TOK), TOK)
        take = iota((TOK, HALF), 0) + start
        packed = sum(
            nn(onehot(pos_row[r : r + 1, :] == take), queries[r]) for r in range(2)
        ).astype(BF16)
        q_held[here, :] = packed
        copy_in(q_held.at[here], q_out.at[here], block_sems.at[0, j])
        for i in range(PAIRS):
            q_pairs[i] = split_heads(packed[:, i * LANES : (i + 1) * LANES])
        for level in range(1, 5):
            pl.when(scal[0, j] == level)(
                functools.partial(
                    attend_level, level * SPAN, start, keys, value_t, key_row, q_pairs, o_held, logs
                )
            )
        lse[j] = logs[...].T[:8]
        copy_in(o_held.at[here], o_out.at[here], block_sems.at[1, j])
        block = o_held[here, :]
        put = iota((HALF, TOK), 1) + start
        for r in range(2):
            spread[r] += nn(onehot(pos_col[:, r : r + 1] == put), block)

    lse_copy = copy_in(lse, lse_out, out_sems.at[4])
    copies[4].wait()
    copies[5].wait()
    mixture = jnp.zeros((HALF, WIDTH), F32)
    for r in range(2):
        full = spread[r].astype(BF16)
        o_spread[r] = full
        expert = 2 * chip + (core if r == 0 else 1 - core)
        mixture = mixture + column(gates[...], expert) * nn(full, out_w[r][...])
    staged[...] = mixture.astype(BF16)
    final = [
        copy_in(staged.at[rows_at(lax.rem(chip + hop, CHIPS))], outs[hop], row_sems.at[hop])
        for hop in range(CHIPS)
    ]
    final.append(copy_in(o_spread.at[0], spread_0, out_sems.at[5]))
    final.append(copy_in(o_spread.at[1], spread_1, out_sems.at[6]))

    @pl.loop(0, blocks)
    def _(j):
        here = rows_at(j)
        pltpu.make_async_copy(q_held.at[here], q_out.at[here], block_sems.at[0, j]).wait()
        pltpu.make_async_copy(o_held.at[here], o_out.at[here], block_sems.at[1, j]).wait()

    for moving in [rows_copy, keys_copy, values_copy, gates_copy, lse_copy, *final]:
        moving.wait()


def attend(table, same, other, key_w, value_w, query_w, out_w, router, plan, vmem):
    outs = [like((TOK, WIDTH), BF16)] * 4 + [
        like((SEQ, WIDTH), BF16),
        like((SEQ, WIDTH), BF16),
        like((SEQ, WIDTH), BF16),
        like((SEQ, WIDTH), BF16),
        like((SEQ, WIDTH), BF16),
        like((HALF, WIDTH), BF16),
        like((HALF, WIDTH), BF16),
        like((8, 8, 2 * TOK), F32),
        like((HALF, LANES), F32),
    ]
    square = pltpu.VMEM((WIDTH, WIDTH), BF16)
    scratch = [
        pltpu.VMEM((SEQ, WIDTH), BF16),
        pltpu.VMEM((HALF, WIDTH), BF16),
        pltpu.VMEM((SEQ, WIDTH), BF16),
        pltpu.VMEM((SEQ, WIDTH), BF16),
        pltpu.VMEM((PAIRS, SEQ, 2 * LANES), BF16),
        square,
        square,
        square,
        square,
        square,
        square,
        pltpu.VMEM((LANES, WIDTH), BF16),
        pltpu.VMEM((HALF, LANES), F32),
        pltpu.VMEM((8, HALF), I32),
        pltpu.VMEM((HALF, LANES), I32),
        pltpu.VMEM((SEQ, LANES), I32),
        pltpu.VMEM((2, HALF, WIDTH), BF16),
        pltpu.VMEM((SEQ, WIDTH), BF16),
        pltpu.VMEM((SEQ, WIDTH), BF16),
        pltpu.VMEM((2, HALF, WIDTH), F32),
        pltpu.VMEM((2, HALF, WIDTH), BF16),
        pltpu.VMEM((HALF, WIDTH), BF16),
        pltpu.VMEM((8, 8, 2 * TOK), F32),
        pltpu.VMEM((HALF, LANES), F32),
        pltpu.VMEM((PAIRS, 2 * TOK, LANES), BF16),
        pltpu.VMEM((8, SEQ), I32),
        pltpu.VMEM((2 * TOK, LANES), F32),
        pltpu.SemaphoreType.DMA((11,)),
        pltpu.SemaphoreType.DMA((8,)),
        pltpu.SemaphoreType.DMA((7,)),
        pltpu.SemaphoreType.DMA((2, 8)),
    ]
    args = [
        table, *same, *other, key_w, value_w, *query_w, *out_w, router,
        plan["chosen"], plan["pos_row"], plan["pos_col"], plan["key_pos"],
    ]
    return call_any("attend", attend_kernel, outs, args, scratch, 6 * 10**9, vmem, range(1, 9), range(4))


def back_level(
    span, start, keys, values, key_pos, q_pairs, o_pairs, logs, inner, sum_k, sum_v, part_q
):
    @pl.loop(0, PAIRS, unroll=UNROLL)
    def _(i):
        pair = pl.ds(pl.multiple_of(i * LANES, LANES), LANES)
        key_block = keys[0:span, pair]
        queries, grads = q_pairs[i], o_pairs[i]
        probs = jnp.exp(nt(key_block, queries) - logs[pl.ds(i, 1), :])
        probs = jnp.where(allowed_keys(key_pos, span, start), probs, 0.0)
        grad_probs = nt(values[0:span, pair], grads)
        grad_scores = (probs * (grad_probs - inner[pl.ds(i, 1), :])).astype(BF16)
        sum_k[0:span, pair] += nn(grad_scores, queries)
        sum_v[0:span, pair] += nn(probs.astype(BF16), grads)
        part_q[i] = tn(grad_scores, key_block)


def attend_back_kernel(*refs):
    scal = refs[0]
    arrived = refs[1:5]
    sources = refs[5:26]
    same, other = refs[26:30], refs[30]
    y_out, q_out, k_out, v_out, tiny_out = refs[31:33], refs[33:35], refs[35], refs[36], refs[37]
    upstream = refs[38]
    held = refs[39:60]
    (
        out_0, out_1, gates, spread_0, spread_1, pos_row, q_held, o_held, lse, keys, values,
        key_pos, pos_col, query_0, query_1, key_w, value_w, rows, router, gain, tiny,
    ) = held
    grad_o, sum_k, sum_v, sum_q, part_q, q_pairs, o_pairs, logs, inner, own, gate_low = refs[60:71]
    grad_y, grad_q, grad_k, grad_v, same_s, other_s = refs[71:77]
    in_sems, row_sems, out_sems = refs[77:80]
    o_spread = (spread_0, spread_1)
    query_w, out_w = (query_0, query_1), (out_0, out_1)
    blocks, chip, core = scal[0, 8], scal[0, 9], scal[0, 10]

    row_copies = [
        copy_in(
            arrived[hop],
            upstream.at[rows_at(lax.rem(chip - hop + CHIPS, CHIPS))],
            row_sems.at[hop],
        )
        for hop in range(CHIPS)
    ]
    copies = [copy_in(sources[i], held[i], in_sems.at[i]) for i in range(21)]
    sum_k[...] = jnp.zeros_like(sum_k)
    sum_v[...] = jnp.zeros_like(sum_v)
    sum_q[...] = jnp.zeros_like(sum_q)
    for moving in row_copies + copies[0:5]:
        moving.wait()
    lanes = iota((HALF, LANES), 1)
    gate_grads = jnp.zeros((HALF, LANES), F32)
    for r in range(2):
        expert = 2 * chip + (core if r == 0 else 1 - core)
        gate = column(gates[...], expert)
        raw = nt(upstream[...], out_w[r][...])
        gate_grads = jnp.where(
            lanes == expert, row_sum(o_spread[r][...].astype(F32) * raw), gate_grads
        )
        grad_o[r] = (gate * raw).astype(BF16)
        grad_y[r] = (gate * upstream[...].astype(F32)).astype(BF16)
    y_copies = [copy_in(grad_y.at[r], y_out[r], out_sems.at[r]) for r in range(2)]
    weights = gates[...]
    gate_low[...] = (weights * (gate_grads - row_sum(weights * gate_grads))).astype(BF16)
    for moving in copies[5:13]:
        moving.wait()

    @pl.loop(0, blocks)
    def _(j):
        start = j * TOK
        here = pl.ds(pl.multiple_of(start, TOK), TOK)
        take = iota((TOK, HALF), 0) + start
        packed = sum(
            nn(onehot(pos_row[r : r + 1, :] == take), grad_o[r]) for r in range(2)
        ).astype(BF16)
        pair_lanes = iota((2 * TOK, LANES), 1)
        inners = jnp.zeros((2 * TOK, LANES), F32)
        for i in range(PAIRS):
            at = slice(i * LANES, (i + 1) * LANES)
            q_pairs[i] = split_heads(q_held[here, at])
            grad_pair = split_heads(packed[:, at])
            o_pairs[i] = grad_pair
            block = o_held[here, at].astype(F32)
            product = row_sum(grad_pair.astype(F32) * jnp.concatenate([block, block], 0))
            inners = jnp.where(pair_lanes == i, product, inners)
        inner[...] = inners.T[:8]
        logs[...] = lse[j]
        for level in range(1, 5):
            pl.when(scal[0, j] == level)(
                functools.partial(
                    back_level, level * SPAN, start, keys, values, key_pos, q_pairs, o_pairs, logs,
                    inner, sum_k, sum_v, part_q,
                )
            )

        block = jnp.concatenate(
            [(join_heads(part_q[i]) * 0.125).astype(BF16) for i in range(PAIRS)], 1
        )
        put = iota((HALF, TOK), 1) + start
        for r in range(2):
            sum_q[r] += nn(onehot(pos_col[:, r : r + 1] == put), block)

    for r in range(2):
        grad_q[r] = sum_q[r].astype(BF16)
    q_copies = [copy_in(grad_q.at[r], q_out[r], out_sems.at[2 + r]) for r in range(2)]
    for moving in copies[13:21]:
        moving.wait()
    for source in range(CHIPS):
        own[source * TOK : (source + 1) * TOK, :] = rows[rows_at(2 * source + core), :]
    sum_q[0] = (
        nt(grad_q[0], query_w[0][...])
        + nt(grad_q[1], query_w[1][...])
        + nn(gate_low[...], router[...])
    )
    gain_part = jnp.sum(sum_q[0] * own[...].astype(F32), 0, keepdims=True)
    sum_q[1, 0:1, :] = gain_part

    @pl.loop(0, 4)
    def _(tile):
        at = pl.ds(pl.multiple_of(tile * 256, 256), 256)
        low_k, low_v = sum_k[at, :].astype(BF16), sum_v[at, :].astype(BF16)
        grad_k[at, :] = low_k
        grad_v[at, :] = low_v
        total = nt(low_k, key_w[...]) + nt(low_v, value_w[...])
        sum_k[at, :] = total
        sum_q[1, 0:1, :] += jnp.sum(total * rows[at, :].astype(F32), 0, keepdims=True)

    k_copy = copy_in(grad_k, k_out, out_sems.at[4])
    v_copy = copy_in(grad_v, v_out, out_sems.at[5])
    final = []
    for hop in range(CHIPS):
        target = lax.rem(chip + hop, CHIPS)
        other_s[hop] = sum_k[rows_at(target * 2 + 1 - core), :].astype(BF16)
    final.append(copy_in(other_s, other, out_sems.at[6]))
    for hop in range(CHIPS):
        target = lax.rem(chip + hop, CHIPS)
        same_s[hop] = (
            sum_k[rows_at(target * 2 + core), :] + sum_q[0, rows_at(target), :]
        ).astype(BF16)
        final.append(copy_in(same_s.at[hop], same[hop], row_sems.at[hop]))
    tiny[...] += tn(own[...], gate_low[...]) + lane_of(sum_q[1, 0:1, :] / gain[...], 8)
    final.append(copy_in(tiny, tiny_out, out_sems.at[7]))
    for moving in [*y_copies, *q_copies, k_copy, v_copy, *final]:
        moving.wait()


def attend_back(table, arrived, held, key_w, value_w, query_w, out_w, plan, rest, vmem):
    outs = [like((TOK, WIDTH), BF16)] * 4 + [
        like((CHIPS, TOK, WIDTH), BF16),
        like((HALF, WIDTH), BF16),
        like((HALF, WIDTH), BF16),
        like((HALF, WIDTH), BF16),
        like((HALF, WIDTH), BF16),
        like((SEQ, WIDTH), BF16),
        like((SEQ, WIDTH), BF16),
        like((WIDTH, LANES), F32),
    ]
    keys, values, q_held, o_held, spread_0, spread_1, lse, gates = held
    sources = [
        *out_w, gates, spread_0, spread_1, plan["pos_row"], q_held, o_held, lse, keys, values,
        plan["key_pos"], plan["pos_col"], *query_w, key_w, value_w, *rest,
    ]
    scratch = [pltpu.VMEM((HALF, WIDTH), BF16)]
    scratch += [pltpu.VMEM(a.shape, a.dtype) for a in sources]
    scratch += [
        pltpu.VMEM((2, HALF, WIDTH), BF16),
        pltpu.VMEM((SEQ, WIDTH), F32),
        pltpu.VMEM((SEQ, WIDTH), F32),
        pltpu.VMEM((2, HALF, WIDTH), F32),
        pltpu.VMEM((PAIRS, 2 * TOK, LANES), F32),
        pltpu.VMEM((PAIRS, 2 * TOK, LANES), BF16),
        pltpu.VMEM((PAIRS, 2 * TOK, LANES), BF16),
        pltpu.VMEM((8, 2 * TOK), F32),
        pltpu.VMEM((8, 2 * TOK), F32),
        pltpu.VMEM((HALF, WIDTH), BF16),
        pltpu.VMEM((HALF, LANES), BF16),
        pltpu.VMEM((2, HALF, WIDTH), BF16),
        pltpu.VMEM((2, HALF, WIDTH), BF16),
        pltpu.VMEM((SEQ, WIDTH), BF16),
        pltpu.VMEM((SEQ, WIDTH), BF16),
        pltpu.VMEM((CHIPS, TOK, WIDTH), BF16),
        pltpu.VMEM((CHIPS, TOK, WIDTH), BF16),
        pltpu.SemaphoreType.DMA((21,)),
        pltpu.SemaphoreType.DMA((4,)),
        pltpu.SemaphoreType.DMA((8,)),
    ]
    args = [table, *arrived, *sources]
    return call_any("attend_back", attend_back_kernel, outs, args, scratch, 10**11, vmem, range(1, 5), range(5))


def pair_sum_kernel(*refs):
    other, outs = refs[4], refs[5:]
    for hop in range(CHIPS):
        outs[hop][...] = (refs[hop][...].astype(F32) + other[hop].astype(F32)).astype(BF16)


def pair_sum(same, other, vmem):
    return call("pair_sum", pair_sum_kernel, [like((TOK, WIDTH), BF16)] * 4, [*same, other], near=range(5), near_out=range(4), vmem=vmem)


def expert_weights_kernel(first, *refs):
    scal, rows = refs[0:2]
    mixes, grad_y, grad_q = refs[2:4], refs[4:6], refs[6:8]
    before = None if first else refs[8]
    after, own = refs[8 if first else 9 :]
    core = scal[0, 10]
    for side in range(2):
        for source in range(CHIPS):
            own[side, source * TOK : (source + 1) * TOK, :] = rows[
                rows_at(2 * source + (core if side == 0 else 1 - core)), :
            ]
    halves = (
        tn(own[0], grad_q[0][...]) + tn(own[1], grad_q[1][...]),
        tn(mixes[0][...], grad_y[0][...]) + tn(mixes[1][...], grad_y[1][...]),
    )
    for half, value in enumerate(halves):
        at = slice(half * WIDTH, (half + 1) * WIDTH)
        if not first:
            value = value + before[:, at]
        after[:, at] = value.astype(after.dtype)


def expert_weights(table, rows, mixes, grad_y, grad_q, before, last, vmem):
    first = before is None
    args = [table, rows, *mixes, *grad_y, *grad_q, *(() if first else (before,))]
    outs = [like((WIDTH, 2 * WIDTH), BF16 if last else F32)]
    return call(
        "expert_weights",
        functools.partial(expert_weights_kernel, first),
        outs,
        args,
        [pltpu.VMEM((2, HALF, WIDTH), BF16)],
        smem=(0,),
        flops=3 * 10**9,
        vmem=vmem,
    )[0]


def shared_weights_kernel(first, rows, grad_k, grad_v, *refs):
    after = refs[-1]
    for half, grad in enumerate((grad_k, grad_v)):
        at = slice(half * WIDTH, (half + 1) * WIDTH)
        value = tn(rows[...], grad[...])
        if not first:
            value = value + refs[0][:, at]
        after[:, at] = value.astype(after.dtype)


def shared_weights_last_kernel(rows, grad_k, grad_v, before, tiny, experts, after):
    after[:, 0 : 2 * WIDTH] = experts[...]
    for half, grad in enumerate((grad_k, grad_v)):
        at = slice(half * WIDTH, (half + 1) * WIDTH)
        there = slice((2 + half) * WIDTH, (3 + half) * WIDTH)
        after[:, there] = (tn(rows[...], grad[...]) + before[:, at]).astype(BF16)
    after[:, 4 * WIDTH :] = tiny[...].astype(BF16)


SHARED = 2 * WIDTH + LANES


def shared_weights(rows, grad_k, grad_v, before):
    first = before is None
    args = [rows, grad_k, grad_v, *(() if first else (before,))]
    outs = [like((WIDTH, 2 * WIDTH), F32)]
    kernel = functools.partial(shared_weights_kernel, first)
    return call("shared_weights", kernel, outs, args, flops=3 * 10**9)[0]


def shared_weights_last(rows, grad_k, grad_v, before, tiny, experts):
    args = [rows, grad_k, grad_v, before, tiny, experts]
    outs = [like((WIDTH, 2 * WIDTH + SHARED), BF16)]
    kernel = shared_weights_last_kernel
    return call("shared_weights", kernel, outs, args, flops=3 * 10**9, vmem=60)[0]


def slot_pick(shape, r, row_dim):
    row, col = iota(shape, row_dim), iota(shape, 1 - row_dim)
    skip = SLOTS * r
    for source in range(1, CHIPS):
        skip = skip + jnp.where(row >= SLOTS * source, SLOTS, 0)
    return onehot(col == row + skip)


ROWS = CHIPS * SLOTS
BLOCK = 2 * SLOTS


def gelu_parts(x):
    scale = 0.7978845608028654
    inner = scale * (x + 0.044715 * x * x * x)
    return jnp.tanh(inner), scale * (1.0 + 3.0 * 0.044715 * x * x)


def store_blocks(results, outs):
    full = sum(
        nn(slot_pick((2 * ROWS, ROWS), r, 1), results[r].astype(BF16)) for r in range(2)
    ).astype(BF16)
    for hop in range(CHIPS):
        outs[hop][...] = full[hop * BLOCK : (hop + 1) * BLOCK]


def hidden_at(step):
    return slice(step * PART, (step + 1) * PART)


def fetch_weights(win, wout, win_far, wout_far, sems):
    copies = []
    for step in range(FFN // PART):
        at = hidden_at(step)
        now = []
        for r in range(2):
            now.append((win_far[r].at[:, at], win.at[r, :, at]))
            now.append((wout_far[r].at[at, :], wout.at[r, at, :]))
        copies.append([copy_in(src, dst, sems.at[step, n]) for n, (src, dst) in enumerate(now)])
    return copies


def feed_kernel(*refs):
    blocks, win_far, wout_far = refs[0:4], refs[4:6], refs[6:8]
    outs, received_out = refs[8:12], refs[12:14]
    win, wout, received, weight_sems, out_sems = refs[14:]
    copies = fetch_weights(win, wout, win_far, wout_far, weight_sems)
    full = jnp.concatenate([b[...] for b in blocks], 0)
    leaving = []
    for r in range(2):
        received[r] = nn(slot_pick((ROWS, 2 * ROWS), r, 0), full).astype(BF16)
        leaving.append(copy_in(received.at[r], received_out[r], out_sems.at[r]))
    total = [jnp.zeros((ROWS, WIDTH), F32)] * 2
    for step in range(FFN // PART):
        at = hidden_at(step)
        for copy in copies[step]:
            copy.wait()
        for r in range(2):
            pre = nn(received[r], win[r, :, at])
            bend, _ = gelu_parts(pre)
            total[r] = total[r] + nn((0.5 * pre * (1.0 + bend)).astype(BF16), wout[r, at, :])
    store_blocks(total, outs)
    for copy in leaving:
        copy.wait()


NEAR = pl.BlockSpec(memory_space=pltpu.VMEM)


def feed(blocks, win, wout):
    return pl.pallas_call(
        feed_kernel,
        in_specs=[NEAR] * 4 + [FAR] * 4,
        out_specs=tuple([NEAR] * 4 + [FAR] * 2),
        out_shape=tuple([like((BLOCK, WIDTH), BF16)] * 4 + [like((ROWS, WIDTH), BF16)] * 2),
        scratch_shapes=[
            pltpu.VMEM((2, WIDTH, FFN), BF16),
            pltpu.VMEM((2, FFN, WIDTH), BF16),
            pltpu.VMEM((2, ROWS, WIDTH), BF16),
            pltpu.SemaphoreType.DMA((FFN // PART, 4)),
            pltpu.SemaphoreType.DMA((2,)),
        ],
        compiler_params=pltpu.CompilerParams(vmem_limit_bytes=24 * 2**20),
        cost_estimate=pl.CostEstimate(flops=2 * 10**9, bytes_accessed=10**7, transcendentals=10**6),
        name="feed",
    )(*blocks, *win, *wout)


def feed_back_kernel(*refs):
    blocks, received_far, win_far, wout_far = refs[0:4], refs[4:6], refs[6:8], refs[8:10]
    outs, rows_out, acts_out, pre_out = refs[10:14], refs[14:16], refs[16:18], refs[18:20]
    win, wout, received, grad_rows, acts, grad_pre = refs[20:26]
    weight_sems, in_sems, out_sems = refs[26:]
    arriving = [copy_in(received_far[r], received.at[r], in_sems.at[r]) for r in range(2)]
    copies = fetch_weights(win, wout, win_far, wout_far, weight_sems)
    full = jnp.concatenate([b[...] for b in blocks], 0)
    leaving = []
    for r in range(2):
        grad_rows[r] = nn(slot_pick((ROWS, 2 * ROWS), r, 0), full).astype(BF16)
        leaving.append(copy_in(grad_rows.at[r], rows_out[r], out_sems.at[r]))
    for copy in arriving:
        copy.wait()
    total = [jnp.zeros((ROWS, WIDTH), F32)] * 2
    for step in range(FFN // PART):
        at = hidden_at(step)
        for copy in copies[step]:
            copy.wait()
        for r in range(2):
            pre = nn(received[r], win[r, :, at])
            bend, slope = gelu_parts(pre)
            acts[r, :, at] = (0.5 * pre * (1.0 + bend)).astype(BF16)
            grad_act = nt(grad_rows[r], wout[r, at, :])
            inner = 0.5 * (1.0 + bend) + 0.5 * pre * (1.0 - bend * bend) * slope
            low = (grad_act * inner).astype(BF16)
            grad_pre[r, :, at] = low
            total[r] = total[r] + nt(low, win[r, :, at])
    for r in range(2):
        leaving.append(copy_in(acts.at[r], acts_out[r], out_sems.at[2 + r]))
        leaving.append(copy_in(grad_pre.at[r], pre_out[r], out_sems.at[4 + r]))
    store_blocks(total, outs)
    for copy in leaving:
        copy.wait()


def feed_back(blocks, received, win, wout):
    return pl.pallas_call(
        feed_back_kernel,
        in_specs=[NEAR] * 4 + [FAR] * 6,
        out_specs=tuple([NEAR] * 4 + [FAR] * 6),
        out_shape=tuple(
            [like((BLOCK, WIDTH), BF16)] * 4
            + [like((ROWS, WIDTH), BF16)] * 2
            + [like((ROWS, FFN), BF16)] * 4
        ),
        scratch_shapes=[
            pltpu.VMEM((2, WIDTH, FFN), BF16),
            pltpu.VMEM((2, FFN, WIDTH), BF16),
            pltpu.VMEM((2, ROWS, WIDTH), BF16),
            pltpu.VMEM((2, ROWS, WIDTH), BF16),
            pltpu.VMEM((2, ROWS, FFN), BF16),
            pltpu.VMEM((2, ROWS, FFN), BF16),
            pltpu.SemaphoreType.DMA((FFN // PART, 4)),
            pltpu.SemaphoreType.DMA((2,)),
            pltpu.SemaphoreType.DMA((6,)),
        ],
        compiler_params=pltpu.CompilerParams(vmem_limit_bytes=28 * 2**20),
        cost_estimate=pl.CostEstimate(flops=3 * 10**9, bytes_accessed=10**7, transcendentals=10**6),
        name="feed_back",
    )(*blocks, *received, *win, *wout)


def feed_weights_kernel(*refs):
    scal, far = refs[0], refs[1:25]
    outs_in, outs_out = refs[25:29], refs[29:33]
    received, grad_rows, acts, grad_pre, total_in, total_out, in_sems, out_sems = refs[33:]
    held = (received, grad_pre, grad_rows, acts)
    copies = [
        [
            copy_in(far[6 * n + s], held[n].at[ROWS * s : ROWS * (s + 1)], in_sems.at[n, s])
            for s in range(6)
        ]
        for n in range(4)
    ]
    row, col = scal[0, 11], scal[0, 12]
    leaving = []
    for copy in copies[0] + copies[1]:
        copy.wait()
    for step in range(FFN // PART):
        at = hidden_at(step)
        total_in[:, at] = tn(received[...], grad_pre[:, at]).astype(BF16)
    for hop in range(4):
        there = rows_at(lax.rem(row + hop, 4))
        leaving.append(copy_in(total_in.at[there], outs_in[hop], out_sems.at[0, hop]))
    for copy in copies[2] + copies[3]:
        copy.wait()
    for step in range(FFN // PART):
        total_out[step] = tn(acts[:, hidden_at(step)], grad_rows[...]).astype(BF16)
        for hop in range(4):
            there = rows_at(lax.rem(col + hop, 4))
            out = outs_out[hop].at[step * TOK : (step + 1) * TOK]
            leaving.append(copy_in(total_out.at[step, there], out, out_sems.at[1 + step, hop]))
    for copy in leaving:
        copy.wait()


def feed_weights(table, received, grad_rows, acts, grad_pre):
    return pl.pallas_call(
        feed_weights_kernel,
        in_specs=[pl.BlockSpec(memory_space=pltpu.SMEM)] + [FAR] * 24,
        out_specs=tuple([FAR] * 8),
        out_shape=tuple([like((TOK, FFN), BF16)] * 4 + [like((4 * TOK, WIDTH), BF16)] * 4),
        scratch_shapes=[
            pltpu.VMEM((6 * ROWS, WIDTH), BF16),
            pltpu.VMEM((6 * ROWS, WIDTH), BF16),
            pltpu.VMEM((6 * ROWS, FFN), BF16),
            pltpu.VMEM((6 * ROWS, FFN), BF16),
            pltpu.VMEM((WIDTH, FFN), BF16),
            pltpu.VMEM((4, PART, WIDTH), BF16),
            pltpu.SemaphoreType.DMA((4, 6)),
            pltpu.SemaphoreType.DMA((5, 4)),
        ],
        compiler_params=pltpu.CompilerParams(vmem_limit_bytes=60 * 2**20),
        cost_estimate=pl.CostEstimate(flops=8 * 10**9, bytes_accessed=2 * 10**7, transcendentals=0),
        name="feed_weights",
    )(table, *received, *grad_pre, *grad_rows, *acts)


def fold_kernel(axes, scal, *refs):
    count = len(axes)
    for n, axis in enumerate(axes):
        parts = refs[4 * n : 4 * n + 4]
        outs = refs[4 * (count + n) : 4 * (count + n) + 4]
        total = refs[8 * count + n]
        unit = total.shape[0] // 4
        total[...] = sum(p[...].astype(F32) for p in parts)
        place = scal[0, axis]
        for hop in range(4):
            at = pl.ds(pl.multiple_of(lax.rem(place + hop, 4) * unit, unit), unit)
            outs[hop][...] = total[at, :].astype(BF16)


def fold(table, groups, axes):
    outs = []
    for parts in groups:
        rows, cols = parts[0].shape
        outs += [like((rows // 4, cols), BF16)] * 4
    scratch = [pltpu.VMEM(parts[0].shape, F32) for parts in groups]
    args = [table] + [p for parts in groups for p in parts]
    places = tuple({"x": 11, "y": 12}[axis] for axis in axes)
    res = call("fold", functools.partial(fold_kernel, places), outs, args, scratch, smem=(0,), vmem=60)
    return [list(res[4 * n : 4 * n + 4]) for n in range(len(groups))]


def last_sum_kernel(count, *refs):
    for n in range(count):
        total = sum(p[...].astype(F32) for p in refs[4 * n : 4 * n + 4])
        refs[4 * count + n][...] = total.astype(refs[4 * count + n].dtype)


def last_sum(groups, dtypes):
    outs = [like(parts[0].shape, dtype) for parts, dtype in zip(groups, dtypes)]
    args = [p for parts in groups for p in parts]
    return call("last_sum", functools.partial(last_sum_kernel, len(groups)), outs, args, vmem=60)


def first_norm_kernel(block, gain, depth, wide, normed, payload, tail):
    value = block[...].astype(F32)
    wide[...] = value
    low = (norm_parts(value)[0] * gain[...]).astype(BF16)
    normed[...] = low
    payload[0:TOK, :] = low
    tail[...] = jnp.zeros_like(tail)
    tail[0:1, 0:TOK] = depth[...].astype(F32)
    payload[TOK : TOK + 16, :] = tail[...].astype(BF16)


def first_norm(block, gain, depth):
    outs = [
        like((TOK, WIDTH), F32),
        like((TOK, WIDTH), BF16),
        like((TOK + 16, WIDTH), BF16),
    ]
    scratch = [pltpu.VMEM((16, WIDTH), F32)]
    args = [block, gain, depth]
    return call("first_norm", first_norm_kernel, outs, args, scratch, near_out=(2,), vmem=60)


def attend_plan_kernel(steps, *refs):
    place, choices = refs[0], refs[1]
    blocks = refs[2:10] if 0 not in steps else ()
    outs = refs[2 + len(blocks) :]
    outs, (spots, named_all, depth_col, tails, sems) = outs[: 5 * len(steps)], outs[5 * len(steps) :]
    chip, core = place[0], place[1]
    dp_row, dp_col = place[2], place[3]
    token = iota((SEQ, LANES), 0)
    lanes = iota((SEQ, LANES), 1)
    held = ((token // TOK) % 2) == core
    if blocks:
        copies = [
            copy_in(ref.at[TOK : TOK + 16, 0:TOK], tails.at[n], sems.at[n])
            for n, ref in enumerate(blocks)
        ]
        for copy in copies:
            copy.wait()
        for hop in range(CHIPS):
            source = lax.rem(chip - hop + CHIPS, CHIPS)
            for side, n in ((core, hop), (1 - core, CHIPS + hop)):
                rows = tails[n].astype(F32)
                rows = jnp.concatenate([rows, jnp.zeros((TOK - 16, TOK), F32)], 0)
                depth_col[rows_at(source * 2 + side), :] = rows.T
    before = onehot(iota((SEQ, SEQ), 1) < iota((SEQ, SEQ), 0))
    for n, s in enumerate(steps):
        table, chosen_out, row_out, col_out, key_out = outs[5 * n : 5 * n + 5]
        turned = jnp.concatenate([choices[s].astype(F32), jnp.zeros((4, SEQ), F32)], 0).T
        named_here = named(turned.astype(I32), 4)
        named_all[...] = jnp.where(named_here, 1.0, 0.0)
        live = held[:, 0:1]
        if blocks:
            live = live & (depth_col[:, 0:1] > s + 0.5)
        live = jnp.where(live, 1.0, 0.0)
        hits = [
            row_sum(jnp.where(lanes == 2 * chip + side, named_all[...], 0.0)) * live
            for side in (core, 1 - core)
        ]
        count = hits[0] + hits[1]
        base = nn(before, jnp.broadcast_to(count, (SEQ, LANES)).astype(BF16))
        key_out[...] = base.astype(I32)
        spot = jnp.where(
            lanes == 0,
            jnp.where(hits[0] > 0, base, -1.0),
            jnp.where(hits[1] > 0, base + hits[0], -1.0),
        )
        spots[...] = jnp.where(lanes < 2, spot, -1.0)
        for source in range(CHIPS):
            at = slice(source * TOK, (source + 1) * TOK)
            chosen_out[at, :] = named_all[rows_at(2 * source + core), :]
            part = spots[rows_at(2 * source + core), :]
            col_out[at, :] = part.astype(I32)
            row_out[:, at] = part.T[:8].astype(I32)
        reach = jnp.sum(
            jnp.where(base <= (lanes * TOK + TOK - 1).astype(F32), 1.0, 0.0), 0, keepdims=True
        )
        total = jnp.sum(count, 0, keepdims=True).astype(I32)
        line = iota((8, LANES), 1)
        chunks = (reach.astype(I32) + (SPAN - 1)) // SPAN
        packed = (total + (TOK - 1)) // TOK
        table[...] = jnp.where(
            line < 8,
            chunks,
            packed,
        )
        for lane, value in ((9, chip), (10, core), (11, dp_row), (12, dp_col)):
            table[...] = jnp.where(line == lane, value, table[...])


def attend_plan(steps, place, choices, blocks):
    outs = [
        like((8, LANES), I32),
        like((HALF, LANES), F32),
        like((8, HALF), I32),
        like((HALF, LANES), I32),
        like((SEQ, LANES), I32),
    ] * len(steps)
    scratch = [pltpu.VMEM((SEQ, LANES), F32)] * 3
    scratch += [pltpu.VMEM((8, 16, TOK), BF16), pltpu.SemaphoreType.DMA((8,))]
    res = call(
        "attend_plan", functools.partial(attend_plan_kernel, steps), outs,
        [place, choices, *blocks], scratch, smem=(0,), raw=range(2, 10), flops=10**9, vmem=60,
    )
    names = ("table", "chosen", "pos_row", "pos_col", "key_pos")
    return [dict(zip(names, res[5 * n : 5 * n + 5])) for n in range(len(steps))]


def slot_plan_kernel(place, choices, depth, *outs):
    chip, core = place[0], place[1]
    lanes = iota((TOK, LANES), 1)
    before = onehot(iota((TOK, TOK), 1) < iota((TOK, TOK), 0))
    hop = (lanes // 2 - chip + CHIPS) % CHIPS
    start = hop * BLOCK + jnp.where(lanes % 2 == core, 0, SLOTS)
    for s in range(3):
        turned = jnp.concatenate([choices[s].astype(F32), jnp.zeros((6, TOK), F32)], 0).T
        choice = turned.astype(I32)
        live = depth[...] > s
        names = [lanes == choice[:, k : k + 1] for k in range(2)]
        hits = jnp.where((names[0] | names[1]) & live, 1.0, 0.0)
        spot = nn(before, hits.astype(BF16)) + start.astype(F32)
        table = jnp.full((TOK, LANES), -1.0, F32)
        for k in range(2):
            slot = jnp.where(live, row_sum(jnp.where(names[k], spot, 0.0)), -1.0)
            table = jnp.where(lanes == k, slot, table)
            table = jnp.where(lanes == 2 + k, choice[:, k : k + 1].astype(F32), table)
        outs[2 * s][...] = table.astype(I32)
        outs[2 * s + 1][...] = table.T[:8].astype(I32)


def slot_plan(place, choices, depth):
    outs = [like((TOK, LANES), I32), like((8, TOK), I32)] * 3
    res = call("slot_plan", slot_plan_kernel, outs, [place, choices, depth], smem=(0,), vmem=60)
    return list(res[0::2]), list(res[1::2])


def dispatch_kernel(*refs):
    state, parts = refs[0], refs[1:5]
    gain, router, slot_row, slot_col = refs[5:9]
    mixed_out, normed_out, gates_out = refs[9:12]
    sends = refs[12:16]
    mixed = state[...] + sum(p[...].astype(F32) for p in parts)
    mixed_out[...] = mixed
    normed = (norm_parts(mixed)[0] * gain[...]).astype(BF16)
    normed_out[...] = normed
    logits = nt(normed, router[...])
    picked = [column(logits, slot_col[:, 2 + k : 3 + k]) for k in range(2)]
    peak = jnp.maximum(picked[0], picked[1])
    weights = [jnp.exp(p - peak) for p in picked]
    total = weights[0] + weights[1]
    lanes = iota((TOK, LANES), 1)
    gates_out[...] = jnp.where(
        lanes == 0, weights[0] / total, jnp.where(lanes == 1, weights[1] / total, 0.0)
    )
    slots = iota((2 * ROWS, TOK), 0)
    hit = (slot_row[0:1, :] == slots) | (slot_row[1:2, :] == slots)
    full = nn(onehot(hit), normed).astype(BF16)
    for hop in range(CHIPS):
        sends[hop][...] = full[hop * BLOCK : (hop + 1) * BLOCK]


def dispatch(state, parts, gain, router, slot_row, slot_col):
    outs = [
        like((TOK, WIDTH), F32),
        like((TOK, WIDTH), BF16),
        like((TOK, LANES), F32),
    ] + [like((BLOCK, WIDTH), BF16)] * 4
    return call("dispatch", dispatch_kernel, outs, [state, *parts, gain, router, slot_row, slot_col], near=range(1, 5), near_out=range(3, 7))


def picked_rows(slot_col, returned):
    full = jnp.concatenate([b[...] for b in returned], 0)
    slots = iota((TOK, 2 * ROWS), 1)
    return [nn(onehot(slot_col[:, k : k + 1] == slots), full) for k in range(2)]


def next_state(mixed, state, gates, slot_col, rows):
    part = gates[:, 0:1] * rows[0] + gates[:, 1:2] * rows[1]
    return jnp.where(slot_col[:, 0:1] >= 0, mixed + part, state)


def advance_kernel(*refs):
    mixed, state, gates, slot_col = refs[0:4]
    returned, gain = refs[4:8], refs[8]
    state_out, normed_out = refs[9:11]
    rows = picked_rows(slot_col[...], returned)
    new = next_state(mixed[...], state[...], gates[...], slot_col[...], rows)
    state_out[...] = new
    normed_out[...] = (norm_parts(new)[0] * gain[...]).astype(BF16)


def advance(mixed, state, gates, slot_col, returned, gain):
    outs = [like((TOK, WIDTH), F32), like((TOK, WIDTH), BF16)]
    return call("advance", advance_kernel, outs, [mixed, state, gates, slot_col, *returned, gain], near=range(4, 8), near_out=(1,))


def send_grads(upstream, rows, gates, slot_row, slot_col, grad_z_out, gate_grads_out, sends):
    grad_z = jnp.where(slot_col[:, 0:1] >= 0, upstream, 0.0)
    grad_z_out[...] = grad_z
    lanes = iota((TOK, LANES), 1)
    gate_grads_out[...] = jnp.where(
        lanes == 0,
        row_sum(rows[0] * grad_z),
        jnp.where(lanes == 1, row_sum(rows[1] * grad_z), 0.0),
    )
    slots = iota((2 * ROWS, TOK), 0)
    full = sum(
        nn(onehot(slot_row[k : k + 1, :] == slots), (gates[:, k : k + 1] * grad_z).astype(BF16))
        for k in range(2)
    ).astype(BF16)
    for hop in range(CHIPS):
        sends[hop][...] = full[hop * BLOCK : (hop + 1) * BLOCK]


SEND_OUTS = [
    like((TOK, WIDTH), F32),
    like((TOK, LANES), F32),
] + [like((BLOCK, WIDTH), BF16)] * 4


def turn_kernel(*refs):
    mixed, state, gates, slot_col, slot_row = refs[0:5]
    returned = refs[5:9]
    first_state, halt, depth, cotangent = refs[9:13]
    output, coefs, tiny, upstream_out, grad_z, gate_grads = refs[13:19]
    sends = refs[19:23]
    rows = picked_rows(slot_col[...], returned)
    second = state[...]
    third = next_state(mixed[...], second, gates[...], slot_col[...], rows)
    first = first_state[...]
    vector = halt[...]
    grad = cotangent[...].astype(F32)
    p1 = jax.nn.sigmoid(row_sum(first * vector))
    p2 = jax.nn.sigmoid(row_sum(second * vector))
    a1, a2, a3 = row_sum(first * grad), row_sum(second * grad), row_sum(third * grad)
    steps = depth[...]
    one, two, three = steps == 1, steps == 2, steps == 3
    c1 = jnp.where(one, 1.0, p1)
    c2 = jnp.where(one, 0.0, jnp.where(two, 1.0 - p1, p2 * (1.0 - p1)))
    c3 = jnp.where(three, (1.0 - p1) * (1.0 - p2), 0.0)
    output[...] = c1 * first + c2 * second + c3 * third
    d1 = jnp.where(
        two, a1 - a2, jnp.where(three, a1 - p2 * a2 - (1.0 - p2) * a3, 0.0)
    ) * (p1 * (1.0 - p1))
    d2 = jnp.where(three, (1.0 - p1) * (a2 - a3), 0.0) * (p2 * (1.0 - p2))
    tiny[...] = lane_of(jnp.sum(d1 * first + d2 * second, 0, keepdims=True), 25)
    lanes = iota((TOK, LANES), 1)
    table = jnp.zeros((TOK, LANES), F32)
    for lane, value in enumerate((c1, c2, c3, d1, d2)):
        table = jnp.where(lanes == lane, value, table)
    coefs[...] = table
    upstream = c3 * grad
    upstream_out[...] = upstream
    send_grads(upstream, rows, gates[...], slot_row[...], slot_col[...], grad_z, gate_grads, sends)


def turn(mixed, state, gates, slot_col, slot_row, returned, first_state, halt, depth, cotangent):
    outs = [
        like((TOK, WIDTH), F32),
        like((TOK, LANES), F32),
        like((WIDTH, LANES), F32),
        like((TOK, WIDTH), F32),
    ] + SEND_OUTS
    args = [mixed, state, gates, slot_col, slot_row, *returned, first_state, halt, depth, cotangent]
    return call("turn", turn_kernel, outs, args, near=range(5, 9), near_out=range(6, 10))


def moe_back_kernel(*refs):
    returned, slot_col, gates, gate_grads = refs[0:4], refs[4], refs[5], refs[6]
    normed, router, mixed, gain, grad_z, tiny = refs[7:13]
    grad_mixed, grad_low, tiny_out = refs[13:]
    full = jnp.concatenate([b[...] for b in returned], 0)
    slots = iota((TOK, 2 * ROWS), 1)
    hit = (slot_col[:, 0:1] == slots) | (slot_col[:, 1:2] == slots)
    grad_normed = nn(onehot(hit), full)
    weights, grads = gates[...], gate_grads[...]
    inner = row_sum(weights * grads)
    lanes = iota((TOK, LANES), 1)
    grad_logits = jnp.zeros((TOK, LANES), F32)
    for k in range(2):
        value = weights[:, k : k + 1] * (grads[:, k : k + 1] - inner)
        grad_logits = grad_logits + jnp.where(lanes == slot_col[:, 2 + k : 3 + k], value, 0.0)
    low = grad_logits.astype(BF16)
    grad_normed = grad_normed + nn(low, router[...])
    out, gain_part = norm_back(grad_normed, mixed[...], gain[...])
    out = out + grad_z[...]
    turned = jnp.concatenate([low[:, LANES - 16 :], low[:, : LANES - 16]], 1)
    tiny_out[...] = tiny[...] + tn(normed[...], turned) + lane_of(gain_part, 24)
    grad_mixed[...] = out
    grad_low[...] = out.astype(BF16)


def moe_back(returned, slot_col, gates, gate_grads, normed, router, mixed, gain, grad_z, tiny):
    outs = [
        like((TOK, WIDTH), F32),
        like((TOK, WIDTH), BF16),
        like((WIDTH, LANES), F32),
    ]
    args = [*returned, slot_col, gates, gate_grads, normed, router, mixed, gain, grad_z, tiny]
    return call("moe_back", moe_back_kernel, outs, args, near=range(4), near_out=(1,))


def retreat_kernel(step, *refs):
    parts = refs[0:4]
    state, gain, slot_col, upstream, grad_mixed = refs[4:9]
    rest = refs[9:]
    total = sum(p[...].astype(F32) for p in parts)
    out, _ = norm_back(total, state[...], gain[...])
    kept = jnp.where(slot_col[:, 0:1] >= 0, 0.0, upstream[...])
    carry = kept + grad_mixed[...] + out
    if step == 0:
        rest[0][...] = carry
        return
    cotangent, halt, coefs, gates, before_col, before_row = rest[0:6]
    returned = rest[6:10]
    upstream_out, grad_z, gate_grads_out = rest[10:13]
    sends = rest[13:17]
    table = coefs[...]
    carry = carry + column(table, step - 1) * cotangent[...].astype(F32)
    carry = carry + column(table, step + 2) * halt[...]
    upstream_out[...] = carry
    rows = picked_rows(before_col[...], returned)
    send_grads(
        carry, rows, gates[...], before_row[...], before_col[...], grad_z, gate_grads_out, sends
    )


def retreat(step, parts, args, extra):
    outs = [like((TOK, WIDTH), F32)] + (SEND_OUTS if step else [])
    return call(
        "retreat", functools.partial(retreat_kernel, step), outs, [*parts, *args, *extra],
        near=range(4), near_out=range(3, 7),
    )


def swap_core(rows):
    return lax.ppermute(rows, "expert", [(i, i ^ 1) for i in range(2 * CHIPS)])


def shift_chip(rows, hops):
    count = 2 * CHIPS
    return lax.ppermute(rows, "expert", [(i, (i + 2 * hops) % count) for i in range(count)])


def send_blocks(blocks):
    return [blocks[0]] + [shift_chip(blocks[d], d) for d in (1, 2, 3)]


def after(value, other):
    return lax.optimization_barrier((value, other))


def return_blocks(blocks):
    return [blocks[0]] + [shift_chip(blocks[d], CHIPS - d) for d in (1, 2, 3)]


def spread_rows(rows):
    return [rows] + [shift_chip(rows, d) for d in (1, 2, 3)]


def shift_x(rows, hops):
    return lax.ppermute(rows, "dp", [(i, (i + 4 * hops) % 16) for i in range(16)])


def shift_y(rows, hops):
    return lax.ppermute(rows, "dp", [(i, i // 4 * 4 + (i + hops) % 4) for i in range(16)])


def go(shift, blocks):
    return [blocks[0]] + [shift(blocks[d], d) for d in (1, 2, 3)]


def block_sum(blocks):
    return jnp.sum(blocks.astype(F32), 0)


def local(
    block_input,
    gain_one,
    gain_two,
    moa_router,
    key_proj,
    value_proj,
    query_proj,
    out_proj,
    moe_router,
    ffn_in,
    ffn_out,
    halt_weight,
    depths,
    moa_choice,
    moe_choice,
    cotangent,
):
    member = lax.axis_index("expert")
    spot = lax.axis_index("dp")
    place = jnp.stack([member // 2, member % 2, spot // 4, spot % 4]).astype(I32)
    gain_a, gain_b = gain_one[None, :], gain_two[None, :]
    halt = halt_weight[None, :]
    router_a = jnp.pad(moa_router.T, ((0, LANES - 8), (0, 0)))
    router_b = jnp.pad(moe_router.T, ((0, LANES - 8), (0, 0)))
    depth = depths[:, None]
    moa_rows, moe_rows = moa_choice.swapaxes(1, 2), moe_choice.swapaxes(1, 2)

    state, normed, payload = first_norm(block_input, gain_a, depths[None, :])
    same = spread_rows(payload)
    plan = attend_plan((0,), place, moa_rows, ())
    same[1], plan[0]["table"] = after(same[1], plan[0]["table"])
    query_w = [query_proj[0], swap_core(query_proj[0])]
    out_w = [out_proj[0], swap_core(out_proj[0])]
    other = [swap_core(rows) for rows in same]
    slot_cols = slot_rows = None
    win = wout = None

    kept = []
    states = [state]
    for s in range(3):
        if s:
            same = spread_rows(normed)
            other = [swap_core(rows) for rows in same]
        p = plan[s]
        res = attend(
            p["table"], same, other, key_proj, value_proj, query_w, out_w, router_a, p,
            32 if s else 60,
        )
        parts = list(res[:4])
        if s == 0:
            parts[0], place_late = after(parts[0], place)
            slot_cols, slot_rows = slot_plan(place_late, moe_rows, depth)
            parts[3], slot_cols[0] = after(parts[3], slot_cols[0])
            win = [ffn_in[0], swap_core(ffn_in[0])]
            wout = [ffn_out[0], swap_core(ffn_out[0])]
            tails = (*same, *other)
        parts = send_blocks(parts)
        mixed, normed_b, gates, *sends = dispatch(
            state, parts, gain_b, router_b, slot_rows[s], slot_cols[s]
        )
        if s == 0:
            plan = plan + attend_plan((1,), place, moa_rows, tails)
            sends[3], plan[1]["table"] = after(sends[3], plan[1]["table"])
        sends = send_blocks(sends)
        *sends, mine, others = feed(sends, win, wout)
        if s == 0:
            plan = plan + attend_plan((2,), place, moa_rows, tails)
            sends[3], plan[2]["table"] = after(sends[3], plan[2]["table"])
        returned = return_blocks(sends)
        *saved, spread_0, spread_1, lse, weights = res[4:]
        kept.append(
            dict(
                normed=normed, rows=saved[0], mixed=mixed, normed_b=normed_b, gates=gates,
                attend=(*saved[1:], spread_0, spread_1, lse, weights),
                mixes=(spread_0, swap_core(spread_1)),
                received=(mine, others), returned=returned, state=state,
                received_all=(mine, swap_core(others)),
            )
        )
        if s < 2:
            state, normed = advance(mixed, state, gates, slot_cols[s], returned, gain_a)
            states.append(state)

    output, coefs, tiny, upstream, grad_z, gate_grads, *sends = turn(
        mixed, state, gates, slot_cols[2], slot_rows[2], returned, states[1], halt, depth, cotangent
    )
    expert_acc = shared_acc = None
    received, acts, grad_pres, grad_rows = [], [], [], []
    for s in (2, 1, 0):
        k, p = kept[s], plan[s]
        table = p["table"]
        *sends, rows_0, rows_1, act_0, act_1, pre_0, pre_1 = feed_back(
            send_blocks(sends), k["received"], win, wout
        )
        back = return_blocks(sends)
        received += k["received_all"]
        acts += [act_0, swap_core(act_1)]
        grad_pres += [pre_0, swap_core(pre_1)]
        grad_rows += [rows_0, swap_core(rows_1)]
        grad_mixed, grad_low, tiny = moe_back(
            back, slot_cols[s], k["gates"], gate_grads, k["normed_b"], router_b, k["mixed"],
            gain_b, grad_z, tiny,
        )
        limit = 20 if s else 60
        if s == 0:
            blocks = feed_weights(table, received, grad_rows, acts, grad_pres)
            grad_low, *blocks = lax.optimization_barrier((grad_low, *blocks))
            grads_in, grads_out = go(shift_x, blocks[:4]), go(shift_y, blocks[4:])
        *same, other, y_0, y_1, q_0, q_1, grad_k, grad_v, tiny = attend_back(
            table, spread_rows(grad_low), k["attend"], key_proj, value_proj, query_w, out_w, p,
            (k["rows"], router_a, gain_a, tiny), 36 if s else 60,
        )
        if s == 0:
            other, y_1, q_0, q_1, grad_k, *arrived = lax.optimization_barrier(
                (other, y_1, q_0, q_1, grad_k, *grads_in[1:], *grads_out[1:])
            )
            grads_in[1:], grads_out[1:] = arrived[:3], arrived[3:]
        other = swap_core(other)
        if s:
            parts = pair_sum(same, other, limit)
            q_0, grad_k, *parts = lax.optimization_barrier((q_0, grad_k, *parts))
        expert_acc = expert_weights(
            table, k["rows"], k["mixes"], (y_0, swap_core(y_1)), (q_0, swap_core(q_1)),
            expert_acc, s == 0, limit,
        )
        if s:
            shared_acc = shared_weights(k["rows"], grad_k, grad_v, shared_acc)
            parts = send_blocks(parts)
            *parts, shared_acc, expert_acc = lax.optimization_barrier(
                (*parts, shared_acc, expert_acc)
            )
        else:
            weights_last = shared_weights_last(
                k["rows"], grad_k, grad_v, shared_acc, tiny, expert_acc
            )
            other, weights_last = lax.optimization_barrier((other, weights_last))
            moved = lax.all_to_all(
                weights_last.reshape(16, 32, -1), "dp", split_axis=0, concat_axis=0, tiled=True
            )
            parts = send_blocks(pair_sum(same, other, limit))
        if s == 0:
            summed = block_sum(moved)
            low = summed[:, 2 * WIDTH :].astype(BF16)
            parts[1], low = after(parts[1], low)
            shared = lax.all_to_all(
                low.reshape(8, 4, SHARED), "expert", split_axis=0, concat_axis=0, tiled=True
            )
        args = (k["state"], gain_a, slot_cols[s], upstream, grad_mixed)
        if s:
            b = kept[s - 1]
            extra = (
                cotangent, halt, coefs, b["gates"], slot_cols[s - 1], slot_rows[s - 1],
                *b["returned"],
            )
            upstream, grad_z, gate_grads, *sends = retreat(s, parts, args, extra)
        else:
            (grad_input,) = retreat(s, parts, args, ())

    grads_in, grads_out = fold(table, (grads_in, grads_out), "yx")
    grads_in, grads_out = go(shift_y, grads_in), go(shift_x, grads_out)
    grads_in[1], low = after(grads_in[1], low)
    shared = block_sum(shared)
    tiny = shared[:, 2 * WIDTH :]
    grad_in, grad_out = last_sum((grads_in, grads_out), (F32, F32))
    return (
        output,
        grad_input,
        tiny[:, 8],
        tiny[:, 24],
        tiny[:, :8],
        shared[:, :WIDTH],
        shared[:, WIDTH : 2 * WIDTH],
        summed[:, :WIDTH][None],
        summed[:, WIDTH : 2 * WIDTH][None],
        tiny[:, 16:24],
        grad_in[None],
        grad_out[None],
        tiny[:, 25],
    )


def solution(mesh):
    in_specs = (
        P(("dp", "expert"), None),
        P(),
        P(),
        P(),
        P(),
        P(),
        P("expert", None, None),
        P("expert", None, None),
        P(),
        P("expert", None, None),
        P("expert", None, None),
        P(),
        P(("dp", "expert")),
        P(None, "dp", None),
        P(None, ("dp", "expert"), None),
        P(("dp", "expert"), None),
    )
    out_specs = (
        P(("dp", "expert"), None),
        P(("dp", "expert"), None),
        P(("dp", "expert")),
        P(("dp", "expert")),
        P(("dp", "expert"), None),
        P(("dp", "expert"), None),
        P(("dp", "expert"), None),
        P("expert", "dp", None),
        P("expert", "dp", None),
        P(("dp", "expert"), None),
        P("expert", "dp", None),
        P("expert", "dp", None),
        P(("dp", "expert")),
    )
    return jax.shard_map(local, mesh=mesh, in_specs=in_specs, out_specs=out_specs, check_vma=False)
```

```python
import functools

import jax
import jax.numpy as jnp
from jax import lax
from jax.experimental import pallas as pl
from jax.experimental.pallas import tpu as pltpu
from jax.sharding import PartitionSpec as P

F32 = jnp.float32
BF16 = jnp.bfloat16
I32 = jnp.int32

WIDTH = 512
SEQ = 1024
TOK = 128
HALF = 512
CHIPS = 4
PAIRS = 4
SLOTS = 40
SPAN = 256
FFN = 2048
UNROLL = 4
PART = 512
LANES = 128


def nn(a, b):
    return lax.dot_general(a, b, (((1,), (0,)), ((), ())), preferred_element_type=F32)


def nt(a, b):
    return lax.dot_general(a, b, (((1,), (1,)), ((), ())), preferred_element_type=F32)


def tn(a, b):
    return lax.dot_general(a, b, (((0,), (0,)), ((), ())), preferred_element_type=F32)


def iota(shape, dim):
    return lax.broadcasted_iota(I32, shape, dim)


def onehot(mask):
    return jnp.where(mask, 1.0, 0.0).astype(BF16)


def row_sum(x):
    return jnp.sum(x, -1, keepdims=True)


def norm_parts(x):
    centred = x - jnp.mean(x, -1, keepdims=True)
    rstd = lax.rsqrt(jnp.mean(centred * centred, -1, keepdims=True) + 1e-05)
    return centred * rstd, rstd


def norm_back(grad, x, gain):
    hat, rstd = norm_parts(x)
    inner = grad * gain
    out = rstd * (
        inner
        - jnp.mean(inner, -1, keepdims=True)
        - hat * jnp.mean(inner * hat, -1, keepdims=True)
    )
    return out, jnp.sum(grad * hat, 0, keepdims=True)


def column(table, index):
    return row_sum(jnp.where(iota(table.shape, 1) == index, table, 0.0))


def masked_softmax(logits, chosen):
    peak = jnp.max(jnp.where(chosen, logits, -jnp.inf), -1, keepdims=True)
    weights = jnp.where(chosen, jnp.exp(logits - peak), 0.0)
    return weights / row_sum(weights)


def named(choice, count):
    lanes = iota((choice.shape[0], LANES), 1)
    mask = lanes == choice[:, 0:1]
    for k in range(1, count):
        mask = mask | (lanes == choice[:, k : k + 1])
    return mask


def lane_of(row, lane):
    return jnp.where(iota((LANES, WIDTH), 0) == lane, row, 0.0).T


def turned_row(row):
    wide = jnp.concatenate([row.astype(F32), jnp.zeros((7, TOK), F32)], 0)
    return wide.T[:, 0:1].astype(I32)


def rows_at(block):
    return pl.ds(pl.multiple_of(block * TOK, TOK), TOK)


def split_heads(pair):
    lanes = iota((1, LANES), 1)
    low = jnp.where(lanes < 64, 1.0, 0.0).astype(BF16)
    high = jnp.where(lanes < 64, 0.0, 1.0).astype(BF16)
    return jnp.concatenate([pair * low, pair * high], 0)


def join_heads(both, rows):
    return jnp.where(iota((rows, LANES), 1) < 64, both[:rows], both[rows:])


def call(name, kernel, outs, args, scratch=(), smem=(), near=(), near_out=(), raw=(), flops=0, vmem=20):
    far = [i for i in range(len(args)) if i not in smem and i not in near and i not in raw]
    far_out = [i for i in range(len(outs)) if i not in near_out]
    count, total = len(args), len(args) + len(outs)

    def body(*refs):
        held = refs[total : total + len(far) + len(far_out)]
        in_sems, out_sems = refs[-2:]
        given, results = list(refs[:count]), list(refs[count:total])
        moving = []
        for n, i in enumerate(far):
            moving.append(pltpu.make_async_copy(given[i], held[n], in_sems.at[n]))
            moving[-1].start()
            given[i] = held[n]
        for n, i in enumerate(far_out):
            results[i] = held[len(far) + n]
        for copy in moving:
            copy.wait()
        kernel(*given, *results, *refs[total + len(far) + len(far_out) : -2])
        leaving = []
        for n, i in enumerate(far_out):
            leaving.append(pltpu.make_async_copy(results[i], refs[count + i], out_sems.at[n]))
            leaving[-1].start()
        for copy in leaving:
            copy.wait()

    def spec(i, places, nearby):
        if i in places:
            return pl.BlockSpec(memory_space=pltpu.SMEM)
        return pl.BlockSpec(memory_space=pltpu.VMEM if i in nearby else pltpu.HBM)

    moved = sum(a.size * a.dtype.itemsize for a in args) + sum(
        o.size * o.dtype.itemsize for o in outs
    )
    return pl.pallas_call(
        body,
        out_shape=tuple(outs),
        in_specs=[spec(i, smem, near) for i in range(count)],
        out_specs=tuple(spec(i, (), near_out) for i in range(len(outs))),
        scratch_shapes=[pltpu.VMEM(args[i].shape, args[i].dtype) for i in far]
        + [pltpu.VMEM(outs[i].shape, outs[i].dtype) for i in far_out]
        + list(scratch)
        + [pltpu.SemaphoreType.DMA((max(1, len(far)),)), pltpu.SemaphoreType.DMA((max(1, len(far_out)),))],
        compiler_params=pltpu.CompilerParams(vmem_limit_bytes=vmem * 2**20),
        cost_estimate=pl.CostEstimate(flops=flops, bytes_accessed=moved, transcendentals=0),
        name=name,
    )(*args)


def like(shape, dtype):
    return jax.ShapeDtypeStruct(shape, dtype)


ANY = pl.BlockSpec(memory_space=pl.ANY)
FAR = pl.BlockSpec(memory_space=pltpu.HBM)


def copy_in(src, dst, sem):
    moving = pltpu.make_async_copy(src, dst, sem)
    moving.start()
    return moving


def call_any(name, kernel, outs, args, scratch, flops, vmem, near, near_out):
    moved = sum(a.size * a.dtype.itemsize for a in args) + sum(
        o.size * o.dtype.itemsize for o in outs
    )
    return pl.pallas_call(
        kernel,
        out_shape=tuple(outs),
        in_specs=[pl.BlockSpec(memory_space=pltpu.SMEM)]
        + [ANY if i in near else FAR for i in range(1, len(args))],
        out_specs=tuple(ANY if i in near_out else FAR for i in range(len(outs))),
        scratch_shapes=list(scratch),
        compiler_params=pltpu.CompilerParams(vmem_limit_bytes=vmem * 2**20),
        cost_estimate=pl.CostEstimate(flops=flops, bytes_accessed=moved, transcendentals=0),
        name=name,
    )(*args)


def allowed_keys(key_pos, span, start, rows):
    number = lax.rem(iota((span, 2 * rows), 1), rows) + start
    column_pos = key_pos[0:span, :]
    if rows == TOK:
        column_pos = jnp.concatenate([column_pos, column_pos], 1)
    return column_pos <= number


def packed_rows(start, rows):
    return pl.ds(pl.multiple_of(start, TOK), rows)


def attend_level(rows, span, start, keys, value_x, key_row, q_held, o_held, logs):
    here = packed_rows(start, rows)

    @pl.loop(0, PAIRS, unroll=UNROLL)
    def _(i):
        pair = pl.ds(pl.multiple_of(i * LANES, LANES), LANES)
        part = nt(split_heads(q_held[here, pair]), keys[0:span, pair])
        number = lax.rem(iota((2 * rows, span), 0), rows) + start
        part = jnp.where(key_row[0:1, 0:span] <= number, part, -jnp.inf)
        top = jnp.max(part, -1, keepdims=True)
        mixed = nn(jnp.exp(part - top).astype(BF16), value_x[i, 0:span, :])
        total = mixed[:, LANES : 2 * LANES]
        o_held[here, pair] = join_heads(mixed[:, 0:LANES] / total, rows).astype(BF16)
        lanes = iota((2 * rows, LANES), 1)
        logs[0 : 2 * rows, :] = jnp.where(
            lanes == i, top + jnp.log(total), logs[0 : 2 * rows, :]
        )

    if rows < TOK:
        rest = pl.ds(pl.multiple_of(start + rows, rows), TOK - rows)
        o_held[rest, :] = jnp.zeros((TOK - rows, WIDTH), BF16)


SMALL = 5
LEVELS = [(TOK, level * SPAN, level) for level in range(1, 5)] + [(TOK // 2, SEQ, SMALL)]


def attend_kernel(*refs):
    scal = refs[0]
    same, other = refs[1:5], refs[5:9]
    sources = refs[9:19]
    outs = refs[20:24]
    rows_out, keys_out, values_out, q_out, o_out, spread_0, spread_1, lse_out, gates_out = refs[24:33]
    rows, own, keys, values, value_t = refs[33:38]
    held = refs[38:48]
    key_w, value_w, query_0, query_1, out_0, out_1, router, chosen, pos_row, pos_col = held[:10]
    key_pos = refs[48]
    queries, q_held, o_held, spread, o_spread, staged, lse, gates = refs[49:57]
    key_row, logs = refs[57:59]
    in_sems, row_sems, out_sems, block_sems = refs[59:63]
    query_w, out_w = (query_0, query_1), (out_0, out_1)
    blocks, chip, core = scal[0, 8], scal[0, 9], scal[0, 10]

    row_copies = []
    for hop in range(CHIPS):
        source = lax.rem(chip - hop + CHIPS, CHIPS)
        row_copies.append(
            copy_in(same[hop].at[0:TOK], rows.at[rows_at(source * 2 + core)], row_sems.at[2 * hop])
        )
        row_copies.append(
            copy_in(
                other[hop].at[0:TOK], rows.at[rows_at(source * 2 + 1 - core)], row_sems.at[2 * hop + 1]
            )
        )
    order = (0, 1, 2, 3, 6, 7, 8, 9, 4, 5)
    copies = {i: copy_in(sources[i], held[i], in_sems.at[i]) for i in order}
    key_copy = copy_in(refs[19], key_pos, in_sems.at[10])
    for moving in row_copies:
        moving.wait()
    rows_copy = copy_in(rows, rows_out, out_sems.at[0])
    for source in range(CHIPS):
        own[source * TOK : (source + 1) * TOK, :] = rows[rows_at(2 * source + core), :]
    copies[0].wait()
    copies[1].wait()

    @pl.loop(0, 4)
    def _(tile):
        at = pl.ds(pl.multiple_of(tile * 256, 256), 256)
        block = rows[at, :]
        keys[at, :] = nn(block, key_w[...]).astype(BF16)
        low = nn(block, value_w[...]).astype(BF16)
        values[at, :] = low
        for i in range(PAIRS):
            value_t[i, at, 0:LANES] = low[:, i * LANES : (i + 1) * LANES]
            value_t[i, at, LANES : 2 * LANES] = jnp.ones((256, LANES), BF16)

    keys_copy = copy_in(keys, keys_out, out_sems.at[1])
    values_copy = copy_in(values, values_out, out_sems.at[2])
    mine = own[...]
    for r in range(2):
        copies[2 + r].wait()
        full = nn(mine, query_w[r][...]).astype(BF16)
        queries[r] = full * jnp.asarray(0.125, BF16)
    copies[6].wait()
    copies[7].wait()
    weights = masked_softmax(nt(mine, router[...]), chosen[...] > 0.0)
    gates[...] = weights
    gates_copy = copy_in(gates, gates_out, out_sems.at[3])
    spread[...] = jnp.zeros_like(spread)
    copies[8].wait()
    copies[9].wait()
    key_copy.wait()
    for part in range(8):
        at = slice(part * TOK, (part + 1) * TOK)
        key_row[:, at] = key_pos[at, :].astype(F32).T[:8].astype(I32)

    @pl.loop(0, blocks)
    def _(j):
        start = j * TOK
        here = pl.ds(pl.multiple_of(start, TOK), TOK)
        take = iota((TOK, HALF), 0) + start
        packed = sum(
            nn(onehot(pos_row[r : r + 1, :] == take), queries[r]) for r in range(2)
        ).astype(BF16)
        q_held[here, :] = packed
        copy_in(q_held.at[here], q_out.at[here], block_sems.at[0, j])
        for rows_now, span, level in LEVELS:
            pl.when(scal[0, j] == level)(
                functools.partial(
                    attend_level, rows_now, span, start, keys, value_t, key_row, q_held, o_held, logs
                )
            )
        lse[j] = logs[...].T[:8]
        copy_in(o_held.at[here], o_out.at[here], block_sems.at[1, j])
        block = o_held[here, :]
        put = iota((HALF, TOK), 1) + start
        for r in range(2):
            spread[r] += nn(onehot(pos_col[:, r : r + 1] == put), block)

    lse_copy = copy_in(lse, lse_out, out_sems.at[4])
    copies[4].wait()
    copies[5].wait()
    mixture = jnp.zeros((HALF, WIDTH), F32)
    for r in range(2):
        full = spread[r].astype(BF16)
        o_spread[r] = full
        expert = 2 * chip + (core if r == 0 else 1 - core)
        mixture = mixture + column(gates[...], expert) * nn(full, out_w[r][...])
    staged[...] = mixture.astype(BF16)
    final = [
        copy_in(staged.at[rows_at(lax.rem(chip + hop, CHIPS))], outs[hop], row_sems.at[hop])
        for hop in range(CHIPS)
    ]
    final.append(copy_in(o_spread.at[0], spread_0, out_sems.at[5]))
    final.append(copy_in(o_spread.at[1], spread_1, out_sems.at[6]))

    @pl.loop(0, blocks)
    def _(j):
        here = rows_at(j)
        pltpu.make_async_copy(q_held.at[here], q_out.at[here], block_sems.at[0, j]).wait()
        pltpu.make_async_copy(o_held.at[here], o_out.at[here], block_sems.at[1, j]).wait()

    for moving in [rows_copy, keys_copy, values_copy, gates_copy, lse_copy, *final]:
        moving.wait()


def attend(table, same, other, key_w, value_w, query_w, out_w, router, plan, vmem):
    outs = [like((TOK, WIDTH), BF16)] * 4 + [
        like((SEQ, WIDTH), BF16),
        like((SEQ, WIDTH), BF16),
        like((SEQ, WIDTH), BF16),
        like((SEQ, WIDTH), BF16),
        like((SEQ, WIDTH), BF16),
        like((HALF, WIDTH), BF16),
        like((HALF, WIDTH), BF16),
        like((8, 8, 2 * TOK), F32),
        like((HALF, LANES), F32),
    ]
    square = pltpu.VMEM((WIDTH, WIDTH), BF16)
    scratch = [
        pltpu.VMEM((SEQ, WIDTH), BF16),
        pltpu.VMEM((HALF, WIDTH), BF16),
        pltpu.VMEM((SEQ, WIDTH), BF16),
        pltpu.VMEM((SEQ, WIDTH), BF16),
        pltpu.VMEM((PAIRS, SEQ, 2 * LANES), BF16),
        square,
        square,
        square,
        square,
        square,
        square,
        pltpu.VMEM((LANES, WIDTH), BF16),
        pltpu.VMEM((HALF, LANES), F32),
        pltpu.VMEM((8, HALF), I32),
        pltpu.VMEM((HALF, LANES), I32),
        pltpu.VMEM((SEQ, LANES), I32),
        pltpu.VMEM((2, HALF, WIDTH), BF16),
        pltpu.VMEM((SEQ, WIDTH), BF16),
        pltpu.VMEM((SEQ, WIDTH), BF16),
        pltpu.VMEM((2, HALF, WIDTH), F32),
        pltpu.VMEM((2, HALF, WIDTH), BF16),
        pltpu.VMEM((HALF, WIDTH), BF16),
        pltpu.VMEM((8, 8, 2 * TOK), F32),
        pltpu.VMEM((HALF, LANES), F32),
        pltpu.VMEM((8, SEQ), I32),
        pltpu.VMEM((2 * TOK, LANES), F32),
        pltpu.SemaphoreType.DMA((11,)),
        pltpu.SemaphoreType.DMA((8,)),
        pltpu.SemaphoreType.DMA((7,)),
        pltpu.SemaphoreType.DMA((2, 8)),
    ]
    args = [
        table, *same, *other, key_w, value_w, *query_w, *out_w, router,
        plan["chosen"], plan["pos_row"], plan["pos_col"], plan["key_pos"],
    ]
    return call_any("attend", attend_kernel, outs, args, scratch, 6 * 10**9, vmem, range(1, 9), range(4))


def back_level(
    rows, span, start, keys, values, key_pos, q_held, o_held, packed, logs, inner,
    sum_k, sum_v, part_q, block,
):
    here = packed_rows(start, rows)
    lanes = iota((2 * rows, LANES), 1)
    inners = jnp.zeros((2 * rows, LANES), F32)
    for i in range(PAIRS):
        at = slice(i * LANES, (i + 1) * LANES)
        held = o_held[here, at].astype(F32)
        grads = split_heads(packed[0:rows, at]).astype(F32)
        inners = jnp.where(lanes == i, row_sum(grads * jnp.concatenate([held, held], 0)), inners)
    inner[:, 0 : 2 * rows] = inners.T[:8]

    @pl.loop(0, PAIRS, unroll=UNROLL)
    def _(i):
        pair = pl.ds(pl.multiple_of(i * LANES, LANES), LANES)
        key_block = keys[0:span, pair]
        queries, grads = split_heads(q_held[here, pair]), split_heads(packed[0:rows, pair])
        probs = jnp.exp(nt(key_block, queries) - logs[pl.ds(i, 1), 0 : 2 * rows])
        probs = jnp.where(allowed_keys(key_pos, span, start, rows), probs, 0.0)
        grad_probs = nt(values[0:span, pair], grads)
        grad_scores = (probs * (grad_probs - inner[pl.ds(i, 1), 0 : 2 * rows])).astype(BF16)
        sum_k[0:span, pair] += nn(grad_scores, queries)
        sum_v[0:span, pair] += nn(probs.astype(BF16), grads)
        part_q[i, 0 : 2 * rows] = tn(grad_scores, key_block)

    for i in range(PAIRS):
        at = slice(i * LANES, (i + 1) * LANES)
        block[0:rows, at] = (join_heads(part_q[i, 0 : 2 * rows], rows) * 0.125).astype(BF16)
    if rows < TOK:
        block[rows:TOK, :] = jnp.zeros((TOK - rows, WIDTH), BF16)


def attend_back_kernel(*refs):
    scal = refs[0]
    arrived = refs[1:5]
    sources = refs[5:26]
    same, other = refs[26:30], refs[30]
    y_out, q_out, k_out, v_out, tiny_out = refs[31:33], refs[33:35], refs[35], refs[36], refs[37]
    upstream = refs[38]
    held = refs[39:60]
    (
        out_0, out_1, gates, spread_0, spread_1, pos_row, q_held, o_held, lse, keys, values,
        key_pos, pos_col, query_0, query_1, key_w, value_w, rows, router, gain, tiny,
    ) = held
    grad_o, sum_k, sum_v, sum_q, part_q, packed_s, block_q, logs, inner, own, gate_low = refs[60:71]
    grad_y, grad_q, grad_k, grad_v, same_s, other_s = refs[71:77]
    in_sems, row_sems, out_sems = refs[77:80]
    o_spread = (spread_0, spread_1)
    query_w, out_w = (query_0, query_1), (out_0, out_1)
    blocks, chip, core = scal[0, 8], scal[0, 9], scal[0, 10]

    row_copies = [
        copy_in(
            arrived[hop],
            upstream.at[rows_at(lax.rem(chip - hop + CHIPS, CHIPS))],
            row_sems.at[hop],
        )
        for hop in range(CHIPS)
    ]
    copies = [copy_in(sources[i], held[i], in_sems.at[i]) for i in range(21)]
    sum_k[...] = jnp.zeros_like(sum_k)
    sum_v[...] = jnp.zeros_like(sum_v)
    sum_q[...] = jnp.zeros_like(sum_q)
    for moving in row_copies + copies[0:5]:
        moving.wait()
    lanes = iota((HALF, LANES), 1)
    gate_grads = jnp.zeros((HALF, LANES), F32)
    for r in range(2):
        expert = 2 * chip + (core if r == 0 else 1 - core)
        gate = column(gates[...], expert)
        raw = nt(upstream[...], out_w[r][...])
        gate_grads = jnp.where(
            lanes == expert, row_sum(o_spread[r][...].astype(F32) * raw), gate_grads
        )
        grad_o[r] = (gate * raw).astype(BF16)
        grad_y[r] = (gate * upstream[...].astype(F32)).astype(BF16)
    y_copies = [copy_in(grad_y.at[r], y_out[r], out_sems.at[r]) for r in range(2)]
    weights = gates[...]
    gate_low[...] = (weights * (gate_grads - row_sum(weights * gate_grads))).astype(BF16)
    for moving in copies[5:13]:
        moving.wait()

    @pl.loop(0, blocks)
    def _(j):
        start = j * TOK
        here = pl.ds(pl.multiple_of(start, TOK), TOK)
        take = iota((TOK, HALF), 0) + start
        packed = sum(
            nn(onehot(pos_row[r : r + 1, :] == take), grad_o[r]) for r in range(2)
        ).astype(BF16)
        packed_s[...] = packed
        logs[...] = lse[j]
        for rows_now, span, level in LEVELS:
            pl.when(scal[0, j] == level)(
                functools.partial(
                    back_level, rows_now, span, start, keys, values, key_pos, q_held, o_held,
                    packed_s, logs, inner, sum_k, sum_v, part_q, block_q,
                )
            )

        block = block_q[...]
        put = iota((HALF, TOK), 1) + start
        for r in range(2):
            sum_q[r] += nn(onehot(pos_col[:, r : r + 1] == put), block)

    for r in range(2):
        grad_q[r] = sum_q[r].astype(BF16)
    q_copies = [copy_in(grad_q.at[r], q_out[r], out_sems.at[2 + r]) for r in range(2)]
    for moving in copies[13:21]:
        moving.wait()
    for source in range(CHIPS):
        own[source * TOK : (source + 1) * TOK, :] = rows[rows_at(2 * source + core), :]
    sum_q[0] = (
        nt(grad_q[0], query_w[0][...])
        + nt(grad_q[1], query_w[1][...])
        + nn(gate_low[...], router[...])
    )
    gain_part = jnp.sum(sum_q[0] * own[...].astype(F32), 0, keepdims=True)
    sum_q[1, 0:1, :] = gain_part

    @pl.loop(0, 4)
    def _(tile):
        at = pl.ds(pl.multiple_of(tile * 256, 256), 256)
        low_k, low_v = sum_k[at, :].astype(BF16), sum_v[at, :].astype(BF16)
        grad_k[at, :] = low_k
        grad_v[at, :] = low_v
        total = nt(low_k, key_w[...]) + nt(low_v, value_w[...])
        sum_k[at, :] = total
        sum_q[1, 0:1, :] += jnp.sum(total * rows[at, :].astype(F32), 0, keepdims=True)

    k_copy = copy_in(grad_k, k_out, out_sems.at[4])
    v_copy = copy_in(grad_v, v_out, out_sems.at[5])
    final = []
    for hop in range(CHIPS):
        target = lax.rem(chip + hop, CHIPS)
        other_s[hop] = sum_k[rows_at(target * 2 + 1 - core), :].astype(BF16)
    final.append(copy_in(other_s, other, out_sems.at[6]))
    for hop in range(CHIPS):
        target = lax.rem(chip + hop, CHIPS)
        same_s[hop] = (
            sum_k[rows_at(target * 2 + core), :] + sum_q[0, rows_at(target), :]
        ).astype(BF16)
        final.append(copy_in(same_s.at[hop], same[hop], row_sems.at[hop]))
    tiny[...] += tn(own[...], gate_low[...]) + lane_of(sum_q[1, 0:1, :] / gain[...], 8)
    final.append(copy_in(tiny, tiny_out, out_sems.at[7]))
    for moving in [*y_copies, *q_copies, k_copy, v_copy, *final]:
        moving.wait()


def attend_back(table, arrived, held, key_w, value_w, query_w, out_w, plan, rest, vmem):
    outs = [like((TOK, WIDTH), BF16)] * 4 + [
        like((CHIPS, TOK, WIDTH), BF16),
        like((HALF, WIDTH), BF16),
        like((HALF, WIDTH), BF16),
        like((HALF, WIDTH), BF16),
        like((HALF, WIDTH), BF16),
        like((SEQ, WIDTH), BF16),
        like((SEQ, WIDTH), BF16),
        like((WIDTH, LANES), F32),
    ]
    keys, values, q_held, o_held, spread_0, spread_1, lse, gates = held
    sources = [
        *out_w, gates, spread_0, spread_1, plan["pos_row"], q_held, o_held, lse, keys, values,
        plan["key_pos"], plan["pos_col"], *query_w, key_w, value_w, *rest,
    ]
    scratch = [pltpu.VMEM((HALF, WIDTH), BF16)]
    scratch += [pltpu.VMEM(a.shape, a.dtype) for a in sources]
    scratch += [
        pltpu.VMEM((2, HALF, WIDTH), BF16),
        pltpu.VMEM((SEQ, WIDTH), F32),
        pltpu.VMEM((SEQ, WIDTH), F32),
        pltpu.VMEM((2, HALF, WIDTH), F32),
        pltpu.VMEM((PAIRS, 2 * TOK, LANES), F32),
        pltpu.VMEM((TOK, WIDTH), BF16),
        pltpu.VMEM((TOK, WIDTH), BF16),
        pltpu.VMEM((8, 2 * TOK), F32),
        pltpu.VMEM((8, 2 * TOK), F32),
        pltpu.VMEM((HALF, WIDTH), BF16),
        pltpu.VMEM((HALF, LANES), BF16),
        pltpu.VMEM((2, HALF, WIDTH), BF16),
        pltpu.VMEM((2, HALF, WIDTH), BF16),
        pltpu.VMEM((SEQ, WIDTH), BF16),
        pltpu.VMEM((SEQ, WIDTH), BF16),
        pltpu.VMEM((CHIPS, TOK, WIDTH), BF16),
        pltpu.VMEM((CHIPS, TOK, WIDTH), BF16),
        pltpu.SemaphoreType.DMA((21,)),
        pltpu.SemaphoreType.DMA((4,)),
        pltpu.SemaphoreType.DMA((8,)),
    ]
    args = [table, *arrived, *sources]
    return call_any("attend_back", attend_back_kernel, outs, args, scratch, 10**11, vmem, range(1, 5), range(5))


def pair_sum_kernel(*refs):
    other, outs = refs[4], refs[5:]
    for hop in range(CHIPS):
        outs[hop][...] = (refs[hop][...].astype(F32) + other[hop].astype(F32)).astype(BF16)


def pair_sum(same, other, vmem):
    return call("pair_sum", pair_sum_kernel, [like((TOK, WIDTH), BF16)] * 4, [*same, other], near=range(5), near_out=range(4), vmem=vmem)


def expert_weights_kernel(first, *refs):
    scal, rows = refs[0:2]
    mixes, grad_y, grad_q = refs[2:4], refs[4:6], refs[6:8]
    before = None if first else refs[8]
    after, own = refs[8 if first else 9 :]
    core = scal[0, 10]
    for side in range(2):
        for source in range(CHIPS):
            own[side, source * TOK : (source + 1) * TOK, :] = rows[
                rows_at(2 * source + (core if side == 0 else 1 - core)), :
            ]
    halves = (
        tn(own[0], grad_q[0][...]) + tn(own[1], grad_q[1][...]),
        tn(mixes[0][...], grad_y[0][...]) + tn(mixes[1][...], grad_y[1][...]),
    )
    for half, value in enumerate(halves):
        at = slice(half * WIDTH, (half + 1) * WIDTH)
        if not first:
            value = value + before[:, at]
        after[:, at] = value.astype(after.dtype)


def expert_weights(table, rows, mixes, grad_y, grad_q, before, last, vmem):
    first = before is None
    args = [table, rows, *mixes, *grad_y, *grad_q, *(() if first else (before,))]
    outs = [like((WIDTH, 2 * WIDTH), BF16 if last else F32)]
    return call(
        "expert_weights",
        functools.partial(expert_weights_kernel, first),
        outs,
        args,
        [pltpu.VMEM((2, HALF, WIDTH), BF16)],
        smem=(0,),
        flops=3 * 10**9,
        vmem=vmem,
    )[0]


def shared_weights_kernel(first, rows, grad_k, grad_v, *refs):
    after = refs[-1]
    for half, grad in enumerate((grad_k, grad_v)):
        at = slice(half * WIDTH, (half + 1) * WIDTH)
        value = tn(rows[...], grad[...])
        if not first:
            value = value + refs[0][:, at]
        after[:, at] = value.astype(after.dtype)


def shared_last_kernel(*refs):
    scal, far, outs = refs[0], refs[1:6], refs[6:8]
    held, (total, packed, in_sems, out_sems) = refs[8:13], refs[13:]
    rows, grad_k, before, grad_v, tiny = held
    copies = [copy_in(far[n], held[n], in_sems.at[n]) for n in range(5)]
    for n in range(3):
        copies[n].wait()
    total[:, 0:WIDTH] = (tn(rows[...], grad_k[...]) + before[:, 0:WIDTH]).astype(BF16)
    copies[3].wait()
    copies[4].wait()
    total[:, WIDTH : 2 * WIDTH] = (
        tn(rows[...], grad_v[...]) + before[:, WIDTH : 2 * WIDTH]
    ).astype(BF16)
    total[:, 2 * WIDTH :] = tiny[...].astype(BF16)
    row = iota((WIDTH, WIDTH), 0)
    side, hop, spot = row >> 8, (row >> 6) & 3, (row >> 2) & 15
    owner = ((scal[0, 9] + hop) & 3) * 2 + (side ^ scal[0, 10])
    source = spot * 32 + owner * 4 + (row & 3)
    pick = onehot(source == iota((WIDTH, WIDTH), 1))
    packed[...] = nn(pick, total[...]).astype(BF16).reshape(2, CHIPS, 64, SHARED)
    leaving = [copy_in(packed.at[n], outs[n], out_sems.at[n]) for n in range(2)]
    for copy in leaving:
        copy.wait()


def shared_last(table, rows, grad_k, grad_v, before, tiny):
    args = [rows, grad_k, before, grad_v, tiny]
    scratch = [pltpu.VMEM(a.shape, a.dtype) for a in args] + [
        pltpu.VMEM((WIDTH, SHARED), BF16),
        pltpu.VMEM((2, CHIPS, 64, SHARED), BF16),
        pltpu.SemaphoreType.DMA((5,)),
        pltpu.SemaphoreType.DMA((2,)),
    ]
    outs = [like((CHIPS, 64, SHARED), BF16)] * 2
    return call_any(
        "shared_last", shared_last_kernel, outs, [table, *args], scratch, 4 * 10**9, 60, (), ()
    )


def core_sum_kernel(mine, other, *outs):
    for hop in range(CHIPS):
        outs[hop][...] = (mine[hop].astype(F32) + other[hop].astype(F32)).astype(BF16)


def core_sum(mine, other):
    outs = [like((64, SHARED), BF16)] * CHIPS
    return call("core_sum", core_sum_kernel, outs, [mine, other], vmem=60)


def last_weights_kernel(*refs):
    scal, far, out = refs[0], refs[1:13], refs[13]
    held, (own, total, in_sems, out_sem) = refs[14:26], refs[26:]
    rows, q_0, q_1, expert_acc, mix_0, y_0, mix_1, y_1 = held[:8]
    parts = held[8:]
    copies = [copy_in(far[n], held[n], in_sems.at[n]) for n in range(12)]
    core = scal[0, 10]
    copies[0].wait()
    for side in range(2):
        for source in range(CHIPS):
            own[side, source * TOK : (source + 1) * TOK, :] = rows[
                rows_at(2 * source + (core if side == 0 else 1 - core)), :
            ]
    for n in range(1, 4):
        copies[n].wait()
    value = tn(own[0], q_0[...]) + tn(own[1], q_1[...]) + expert_acc[:, 0:WIDTH]
    total[:, 0:32, :] = value.astype(BF16).reshape(16, 32, WIDTH)
    for n in range(4, 8):
        copies[n].wait()
    value = tn(mix_0[...], y_0[...]) + tn(mix_1[...], y_1[...]) + expert_acc[:, WIDTH : 2 * WIDTH]
    total[:, 32:64, :] = value.astype(BF16).reshape(16, 32, WIDTH)
    for n in range(8, 12):
        copies[n].wait()
    summed = sum(p[...].astype(F32) for p in parts).astype(BF16)
    small = jnp.concatenate(
        [summed[:, 2 * WIDTH :], jnp.zeros((64, WIDTH - LANES), BF16)], 1
    )
    row, col = iota((256, 64), 0), iota((256, 64), 1)
    spread = jnp.zeros((256, WIDTH), F32)
    for n, value in enumerate((summed[:, 0:WIDTH], summed[:, WIDTH : 2 * WIDTH], small)):
        pick = onehot(((row >> 4) * 4 + (row & 15) - 4 * n == col) & (((row >> 2) & 3) == n))
        spread = spread + nn(pick, value)
    total[:, 64:80, :] = spread.astype(BF16).reshape(16, 16, WIDTH)
    copy_in(total, out, out_sem.at[0]).wait()


def last_weights(table, rows, mixes, grad_y, grad_q, expert_acc, parts):
    args = [rows, *grad_q, expert_acc, mixes[0], grad_y[0], mixes[1], grad_y[1], *parts]
    scratch = [pltpu.VMEM(a.shape, a.dtype) for a in args] + [
        pltpu.VMEM((2, HALF, WIDTH), BF16),
        pltpu.VMEM((16, 80, WIDTH), BF16),
        pltpu.SemaphoreType.DMA((12,)),
        pltpu.SemaphoreType.DMA((1,)),
    ]
    outs = [like((16, 80, WIDTH), BF16)]
    return call_any(
        "last_weights", last_weights_kernel, outs, [table, *args], scratch, 4 * 10**9, 60, (), ()
    )[0]


SHARED = 2 * WIDTH + LANES


def shared_weights(rows, grad_k, grad_v, before, vmem=20):
    first = before is None
    args = [rows, grad_k, grad_v, *(() if first else (before,))]
    outs = [like((WIDTH, 2 * WIDTH), F32)]
    kernel = functools.partial(shared_weights_kernel, first)
    return call("shared_weights", kernel, outs, args, flops=3 * 10**9, vmem=vmem)[0]


def slot_pick(shape, r, row_dim):
    row, col = iota(shape, row_dim), iota(shape, 1 - row_dim)
    skip = SLOTS * r
    for source in range(1, CHIPS):
        skip = skip + jnp.where(row >= SLOTS * source, SLOTS, 0)
    return onehot(col == row + skip)


ROWS = CHIPS * SLOTS
BLOCK = 2 * SLOTS


def gelu_parts(x):
    scale = 0.7978845608028654
    inner = scale * (x + 0.044715 * x * x * x)
    return jnp.tanh(inner), scale * (1.0 + 3.0 * 0.044715 * x * x)


def store_blocks(results, outs):
    full = sum(
        nn(slot_pick((2 * ROWS, ROWS), r, 1), results[r].astype(BF16)) for r in range(2)
    ).astype(BF16)
    for hop in range(CHIPS):
        outs[hop][...] = full[hop * BLOCK : (hop + 1) * BLOCK]


def hidden_at(step):
    return slice(step * PART, (step + 1) * PART)


def fetch_weights(win, wout, win_far, wout_far, sems):
    copies = []
    for step in range(FFN // PART):
        at = hidden_at(step)
        now = []
        for r in range(2):
            now.append((win_far[r].at[:, at], win.at[r, :, at]))
            now.append((wout_far[r].at[at, :], wout.at[r, at, :]))
        copies.append([copy_in(src, dst, sems.at[step, n]) for n, (src, dst) in enumerate(now)])
    return copies


def feed_kernel(*refs):
    blocks, win_far, wout_far = refs[0:4], refs[4:6], refs[6:8]
    outs, received_out = refs[8:12], refs[12:14]
    win, wout, received, weight_sems, out_sems = refs[14:]
    copies = fetch_weights(win, wout, win_far, wout_far, weight_sems)
    full = jnp.concatenate([b[...] for b in blocks], 0)
    leaving = []
    for r in range(2):
        received[r] = nn(slot_pick((ROWS, 2 * ROWS), r, 0), full).astype(BF16)
        leaving.append(copy_in(received.at[r], received_out[r], out_sems.at[r]))
    total = [jnp.zeros((ROWS, WIDTH), F32)] * 2
    for step in range(FFN // PART):
        at = hidden_at(step)
        for copy in copies[step]:
            copy.wait()
        for r in range(2):
            pre = nn(received[r], win[r, :, at])
            bend, _ = gelu_parts(pre)
            total[r] = total[r] + nn((0.5 * pre * (1.0 + bend)).astype(BF16), wout[r, at, :])
    store_blocks(total, outs)
    for copy in leaving:
        copy.wait()


NEAR = pl.BlockSpec(memory_space=pltpu.VMEM)


def feed(blocks, win, wout):
    return pl.pallas_call(
        feed_kernel,
        in_specs=[NEAR] * 4 + [FAR] * 4,
        out_specs=tuple([NEAR] * 4 + [FAR] * 2),
        out_shape=tuple([like((BLOCK, WIDTH), BF16)] * 4 + [like((ROWS, WIDTH), BF16)] * 2),
        scratch_shapes=[
            pltpu.VMEM((2, WIDTH, FFN), BF16),
            pltpu.VMEM((2, FFN, WIDTH), BF16),
            pltpu.VMEM((2, ROWS, WIDTH), BF16),
            pltpu.SemaphoreType.DMA((FFN // PART, 4)),
            pltpu.SemaphoreType.DMA((2,)),
        ],
        compiler_params=pltpu.CompilerParams(vmem_limit_bytes=24 * 2**20),
        cost_estimate=pl.CostEstimate(flops=2 * 10**9, bytes_accessed=10**7, transcendentals=10**6),
        name="feed",
    )(*blocks, *win, *wout)


def feed_back_kernel(*refs):
    blocks, received_far, win_far, wout_far = refs[0:4], refs[4:6], refs[6:8], refs[8:10]
    outs, rows_out, acts_out, pre_out = refs[10:14], refs[14:16], refs[16:18], refs[18:20]
    win, wout, received, grad_rows, acts, grad_pre = refs[20:26]
    weight_sems, in_sems, out_sems = refs[26:]
    arriving = [copy_in(received_far[r], received.at[r], in_sems.at[r]) for r in range(2)]
    copies = fetch_weights(win, wout, win_far, wout_far, weight_sems)
    full = jnp.concatenate([b[...] for b in blocks], 0)
    leaving = []
    for r in range(2):
        grad_rows[r] = nn(slot_pick((ROWS, 2 * ROWS), r, 0), full).astype(BF16)
        leaving.append(copy_in(grad_rows.at[r], rows_out[r], out_sems.at[r]))
    for copy in arriving:
        copy.wait()
    total = [jnp.zeros((ROWS, WIDTH), F32)] * 2
    for step in range(FFN // PART):
        at = hidden_at(step)
        for copy in copies[step]:
            copy.wait()
        for r in range(2):
            pre = nn(received[r], win[r, :, at])
            bend, slope = gelu_parts(pre)
            acts[r, :, at] = (0.5 * pre * (1.0 + bend)).astype(BF16)
            grad_act = nt(grad_rows[r], wout[r, at, :])
            inner = 0.5 * (1.0 + bend) + 0.5 * pre * (1.0 - bend * bend) * slope
            low = (grad_act * inner).astype(BF16)
            grad_pre[r, :, at] = low
            total[r] = total[r] + nt(low, win[r, :, at])
    for r in range(2):
        leaving.append(copy_in(acts.at[r], acts_out[r], out_sems.at[2 + r]))
        leaving.append(copy_in(grad_pre.at[r], pre_out[r], out_sems.at[4 + r]))
    store_blocks(total, outs)
    for copy in leaving:
        copy.wait()


def feed_back(blocks, received, win, wout):
    return pl.pallas_call(
        feed_back_kernel,
        in_specs=[NEAR] * 4 + [FAR] * 6,
        out_specs=tuple([NEAR] * 4 + [FAR] * 6),
        out_shape=tuple(
            [like((BLOCK, WIDTH), BF16)] * 4
            + [like((ROWS, WIDTH), BF16)] * 2
            + [like((ROWS, FFN), BF16)] * 4
        ),
        scratch_shapes=[
            pltpu.VMEM((2, WIDTH, FFN), BF16),
            pltpu.VMEM((2, FFN, WIDTH), BF16),
            pltpu.VMEM((2, ROWS, WIDTH), BF16),
            pltpu.VMEM((2, ROWS, WIDTH), BF16),
            pltpu.VMEM((2, ROWS, FFN), BF16),
            pltpu.VMEM((2, ROWS, FFN), BF16),
            pltpu.SemaphoreType.DMA((FFN // PART, 4)),
            pltpu.SemaphoreType.DMA((2,)),
            pltpu.SemaphoreType.DMA((6,)),
        ],
        compiler_params=pltpu.CompilerParams(vmem_limit_bytes=28 * 2**20),
        cost_estimate=pl.CostEstimate(flops=3 * 10**9, bytes_accessed=10**7, transcendentals=10**6),
        name="feed_back",
    )(*blocks, *received, *win, *wout)


def feed_weights_kernel(*refs):
    far, out = refs[0:24], refs[24]
    received, grad_rows, acts, grad_pre, total, in_sems, out_sem = refs[25:]
    held = (received, grad_pre, grad_rows, acts)
    copies = [
        [
            copy_in(far[6 * n + s], held[n].at[ROWS * s : ROWS * (s + 1)], in_sems.at[n, s])
            for s in range(6)
        ]
        for n in range(4)
    ]
    for copy in copies[0] + copies[1]:
        copy.wait()
    for step in range(FFN // PART):
        value = tn(received[...], grad_pre[:, hidden_at(step)]).astype(BF16)
        total[:, step * 32 : (step + 1) * 32, :] = value.reshape(16, 32, PART)
    for copy in copies[2] + copies[3]:
        copy.wait()
    for step in range(FFN // PART):
        value = tn(acts[:, hidden_at(step)], grad_rows[...]).astype(BF16)
        total[4 * step : 4 * step + 4, TOK : 2 * TOK, :] = value.reshape(4, TOK, WIDTH)
    leaving = copy_in(total, out, out_sem.at[0])
    leaving.wait()


def feed_weights(received, grad_rows, acts, grad_pre):
    return pl.pallas_call(
        feed_weights_kernel,
        in_specs=[FAR] * 24,
        out_specs=FAR,
        out_shape=like((16, 2 * TOK, WIDTH), BF16),
        scratch_shapes=[
            pltpu.VMEM((6 * ROWS, WIDTH), BF16),
            pltpu.VMEM((6 * ROWS, WIDTH), BF16),
            pltpu.VMEM((6 * ROWS, FFN), BF16),
            pltpu.VMEM((6 * ROWS, FFN), BF16),
            pltpu.VMEM((16, 2 * TOK, WIDTH), BF16),
            pltpu.SemaphoreType.DMA((4, 6)),
            pltpu.SemaphoreType.DMA((1,)),
        ],
        compiler_params=pltpu.CompilerParams(vmem_limit_bytes=60 * 2**20),
        cost_estimate=pl.CostEstimate(flops=8 * 10**9, bytes_accessed=2 * 10**7, transcendentals=0),
        name="feed_weights",
    )(*received, *grad_pre, *grad_rows, *acts)


def first_norm_kernel(block, gain, depth, wide, normed, payload, tail):
    value = block[...].astype(F32)
    wide[...] = value
    low = (norm_parts(value)[0] * gain[...]).astype(BF16)
    normed[...] = low
    payload[0:TOK, :] = low
    tail[...] = jnp.zeros_like(tail)
    tail[0:1, 0:TOK] = depth[...].astype(F32)
    payload[TOK : TOK + 16, :] = tail[...].astype(BF16)


def first_norm(block, gain, depth):
    outs = [
        like((TOK, WIDTH), F32),
        like((TOK, WIDTH), BF16),
        like((TOK + 16, WIDTH), BF16),
    ]
    scratch = [pltpu.VMEM((16, WIDTH), F32)]
    args = [block, gain, depth]
    return call("first_norm", first_norm_kernel, outs, args, scratch, near_out=(2,), vmem=60)


def attend_plan_kernel(steps, *refs):
    place, choices = refs[0], refs[1]
    blocks = refs[2:10] if 0 not in steps else ()
    outs = refs[2 + len(blocks) :]
    outs, (spots, named_all, depth_col, tails, sems) = outs[: 5 * len(steps)], outs[5 * len(steps) :]
    chip, core = place[0], place[1]
    dp_row, dp_col = place[2], place[3]
    token = iota((SEQ, LANES), 0)
    lanes = iota((SEQ, LANES), 1)
    held = ((token // TOK) % 2) == core
    if blocks:
        copies = [
            copy_in(ref.at[TOK : TOK + 16, 0:TOK], tails.at[n], sems.at[n])
            for n, ref in enumerate(blocks)
        ]
        for copy in copies:
            copy.wait()
        for hop in range(CHIPS):
            source = lax.rem(chip - hop + CHIPS, CHIPS)
            for side, n in ((core, hop), (1 - core, CHIPS + hop)):
                rows = tails[n].astype(F32)
                rows = jnp.concatenate([rows, jnp.zeros((TOK - 16, TOK), F32)], 0)
                depth_col[rows_at(source * 2 + side), :] = rows.T
    before = onehot(iota((SEQ, SEQ), 1) < iota((SEQ, SEQ), 0))
    for n, s in enumerate(steps):
        table, chosen_out, row_out, col_out, key_out = outs[5 * n : 5 * n + 5]
        turned = jnp.concatenate([choices[s].astype(F32), jnp.zeros((4, SEQ), F32)], 0).T
        named_here = named(turned.astype(I32), 4)
        named_all[...] = jnp.where(named_here, 1.0, 0.0)
        live = held[:, 0:1]
        if blocks:
            live = live & (depth_col[:, 0:1] > s + 0.5)
        live = jnp.where(live, 1.0, 0.0)
        hits = [
            row_sum(jnp.where(lanes == 2 * chip + side, named_all[...], 0.0)) * live
            for side in (core, 1 - core)
        ]
        count = hits[0] + hits[1]
        base = nn(before, jnp.broadcast_to(count, (SEQ, LANES)).astype(BF16))
        key_out[...] = base.astype(I32)
        spot = jnp.where(
            lanes == 0,
            jnp.where(hits[0] > 0, base, -1.0),
            jnp.where(hits[1] > 0, base + hits[0], -1.0),
        )
        spots[...] = jnp.where(lanes < 2, spot, -1.0)
        for source in range(CHIPS):
            at = slice(source * TOK, (source + 1) * TOK)
            chosen_out[at, :] = named_all[rows_at(2 * source + core), :]
            part = spots[rows_at(2 * source + core), :]
            col_out[at, :] = part.astype(I32)
            row_out[:, at] = part.T[:8].astype(I32)
        reach = jnp.sum(
            jnp.where(base <= (lanes * TOK + TOK - 1).astype(F32), 1.0, 0.0), 0, keepdims=True
        )
        total = jnp.sum(count, 0, keepdims=True).astype(I32)
        line = iota((8, LANES), 1)
        chunks = (reach.astype(I32) + (SPAN - 1)) // SPAN
        packed = (total + (TOK - 1)) // TOK
        short = (line == packed - 1) & (total - (packed - 1) * TOK <= TOK // 2)
        chunks = jnp.where(short, SMALL, chunks)
        table[...] = jnp.where(
            line < 8,
            chunks,
            packed,
        )
        for lane, value in ((9, chip), (10, core), (11, dp_row), (12, dp_col)):
            table[...] = jnp.where(line == lane, value, table[...])


def attend_plan(steps, place, choices, blocks):
    outs = [
        like((8, LANES), I32),
        like((HALF, LANES), F32),
        like((8, HALF), I32),
        like((HALF, LANES), I32),
        like((SEQ, LANES), I32),
    ] * len(steps)
    scratch = [pltpu.VMEM((SEQ, LANES), F32)] * 3
    scratch += [pltpu.VMEM((8, 16, TOK), BF16), pltpu.SemaphoreType.DMA((8,))]
    res = call(
        "attend_plan", functools.partial(attend_plan_kernel, steps), outs,
        [place, choices, *blocks], scratch, smem=(0,), raw=range(2, 10), flops=10**9, vmem=60,
    )
    names = ("table", "chosen", "pos_row", "pos_col", "key_pos")
    return [dict(zip(names, res[5 * n : 5 * n + 5])) for n in range(len(steps))]


def slot_plan_kernel(place, choices, depth, *outs):
    chip, core = place[0], place[1]
    depth_col = turned_row(depth[...])
    lanes = iota((TOK, LANES), 1)
    before = onehot(iota((TOK, TOK), 1) < iota((TOK, TOK), 0))
    hop = (lanes // 2 - chip + CHIPS) % CHIPS
    start = hop * BLOCK + jnp.where(lanes % 2 == core, 0, SLOTS)
    for s in range(3):
        turned = jnp.concatenate([choices[s].astype(F32), jnp.zeros((6, TOK), F32)], 0).T
        choice = turned.astype(I32)
        live = depth_col > s
        names = [lanes == choice[:, k : k + 1] for k in range(2)]
        hits = jnp.where((names[0] | names[1]) & live, 1.0, 0.0)
        spot = nn(before, hits.astype(BF16)) + start.astype(F32)
        table = jnp.full((TOK, LANES), -1.0, F32)
        for k in range(2):
            slot = jnp.where(live, row_sum(jnp.where(names[k], spot, 0.0)), -1.0)
            table = jnp.where(lanes == k, slot, table)
            table = jnp.where(lanes == 2 + k, choice[:, k : k + 1].astype(F32), table)
        outs[2 * s][...] = table.astype(I32)
        outs[2 * s + 1][...] = table.T[:8].astype(I32)


def slot_plan(place, choices, depth):
    outs = [like((TOK, LANES), I32), like((8, TOK), I32)] * 3
    res = call("slot_plan", slot_plan_kernel, outs, [place, choices, depth], smem=(0,))
    return list(res[0::2]), list(res[1::2])


def dispatch_kernel(*refs):
    state, parts = refs[0], refs[1:5]
    gain, router, slot_row, slot_col = refs[5:9]
    mixed_out, normed_out, gates_out = refs[9:12]
    sends = refs[12:16]
    mixed = state[...] + sum(p[...].astype(F32) for p in parts)
    mixed_out[...] = mixed
    normed = (norm_parts(mixed)[0] * gain[...]).astype(BF16)
    normed_out[...] = normed
    logits = nt(normed, router[...])
    picked = [column(logits, slot_col[:, 2 + k : 3 + k]) for k in range(2)]
    peak = jnp.maximum(picked[0], picked[1])
    weights = [jnp.exp(p - peak) for p in picked]
    total = weights[0] + weights[1]
    lanes = iota((TOK, LANES), 1)
    gates_out[...] = jnp.where(
        lanes == 0, weights[0] / total, jnp.where(lanes == 1, weights[1] / total, 0.0)
    )
    slots = iota((2 * ROWS, TOK), 0)
    hit = (slot_row[0:1, :] == slots) | (slot_row[1:2, :] == slots)
    full = nn(onehot(hit), normed).astype(BF16)
    for hop in range(CHIPS):
        sends[hop][...] = full[hop * BLOCK : (hop + 1) * BLOCK]


def dispatch(state, parts, gain, router, slot_row, slot_col):
    outs = [
        like((TOK, WIDTH), F32),
        like((TOK, WIDTH), BF16),
        like((TOK, LANES), F32),
    ] + [like((BLOCK, WIDTH), BF16)] * 4
    return call("dispatch", dispatch_kernel, outs, [state, *parts, gain, router, slot_row, slot_col], near=range(1, 5), near_out=range(3, 7))


def picked_rows(slot_col, returned):
    full = jnp.concatenate([b[...] for b in returned], 0)
    slots = iota((TOK, 2 * ROWS), 1)
    return [nn(onehot(slot_col[:, k : k + 1] == slots), full) for k in range(2)]


def next_state(mixed, state, gates, slot_col, rows):
    part = gates[:, 0:1] * rows[0] + gates[:, 1:2] * rows[1]
    return jnp.where(slot_col[:, 0:1] >= 0, mixed + part, state)


def advance_kernel(*refs):
    mixed, state, gates, slot_col = refs[0:4]
    returned, gain = refs[4:8], refs[8]
    state_out, normed_out = refs[9:11]
    rows = picked_rows(slot_col[...], returned)
    new = next_state(mixed[...], state[...], gates[...], slot_col[...], rows)
    state_out[...] = new
    normed_out[...] = (norm_parts(new)[0] * gain[...]).astype(BF16)


def advance(mixed, state, gates, slot_col, returned, gain):
    outs = [like((TOK, WIDTH), F32), like((TOK, WIDTH), BF16)]
    return call("advance", advance_kernel, outs, [mixed, state, gates, slot_col, *returned, gain], near=range(4, 8), near_out=(1,))


def send_grads(upstream, rows, gates, slot_row, slot_col, grad_z_out, gate_grads_out, sends):
    grad_z = jnp.where(slot_col[:, 0:1] >= 0, upstream, 0.0)
    grad_z_out[...] = grad_z
    lanes = iota((TOK, LANES), 1)
    gate_grads_out[...] = jnp.where(
        lanes == 0,
        row_sum(rows[0] * grad_z),
        jnp.where(lanes == 1, row_sum(rows[1] * grad_z), 0.0),
    )
    slots = iota((2 * ROWS, TOK), 0)
    full = sum(
        nn(onehot(slot_row[k : k + 1, :] == slots), (gates[:, k : k + 1] * grad_z).astype(BF16))
        for k in range(2)
    ).astype(BF16)
    for hop in range(CHIPS):
        sends[hop][...] = full[hop * BLOCK : (hop + 1) * BLOCK]


SEND_OUTS = [
    like((TOK, WIDTH), F32),
    like((TOK, LANES), F32),
] + [like((BLOCK, WIDTH), BF16)] * 4


def turn_kernel(*refs):
    mixed, state, gates, slot_col, slot_row = refs[0:5]
    returned = refs[5:9]
    first_state, halt, depth, cotangent = refs[9:13]
    output, coefs, tiny, upstream_out, grad_z, gate_grads = refs[13:19]
    sends = refs[19:23]
    rows = picked_rows(slot_col[...], returned)
    second = state[...]
    third = next_state(mixed[...], second, gates[...], slot_col[...], rows)
    first = first_state[...]
    vector = halt[...]
    grad = cotangent[...].astype(F32)
    p1 = jax.nn.sigmoid(row_sum(first * vector))
    p2 = jax.nn.sigmoid(row_sum(second * vector))
    a1, a2, a3 = row_sum(first * grad), row_sum(second * grad), row_sum(third * grad)
    steps = turned_row(depth[...])
    one, two, three = steps == 1, steps == 2, steps == 3
    c1 = jnp.where(one, 1.0, p1)
    c2 = jnp.where(one, 0.0, jnp.where(two, 1.0 - p1, p2 * (1.0 - p1)))
    c3 = jnp.where(three, (1.0 - p1) * (1.0 - p2), 0.0)
    output[...] = c1 * first + c2 * second + c3 * third
    d1 = jnp.where(
        two, a1 - a2, jnp.where(three, a1 - p2 * a2 - (1.0 - p2) * a3, 0.0)
    ) * (p1 * (1.0 - p1))
    d2 = jnp.where(three, (1.0 - p1) * (a2 - a3), 0.0) * (p2 * (1.0 - p2))
    tiny[...] = lane_of(jnp.sum(d1 * first + d2 * second, 0, keepdims=True), 25)
    lanes = iota((TOK, LANES), 1)
    table = jnp.zeros((TOK, LANES), F32)
    for lane, value in enumerate((c1, c2, c3, d1, d2)):
        table = jnp.where(lanes == lane, value, table)
    coefs[...] = table
    upstream = c3 * grad
    upstream_out[...] = upstream
    send_grads(upstream, rows, gates[...], slot_row[...], slot_col[...], grad_z, gate_grads, sends)


def turn(mixed, state, gates, slot_col, slot_row, returned, first_state, halt, depth, cotangent):
    outs = [
        like((TOK, WIDTH), F32),
        like((TOK, LANES), F32),
        like((WIDTH, LANES), F32),
        like((TOK, WIDTH), F32),
    ] + SEND_OUTS
    args = [mixed, state, gates, slot_col, slot_row, *returned, first_state, halt, depth, cotangent]
    return call("turn", turn_kernel, outs, args, near=range(5, 9), near_out=range(6, 10))


def moe_back_kernel(*refs):
    returned, slot_col, gates, gate_grads = refs[0:4], refs[4], refs[5], refs[6]
    normed, router, mixed, gain, grad_z, tiny = refs[7:13]
    grad_mixed, grad_low, tiny_out = refs[13:]
    full = jnp.concatenate([b[...] for b in returned], 0)
    slots = iota((TOK, 2 * ROWS), 1)
    hit = (slot_col[:, 0:1] == slots) | (slot_col[:, 1:2] == slots)
    grad_normed = nn(onehot(hit), full)
    weights, grads = gates[...], gate_grads[...]
    inner = row_sum(weights * grads)
    lanes = iota((TOK, LANES), 1)
    grad_logits = jnp.zeros((TOK, LANES), F32)
    for k in range(2):
        value = weights[:, k : k + 1] * (grads[:, k : k + 1] - inner)
        grad_logits = grad_logits + jnp.where(lanes == slot_col[:, 2 + k : 3 + k], value, 0.0)
    low = grad_logits.astype(BF16)
    grad_normed = grad_normed + nn(low, router[...])
    out, gain_part = norm_back(grad_normed, mixed[...], gain[...])
    out = out + grad_z[...]
    turned = jnp.concatenate([low[:, LANES - 16 :], low[:, : LANES - 16]], 1)
    tiny_out[...] = tiny[...] + tn(normed[...], turned) + lane_of(gain_part, 24)
    grad_mixed[...] = out
    grad_low[...] = out.astype(BF16)


def moe_back(returned, slot_col, gates, gate_grads, normed, router, mixed, gain, grad_z, tiny):
    outs = [
        like((TOK, WIDTH), F32),
        like((TOK, WIDTH), BF16),
        like((WIDTH, LANES), F32),
    ]
    args = [*returned, slot_col, gates, gate_grads, normed, router, mixed, gain, grad_z, tiny]
    return call("moe_back", moe_back_kernel, outs, args, near=range(4), near_out=(1,))


def retreat_kernel(step, *refs):
    parts = refs[0:4]
    state, gain, slot_col, upstream, grad_mixed = refs[4:9]
    rest = refs[9:]
    total = sum(p[...].astype(F32) for p in parts)
    out, _ = norm_back(total, state[...], gain[...])
    kept = jnp.where(slot_col[:, 0:1] >= 0, 0.0, upstream[...])
    carry = kept + grad_mixed[...] + out
    if step == 0:
        rest[0][...] = carry
        return
    cotangent, halt, coefs, gates, before_col, before_row = rest[0:6]
    returned = rest[6:10]
    upstream_out, grad_z, gate_grads_out = rest[10:13]
    sends = rest[13:17]
    table = coefs[...]
    carry = carry + column(table, step - 1) * cotangent[...].astype(F32)
    carry = carry + column(table, step + 2) * halt[...]
    upstream_out[...] = carry
    rows = picked_rows(before_col[...], returned)
    send_grads(
        carry, rows, gates[...], before_row[...], before_col[...], grad_z, gate_grads_out, sends
    )


def retreat(step, parts, args, extra):
    outs = [like((TOK, WIDTH), F32)] + (SEND_OUTS if step else [])
    return call(
        "retreat", functools.partial(retreat_kernel, step), outs, [*parts, *args, *extra],
        near=range(4), near_out=range(3, 7),
    )


def swap_core(rows):
    return lax.ppermute(rows, "expert", [(i, i ^ 1) for i in range(2 * CHIPS)])


def shift_chip(rows, hops):
    count = 2 * CHIPS
    return lax.ppermute(rows, "expert", [(i, (i + 2 * hops) % count) for i in range(count)])


def send_blocks(blocks):
    return [blocks[0]] + [shift_chip(blocks[d], d) for d in (1, 2, 3)]


def after(value, other):
    return lax.optimization_barrier((value, other))


def return_blocks(blocks):
    return [blocks[0]] + [shift_chip(blocks[d], CHIPS - d) for d in (1, 2, 3)]


def spread_rows(rows):
    return [rows] + [shift_chip(rows, d) for d in (1, 2, 3)]


def dp_move(blocks):
    return lax.all_to_all(blocks, "dp", split_axis=0, concat_axis=0, tiled=True)


def block_sum(blocks):
    return jnp.sum(blocks.astype(F32), 0)


def local(
    block_input,
    gain_one,
    gain_two,
    moa_router,
    key_proj,
    value_proj,
    query_proj,
    out_proj,
    moe_router,
    ffn_in,
    ffn_out,
    halt_weight,
    depths,
    moa_choice,
    moe_choice,
    cotangent,
):
    member = lax.axis_index("expert")
    spot = lax.axis_index("dp")
    place = jnp.stack([member // 2, member % 2, spot // 4, spot % 4]).astype(I32)
    gain_a, gain_b = gain_one[None, :], gain_two[None, :]
    halt = halt_weight[None, :]
    router_a = jnp.pad(moa_router.T, ((0, LANES - 8), (0, 0)))
    router_b = jnp.pad(moe_router.T, ((0, LANES - 8), (0, 0)))
    depth = depths[None, :]
    moa_rows, moe_rows = moa_choice.swapaxes(1, 2), moe_choice.swapaxes(1, 2)

    state, normed, payload = first_norm(block_input, gain_a, depth)
    same = spread_rows(payload)
    same[1], place_late = after(same[1], place)
    plan = attend_plan((0,), place_late, moa_rows, ())
    same[2], plan[0]["table"] = after(same[2], plan[0]["table"])
    query_w = [query_proj[0], swap_core(query_proj[0])]
    out_w = [out_proj[0], swap_core(out_proj[0])]
    other = [swap_core(rows) for rows in same]
    slot_cols = slot_rows = None
    win = wout = None

    kept = []
    states = [state]
    for s in range(3):
        if s:
            same = spread_rows(normed)
            other = [swap_core(rows) for rows in same]
        p = plan[s]
        res = attend(
            p["table"], same, other, key_proj, value_proj, query_w, out_w, router_a, p,
            60,
        )
        parts = send_blocks(res[:4])
        if s == 0:
            parts[1], place_late = after(parts[1], place)
            slot_cols, slot_rows = slot_plan(place_late, moe_rows, depth)
            parts[2], slot_cols[0] = after(parts[2], slot_cols[0])
            win = [ffn_in[0], swap_core(ffn_in[0])]
            wout = [ffn_out[0], swap_core(ffn_out[0])]
            tails = (*same, *other)
        mixed, normed_b, gates, *sends = dispatch(
            state, parts, gain_b, router_b, slot_rows[s], slot_cols[s]
        )
        *sends, mine, others = feed(send_blocks(sends), win, wout)
        returned = return_blocks(sends)
        if s < 2:
            returned[1], place_late = after(returned[1], place)
            plan = plan + attend_plan((s + 1,), place_late, moa_rows, tails)
            returned[2], plan[s + 1]["table"] = after(returned[2], plan[s + 1]["table"])
        *saved, spread_0, spread_1, lse, weights = res[4:]
        kept.append(
            dict(
                normed=normed, rows=saved[0], mixed=mixed, normed_b=normed_b, gates=gates,
                attend=(*saved[1:], spread_0, spread_1, lse, weights),
                mixes=(spread_0, swap_core(spread_1)),
                received=(mine, others), returned=returned, state=state,
                received_all=(mine, swap_core(others)),
            )
        )
        if s < 2:
            state, normed = advance(mixed, state, gates, slot_cols[s], returned, gain_a)
            states.append(state)

    output, coefs, tiny, upstream, grad_z, gate_grads, *sends = turn(
        mixed, state, gates, slot_cols[2], slot_rows[2], returned, states[1], halt, depth, cotangent
    )
    expert_acc = shared_acc = pending = None
    received, acts, grad_pres, grad_rows = [], [], [], []
    for s in (2, 1, 0):
        k, p = kept[s], plan[s]
        table = p["table"]
        *sends, rows_0, rows_1, act_0, act_1, pre_0, pre_1 = feed_back(
            send_blocks(sends), k["received"], win, wout
        )
        back = return_blocks(sends)
        if pending and s:
            back[1], grad_k = after(back[1], pending[1])
            shared_acc = shared_weights(pending[0], grad_k, pending[2], shared_acc)
            back[2], shared_acc = after(back[2], shared_acc)
        received += k["received_all"]
        acts += [act_0, swap_core(act_1)]
        grad_pres += [pre_0, swap_core(pre_1)]
        grad_rows += [rows_0, swap_core(rows_1)]
        if s == 0:
            feed_grads = feed_weights(received, grad_rows, acts, grad_pres)
            back[2], feed_grads = after(back[2], feed_grads)
            feed_grads = dp_move(feed_grads)
        grad_mixed, grad_low, tiny = moe_back(
            back, slot_cols[s], k["gates"], gate_grads, k["normed_b"], router_b, k["mixed"],
            gain_b, grad_z, tiny,
        )
        limit = 20 if s else 60
        arrived = spread_rows(grad_low)
        if s == 0:
            arrived[1], grad_k = after(arrived[1], pending[1])
            shared_acc = shared_weights(pending[0], grad_k, pending[2], shared_acc, 60)
            arrived[2], shared_acc = after(arrived[2], shared_acc)
        *same, other, y_0, y_1, q_0, q_1, grad_k, grad_v, tiny = attend_back(
            table, arrived, k["attend"], key_proj, value_proj, query_w, out_w, p,
            (k["rows"], router_a, gain_a, tiny), 36 if s else 60,
        )
        other = swap_core(other)
        if s:
            parts = send_blocks(pair_sum(same, other, limit))
            parts[1], q_0 = after(parts[1], q_0)
        if s:
            expert_acc = expert_weights(
                table, k["rows"], k["mixes"], (y_0, swap_core(y_1)), (q_0, swap_core(q_1)),
                expert_acc, False, 20,
            )
            parts[2], expert_acc = after(parts[2], expert_acc)
            pending = (k["rows"], grad_k, grad_v)
        else:
            mine, others = shared_last(table, k["rows"], grad_k, grad_v, shared_acc, tiny)
            shared = send_blocks(core_sum(mine, swap_core(others)))
            parts = send_blocks(pair_sum(same, other, limit))
            weights_last = last_weights(
                table, k["rows"], k["mixes"], (y_0, swap_core(y_1)), (q_0, swap_core(q_1)),
                expert_acc, shared,
            )
            weights_last, feed_grads, *parts = lax.optimization_barrier(
                (weights_last, feed_grads, *parts)
            )
            moved = dp_move(weights_last)
        args = (k["state"], gain_a, slot_cols[s], upstream, grad_mixed)
        if s:
            b = kept[s - 1]
            extra = (
                cotangent, halt, coefs, b["gates"], slot_cols[s - 1], slot_rows[s - 1],
                *b["returned"],
            )
            upstream, grad_z, gate_grads, *sends = retreat(s, parts, args, extra)
        else:
            (grad_input,) = retreat(s, parts, args, ())

    summed = block_sum(moved)
    tiny = summed[72:76]
    feed_grads = block_sum(feed_grads)
    grad_in = feed_grads[:TOK].reshape(4, 32, PART).swapaxes(0, 1).reshape(32, FFN)
    grad_out = feed_grads[TOK:]
    return (
        output,
        grad_input,
        tiny[:, 8],
        tiny[:, 24],
        tiny[:, :8],
        summed[64:68],
        summed[68:72],
        summed[0:32][None],
        summed[32:64][None],
        tiny[:, 16:24],
        grad_in[None],
        grad_out[None],
        tiny[:, 25],
    )


def solution(mesh):
    in_specs = (
        P(("dp", "expert"), None),
        P(),
        P(),
        P(),
        P(),
        P(),
        P("expert", None, None),
        P("expert", None, None),
        P(),
        P("expert", None, None),
        P("expert", None, None),
        P(),
        P(("dp", "expert")),
        P(None, "dp", None),
        P(None, ("dp", "expert"), None),
        P(("dp", "expert"), None),
    )
    out_specs = (
        P(("dp", "expert"), None),
        P(("dp", "expert"), None),
        P(("dp", "expert")),
        P(("dp", "expert")),
        P(("dp", "expert"), None),
        P(("dp", "expert"), None),
        P(("dp", "expert"), None),
        P("expert", "dp", None),
        P("expert", "dp", None),
        P(("dp", "expert"), None),
        P("expert", "dp", None),
        P("expert", "dp", None),
        P(("dp", "expert")),
    )
    return jax.shard_map(local, mesh=mesh, in_specs=in_specs, out_specs=out_specs, check_vma=False)
```

```python
import functools

import jax
import jax.numpy as jnp
from jax import lax
from jax.experimental import pallas as pl
from jax.experimental.pallas import tpu as pltpu
from jax.sharding import PartitionSpec as P

F32 = jnp.float32
BF16 = jnp.bfloat16
I32 = jnp.int32

WIDTH = 512
SEQ = 1024
TOK = 128
HALF = 512
CHIPS = 4
PAIRS = 4
SLOTS = 40
SPAN = 256
FFN = 2048
UNROLL = 4
PART = 512
LANES = 128


def nn(a, b):
    return lax.dot_general(a, b, (((1,), (0,)), ((), ())), preferred_element_type=F32)


def nt(a, b):
    return lax.dot_general(a, b, (((1,), (1,)), ((), ())), preferred_element_type=F32)


def tn(a, b):
    return lax.dot_general(a, b, (((0,), (0,)), ((), ())), preferred_element_type=F32)


def iota(shape, dim):
    return lax.broadcasted_iota(I32, shape, dim)


def onehot(mask):
    return jnp.where(mask, 1.0, 0.0).astype(BF16)


def row_sum(x):
    return jnp.sum(x, -1, keepdims=True)


def norm_parts(x):
    centred = x - jnp.mean(x, -1, keepdims=True)
    rstd = lax.rsqrt(jnp.mean(centred * centred, -1, keepdims=True) + 1e-05)
    return centred * rstd, rstd


def norm_back(grad, x, gain):
    hat, rstd = norm_parts(x)
    inner = grad * gain
    out = rstd * (
        inner
        - jnp.mean(inner, -1, keepdims=True)
        - hat * jnp.mean(inner * hat, -1, keepdims=True)
    )
    return out, jnp.sum(grad * hat, 0, keepdims=True)


def column(table, index):
    return row_sum(jnp.where(iota(table.shape, 1) == index, table, 0.0))


def masked_softmax(logits, chosen):
    peak = jnp.max(jnp.where(chosen, logits, -jnp.inf), -1, keepdims=True)
    weights = jnp.where(chosen, jnp.exp(logits - peak), 0.0)
    return weights / row_sum(weights)


def named(choice, count):
    lanes = iota((choice.shape[0], LANES), 1)
    mask = lanes == choice[:, 0:1]
    for k in range(1, count):
        mask = mask | (lanes == choice[:, k : k + 1])
    return mask


def lane_of(row, lane):
    return jnp.where(iota((LANES, WIDTH), 0) == lane, row, 0.0).T


def turned_row(row):
    wide = jnp.concatenate([row.astype(F32), jnp.zeros((7, TOK), F32)], 0)
    return wide.T[:, 0:1].astype(I32)


def rows_at(block):
    return pl.ds(pl.multiple_of(block * TOK, TOK), TOK)


def split_heads(pair):
    lanes = iota((1, LANES), 1)
    low = jnp.where(lanes < 64, 1.0, 0.0).astype(BF16)
    high = jnp.where(lanes < 64, 0.0, 1.0).astype(BF16)
    return jnp.concatenate([pair * low, pair * high], 0)


def join_heads(both, rows):
    return jnp.where(iota((rows, LANES), 1) < 64, both[:rows], both[rows:])


def call(name, kernel, outs, args, scratch=(), smem=(), near=(), near_out=(), raw=(), flops=0, vmem=20):
    far = [i for i in range(len(args)) if i not in smem and i not in near and i not in raw]
    far_out = [i for i in range(len(outs)) if i not in near_out]
    count, total = len(args), len(args) + len(outs)

    def body(*refs):
        held = refs[total : total + len(far) + len(far_out)]
        in_sems, out_sems = refs[-2:]
        given, results = list(refs[:count]), list(refs[count:total])
        moving = []
        for n, i in enumerate(far):
            moving.append(pltpu.make_async_copy(given[i], held[n], in_sems.at[n]))
            moving[-1].start()
            given[i] = held[n]
        for n, i in enumerate(far_out):
            results[i] = held[len(far) + n]
        for copy in moving:
            copy.wait()
        kernel(*given, *results, *refs[total + len(far) + len(far_out) : -2])
        leaving = []
        for n, i in enumerate(far_out):
            leaving.append(pltpu.make_async_copy(results[i], refs[count + i], out_sems.at[n]))
            leaving[-1].start()
        for copy in leaving:
            copy.wait()

    def spec(i, places, nearby):
        if i in places:
            return pl.BlockSpec(memory_space=pltpu.SMEM)
        return pl.BlockSpec(memory_space=pltpu.VMEM if i in nearby else pltpu.HBM)

    moved = sum(a.size * a.dtype.itemsize for a in args) + sum(
        o.size * o.dtype.itemsize for o in outs
    )
    return pl.pallas_call(
        body,
        out_shape=tuple(outs),
        in_specs=[spec(i, smem, near) for i in range(count)],
        out_specs=tuple(spec(i, (), near_out) for i in range(len(outs))),
        scratch_shapes=[pltpu.VMEM(args[i].shape, args[i].dtype) for i in far]
        + [pltpu.VMEM(outs[i].shape, outs[i].dtype) for i in far_out]
        + list(scratch)
        + [pltpu.SemaphoreType.DMA((max(1, len(far)),)), pltpu.SemaphoreType.DMA((max(1, len(far_out)),))],
        compiler_params=pltpu.CompilerParams(vmem_limit_bytes=vmem * 2**20),
        cost_estimate=pl.CostEstimate(flops=flops, bytes_accessed=moved, transcendentals=0),
        name=name,
    )(*args)


def like(shape, dtype):
    return jax.ShapeDtypeStruct(shape, dtype)


ANY = pl.BlockSpec(memory_space=pl.ANY)
FAR = pl.BlockSpec(memory_space=pltpu.HBM)


def copy_in(src, dst, sem):
    moving = pltpu.make_async_copy(src, dst, sem)
    moving.start()
    return moving


def call_any(name, kernel, outs, args, scratch, flops, vmem, near, near_out):
    moved = sum(a.size * a.dtype.itemsize for a in args) + sum(
        o.size * o.dtype.itemsize for o in outs
    )
    return pl.pallas_call(
        kernel,
        out_shape=tuple(outs),
        in_specs=[pl.BlockSpec(memory_space=pltpu.SMEM)]
        + [ANY if i in near else FAR for i in range(1, len(args))],
        out_specs=tuple(ANY if i in near_out else FAR for i in range(len(outs))),
        scratch_shapes=list(scratch),
        compiler_params=pltpu.CompilerParams(vmem_limit_bytes=vmem * 2**20),
        cost_estimate=pl.CostEstimate(flops=flops, bytes_accessed=moved, transcendentals=0),
        name=name,
    )(*args)


def allowed_keys(key_pos, span, start, rows):
    number = lax.rem(iota((span, 2 * rows), 1), rows) + start
    column_pos = key_pos[0:span, :]
    if rows == TOK:
        column_pos = jnp.concatenate([column_pos, column_pos], 1)
    return column_pos <= number


def packed_rows(start, rows):
    return pl.ds(pl.multiple_of(start, TOK), rows)


def attend_level(rows, span, start, keys, value_x, key_row, q_held, o_held, logs):
    here = packed_rows(start, rows)

    @pl.loop(0, PAIRS, unroll=UNROLL)
    def _(i):
        pair = pl.ds(pl.multiple_of(i * LANES, LANES), LANES)
        part = nt(split_heads(q_held[here, pair]), keys[0:span, pair])
        number = lax.rem(iota((2 * rows, span), 0), rows) + start
        part = jnp.where(key_row[0:1, 0:span] <= number, part, -jnp.inf)
        top = jnp.max(part, -1, keepdims=True)
        mixed = nn(jnp.exp(part - top).astype(BF16), value_x[i, 0:span, :])
        total = mixed[:, LANES : 2 * LANES]
        o_held[here, pair] = join_heads(mixed[:, 0:LANES] / total, rows).astype(BF16)
        lanes = iota((2 * rows, LANES), 1)
        logs[0 : 2 * rows, :] = jnp.where(
            lanes == i, top + jnp.log(total), logs[0 : 2 * rows, :]
        )

    if rows < TOK:
        rest = pl.ds(pl.multiple_of(start + rows, rows), TOK - rows)
        o_held[rest, :] = jnp.zeros((TOK - rows, WIDTH), BF16)


SMALL = 5
LEVELS = [(TOK, level * SPAN, level) for level in range(1, 5)] + [(TOK // 2, SEQ, SMALL)]


def attend_kernel(*refs):
    scal = refs[0]
    same, other = refs[1:5], refs[5:9]
    sources = refs[9:19]
    outs = refs[20:24]
    rows_out, keys_out, values_out, q_out, o_out, spread_0, spread_1, lse_out, gates_out = refs[24:33]
    rows, own, keys, values, value_t = refs[33:38]
    held = refs[38:48]
    key_w, value_w, query_0, query_1, out_0, out_1, router, chosen, pos_row, pos_col = held[:10]
    key_pos = refs[48]
    queries, q_held, o_held, spread, o_spread, staged, lse, gates = refs[49:57]
    key_row, logs = refs[57:59]
    in_sems, row_sems, out_sems, block_sems = refs[59:63]
    query_w, out_w = (query_0, query_1), (out_0, out_1)
    blocks, chip, core = scal[0, 8], scal[0, 9], scal[0, 10]

    row_copies = []
    for hop in range(CHIPS):
        source = lax.rem(chip - hop + CHIPS, CHIPS)
        row_copies.append(
            copy_in(same[hop].at[0:TOK], rows.at[rows_at(source * 2 + core)], row_sems.at[2 * hop])
        )
        row_copies.append(
            copy_in(
                other[hop].at[0:TOK], rows.at[rows_at(source * 2 + 1 - core)], row_sems.at[2 * hop + 1]
            )
        )
    order = (0, 1, 2, 3, 6, 7, 8, 9, 4, 5)
    copies = {i: copy_in(sources[i], held[i], in_sems.at[i]) for i in order}
    key_copy = copy_in(refs[19], key_pos, in_sems.at[10])
    for moving in row_copies:
        moving.wait()
    rows_copy = copy_in(rows, rows_out, out_sems.at[0])
    for source in range(CHIPS):
        own[source * TOK : (source + 1) * TOK, :] = rows[rows_at(2 * source + core), :]
    copies[0].wait()
    copies[1].wait()

    @pl.loop(0, 4)
    def _(tile):
        at = pl.ds(pl.multiple_of(tile * 256, 256), 256)
        block = rows[at, :]
        keys[at, :] = nn(block, key_w[...]).astype(BF16)
        low = nn(block, value_w[...]).astype(BF16)
        values[at, :] = low
        for i in range(PAIRS):
            value_t[i, at, 0:LANES] = low[:, i * LANES : (i + 1) * LANES]
            value_t[i, at, LANES : 2 * LANES] = jnp.ones((256, LANES), BF16)

    keys_copy = copy_in(keys, keys_out, out_sems.at[1])
    values_copy = copy_in(values, values_out, out_sems.at[2])
    mine = own[...]
    for r in range(2):
        copies[2 + r].wait()
        full = nn(mine, query_w[r][...]).astype(BF16)
        queries[r] = full * jnp.asarray(0.125, BF16)
    copies[6].wait()
    copies[7].wait()
    weights = masked_softmax(nt(mine, router[...]), chosen[...] > 0.0)
    gates[...] = weights
    gates_copy = copy_in(gates, gates_out, out_sems.at[3])
    spread[...] = jnp.zeros_like(spread)
    copies[8].wait()
    copies[9].wait()
    key_copy.wait()
    for part in range(8):
        at = slice(part * TOK, (part + 1) * TOK)
        key_row[:, at] = key_pos[at, :].astype(F32).T[:8].astype(I32)

    @pl.loop(0, blocks)
    def _(j):
        start = j * TOK
        here = pl.ds(pl.multiple_of(start, TOK), TOK)
        take = iota((TOK, HALF), 0) + start
        packed = sum(
            nn(onehot(pos_row[r : r + 1, :] == take), queries[r]) for r in range(2)
        ).astype(BF16)
        q_held[here, :] = packed
        copy_in(q_held.at[here], q_out.at[here], block_sems.at[0, j])
        for rows_now, span, level in LEVELS:
            pl.when(scal[0, j] == level)(
                functools.partial(
                    attend_level, rows_now, span, start, keys, value_t, key_row, q_held, o_held, logs
                )
            )
        lse[j] = logs[...].T[:8]
        copy_in(o_held.at[here], o_out.at[here], block_sems.at[1, j])
        block = o_held[here, :]
        put = iota((HALF, TOK), 1) + start
        for r in range(2):
            spread[r] += nn(onehot(pos_col[:, r : r + 1] == put), block)

    lse_copy = copy_in(lse, lse_out, out_sems.at[4])
    copies[4].wait()
    copies[5].wait()
    mixture = jnp.zeros((HALF, WIDTH), F32)
    for r in range(2):
        full = spread[r].astype(BF16)
        o_spread[r] = full
        expert = 2 * chip + (core if r == 0 else 1 - core)
        mixture = mixture + column(gates[...], expert) * nn(full, out_w[r][...])
    staged[...] = mixture.astype(BF16)
    final = [
        copy_in(staged.at[rows_at(lax.rem(chip + hop, CHIPS))], outs[hop], row_sems.at[hop])
        for hop in range(CHIPS)
    ]
    final.append(copy_in(o_spread.at[0], spread_0, out_sems.at[5]))
    final.append(copy_in(o_spread.at[1], spread_1, out_sems.at[6]))

    @pl.loop(0, blocks)
    def _(j):
        here = rows_at(j)
        pltpu.make_async_copy(q_held.at[here], q_out.at[here], block_sems.at[0, j]).wait()
        pltpu.make_async_copy(o_held.at[here], o_out.at[here], block_sems.at[1, j]).wait()

    for moving in [rows_copy, keys_copy, values_copy, gates_copy, lse_copy, *final]:
        moving.wait()


def attend(table, same, other, key_w, value_w, query_w, out_w, router, plan, vmem):
    outs = [like((TOK, WIDTH), BF16)] * 4 + [
        like((SEQ, WIDTH), BF16),
        like((SEQ, WIDTH), BF16),
        like((SEQ, WIDTH), BF16),
        like((SEQ, WIDTH), BF16),
        like((SEQ, WIDTH), BF16),
        like((HALF, WIDTH), BF16),
        like((HALF, WIDTH), BF16),
        like((8, 8, 2 * TOK), F32),
        like((HALF, LANES), F32),
    ]
    square = pltpu.VMEM((WIDTH, WIDTH), BF16)
    scratch = [
        pltpu.VMEM((SEQ, WIDTH), BF16),
        pltpu.VMEM((HALF, WIDTH), BF16),
        pltpu.VMEM((SEQ, WIDTH), BF16),
        pltpu.VMEM((SEQ, WIDTH), BF16),
        pltpu.VMEM((PAIRS, SEQ, 2 * LANES), BF16),
        square,
        square,
        square,
        square,
        square,
        square,
        pltpu.VMEM((LANES, WIDTH), BF16),
        pltpu.VMEM((HALF, LANES), F32),
        pltpu.VMEM((8, HALF), I32),
        pltpu.VMEM((HALF, LANES), I32),
        pltpu.VMEM((SEQ, LANES), I32),
        pltpu.VMEM((2, HALF, WIDTH), BF16),
        pltpu.VMEM((SEQ, WIDTH), BF16),
        pltpu.VMEM((SEQ, WIDTH), BF16),
        pltpu.VMEM((2, HALF, WIDTH), F32),
        pltpu.VMEM((2, HALF, WIDTH), BF16),
        pltpu.VMEM((HALF, WIDTH), BF16),
        pltpu.VMEM((8, 8, 2 * TOK), F32),
        pltpu.VMEM((HALF, LANES), F32),
        pltpu.VMEM((8, SEQ), I32),
        pltpu.VMEM((2 * TOK, LANES), F32),
        pltpu.SemaphoreType.DMA((11,)),
        pltpu.SemaphoreType.DMA((8,)),
        pltpu.SemaphoreType.DMA((7,)),
        pltpu.SemaphoreType.DMA((2, 8)),
    ]
    args = [
        table, *same, *other, key_w, value_w, *query_w, *out_w, router,
        plan["chosen"], plan["pos_row"], plan["pos_col"], plan["key_pos"],
    ]
    return call_any("attend", attend_kernel, outs, args, scratch, 6 * 10**9, vmem, range(1, 9), range(4))


def back_level(
    rows, span, start, keys, values, key_pos, q_held, o_held, packed, logs, inner,
    sum_k, sum_v, part_q, block,
):
    here = packed_rows(start, rows)
    lanes = iota((2 * rows, LANES), 1)
    inners = jnp.zeros((2 * rows, LANES), F32)
    for i in range(PAIRS):
        at = slice(i * LANES, (i + 1) * LANES)
        held = o_held[here, at].astype(F32)
        grads = split_heads(packed[0:rows, at]).astype(F32)
        inners = jnp.where(lanes == i, row_sum(grads * jnp.concatenate([held, held], 0)), inners)
    inner[:, 0 : 2 * rows] = inners.T[:8]

    @pl.loop(0, PAIRS, unroll=UNROLL)
    def _(i):
        pair = pl.ds(pl.multiple_of(i * LANES, LANES), LANES)
        key_block = keys[0:span, pair]
        queries, grads = split_heads(q_held[here, pair]), split_heads(packed[0:rows, pair])
        probs = jnp.exp(nt(key_block, queries) - logs[pl.ds(i, 1), 0 : 2 * rows])
        probs = jnp.where(allowed_keys(key_pos, span, start, rows), probs, 0.0)
        grad_probs = nt(values[0:span, pair], grads)
        grad_scores = (probs * (grad_probs - inner[pl.ds(i, 1), 0 : 2 * rows])).astype(BF16)
        sum_k[0:span, pair] += nn(grad_scores, queries)
        sum_v[0:span, pair] += nn(probs.astype(BF16), grads)
        part_q[i, 0 : 2 * rows] = tn(grad_scores, key_block)

    for i in range(PAIRS):
        at = slice(i * LANES, (i + 1) * LANES)
        block[0:rows, at] = (join_heads(part_q[i, 0 : 2 * rows], rows) * 0.125).astype(BF16)
    if rows < TOK:
        block[rows:TOK, :] = jnp.zeros((TOK - rows, WIDTH), BF16)


def attend_back_kernel(*refs):
    scal = refs[0]
    arrived = refs[1:5]
    sources = refs[5:26]
    same, other = refs[26:30], refs[30]
    y_out, q_out, k_out, v_out, tiny_out = refs[31:33], refs[33:35], refs[35], refs[36], refs[37]
    upstream = refs[38]
    held = refs[39:60]
    (
        out_0, out_1, gates, spread_0, spread_1, pos_row, q_held, o_held, lse, keys, values,
        key_pos, pos_col, query_0, query_1, key_w, value_w, rows, router, gain, tiny,
    ) = held
    grad_o, sum_k, sum_v, sum_q, part_q, packed_s, block_q, logs, inner, own, gate_low = refs[60:71]
    grad_y, grad_q, grad_k, grad_v, same_s, other_s = refs[71:77]
    in_sems, row_sems, out_sems = refs[77:80]
    o_spread = (spread_0, spread_1)
    query_w, out_w = (query_0, query_1), (out_0, out_1)
    blocks, chip, core = scal[0, 8], scal[0, 9], scal[0, 10]

    row_copies = [
        copy_in(
            arrived[hop],
            upstream.at[rows_at(lax.rem(chip - hop + CHIPS, CHIPS))],
            row_sems.at[hop],
        )
        for hop in range(CHIPS)
    ]
    copies = [copy_in(sources[i], held[i], in_sems.at[i]) for i in range(21)]
    sum_k[...] = jnp.zeros_like(sum_k)
    sum_v[...] = jnp.zeros_like(sum_v)
    sum_q[...] = jnp.zeros_like(sum_q)
    for moving in row_copies + copies[0:5]:
        moving.wait()
    lanes = iota((HALF, LANES), 1)
    gate_grads = jnp.zeros((HALF, LANES), F32)
    for r in range(2):
        expert = 2 * chip + (core if r == 0 else 1 - core)
        gate = column(gates[...], expert)
        raw = nt(upstream[...], out_w[r][...])
        gate_grads = jnp.where(
            lanes == expert, row_sum(o_spread[r][...].astype(F32) * raw), gate_grads
        )
        grad_o[r] = (gate * raw).astype(BF16)
        grad_y[r] = (gate * upstream[...].astype(F32)).astype(BF16)
    y_copies = [copy_in(grad_y.at[r], y_out[r], out_sems.at[r]) for r in range(2)]
    weights = gates[...]
    gate_low[...] = (weights * (gate_grads - row_sum(weights * gate_grads))).astype(BF16)
    for moving in copies[5:13]:
        moving.wait()

    @pl.loop(0, blocks)
    def _(j):
        start = j * TOK
        here = pl.ds(pl.multiple_of(start, TOK), TOK)
        take = iota((TOK, HALF), 0) + start
        packed = sum(
            nn(onehot(pos_row[r : r + 1, :] == take), grad_o[r]) for r in range(2)
        ).astype(BF16)
        packed_s[...] = packed
        logs[...] = lse[j]
        for rows_now, span, level in LEVELS:
            pl.when(scal[0, j] == level)(
                functools.partial(
                    back_level, rows_now, span, start, keys, values, key_pos, q_held, o_held,
                    packed_s, logs, inner, sum_k, sum_v, part_q, block_q,
                )
            )

        block = block_q[...]
        put = iota((HALF, TOK), 1) + start
        for r in range(2):
            sum_q[r] += nn(onehot(pos_col[:, r : r + 1] == put), block)

    for r in range(2):
        grad_q[r] = sum_q[r].astype(BF16)
    q_copies = [copy_in(grad_q.at[r], q_out[r], out_sems.at[2 + r]) for r in range(2)]
    for moving in copies[13:21]:
        moving.wait()
    for source in range(CHIPS):
        own[source * TOK : (source + 1) * TOK, :] = rows[rows_at(2 * source + core), :]
    sum_q[0] = (
        nt(grad_q[0], query_w[0][...])
        + nt(grad_q[1], query_w[1][...])
        + nn(gate_low[...], router[...])
    )
    gain_part = jnp.sum(sum_q[0] * own[...].astype(F32), 0, keepdims=True)
    sum_q[1, 0:1, :] = gain_part

    @pl.loop(0, 4)
    def _(tile):
        at = pl.ds(pl.multiple_of(tile * 256, 256), 256)
        low_k, low_v = sum_k[at, :].astype(BF16), sum_v[at, :].astype(BF16)
        grad_k[at, :] = low_k
        grad_v[at, :] = low_v
        total = nt(low_k, key_w[...]) + nt(low_v, value_w[...])
        sum_k[at, :] = total
        sum_q[1, 0:1, :] += jnp.sum(total * rows[at, :].astype(F32), 0, keepdims=True)

    k_copy = copy_in(grad_k, k_out, out_sems.at[4])
    v_copy = copy_in(grad_v, v_out, out_sems.at[5])
    final = []
    for hop in range(CHIPS):
        target = lax.rem(chip + hop, CHIPS)
        other_s[hop] = sum_k[rows_at(target * 2 + 1 - core), :].astype(BF16)
    final.append(copy_in(other_s, other, out_sems.at[6]))
    for hop in range(CHIPS):
        target = lax.rem(chip + hop, CHIPS)
        same_s[hop] = (
            sum_k[rows_at(target * 2 + core), :] + sum_q[0, rows_at(target), :]
        ).astype(BF16)
        final.append(copy_in(same_s.at[hop], same[hop], row_sems.at[hop]))
    tiny[...] += tn(own[...], gate_low[...]) + lane_of(sum_q[1, 0:1, :] / gain[...], 8)
    final.append(copy_in(tiny, tiny_out, out_sems.at[7]))
    for moving in [*y_copies, *q_copies, k_copy, v_copy, *final]:
        moving.wait()


def attend_back(table, arrived, held, key_w, value_w, query_w, out_w, plan, rest, vmem):
    outs = [like((TOK, WIDTH), BF16)] * 4 + [
        like((CHIPS, TOK, WIDTH), BF16),
        like((HALF, WIDTH), BF16),
        like((HALF, WIDTH), BF16),
        like((HALF, WIDTH), BF16),
        like((HALF, WIDTH), BF16),
        like((SEQ, WIDTH), BF16),
        like((SEQ, WIDTH), BF16),
        like((WIDTH, LANES), F32),
    ]
    keys, values, q_held, o_held, spread_0, spread_1, lse, gates = held
    sources = [
        *out_w, gates, spread_0, spread_1, plan["pos_row"], q_held, o_held, lse, keys, values,
        plan["key_pos"], plan["pos_col"], *query_w, key_w, value_w, *rest,
    ]
    scratch = [pltpu.VMEM((HALF, WIDTH), BF16)]
    scratch += [pltpu.VMEM(a.shape, a.dtype) for a in sources]
    scratch += [
        pltpu.VMEM((2, HALF, WIDTH), BF16),
        pltpu.VMEM((SEQ, WIDTH), F32),
        pltpu.VMEM((SEQ, WIDTH), F32),
        pltpu.VMEM((2, HALF, WIDTH), F32),
        pltpu.VMEM((PAIRS, 2 * TOK, LANES), F32),
        pltpu.VMEM((TOK, WIDTH), BF16),
        pltpu.VMEM((TOK, WIDTH), BF16),
        pltpu.VMEM((8, 2 * TOK), F32),
        pltpu.VMEM((8, 2 * TOK), F32),
        pltpu.VMEM((HALF, WIDTH), BF16),
        pltpu.VMEM((HALF, LANES), BF16),
        pltpu.VMEM((2, HALF, WIDTH), BF16),
        pltpu.VMEM((2, HALF, WIDTH), BF16),
        pltpu.VMEM((SEQ, WIDTH), BF16),
        pltpu.VMEM((SEQ, WIDTH), BF16),
        pltpu.VMEM((CHIPS, TOK, WIDTH), BF16),
        pltpu.VMEM((CHIPS, TOK, WIDTH), BF16),
        pltpu.SemaphoreType.DMA((21,)),
        pltpu.SemaphoreType.DMA((4,)),
        pltpu.SemaphoreType.DMA((8,)),
    ]
    args = [table, *arrived, *sources]
    return call_any("attend_back", attend_back_kernel, outs, args, scratch, 10**11, vmem, range(1, 5), range(5))


def pair_sum_kernel(*refs):
    other, outs = refs[4], refs[5:]
    for hop in range(CHIPS):
        outs[hop][...] = (refs[hop][...].astype(F32) + other[hop].astype(F32)).astype(BF16)


def pair_sum(same, other, vmem):
    return call("pair_sum", pair_sum_kernel, [like((TOK, WIDTH), BF16)] * 4, [*same, other], near=range(5), near_out=range(4), vmem=vmem)


def expert_weights_kernel(first, *refs):
    scal, rows = refs[0:2]
    mixes, grad_y, grad_q = refs[2:4], refs[4:6], refs[6:8]
    before = None if first else refs[8]
    after, own = refs[8 if first else 9 :]
    core = scal[0, 10]
    for side in range(2):
        for source in range(CHIPS):
            own[side, source * TOK : (source + 1) * TOK, :] = rows[
                rows_at(2 * source + (core if side == 0 else 1 - core)), :
            ]
    halves = (
        tn(own[0], grad_q[0][...]) + tn(own[1], grad_q[1][...]),
        tn(mixes[0][...], grad_y[0][...]) + tn(mixes[1][...], grad_y[1][...]),
    )
    for half, value in enumerate(halves):
        at = slice(half * WIDTH, (half + 1) * WIDTH)
        if not first:
            value = value + before[:, at]
        after[:, at] = value.astype(after.dtype)


def expert_weights(table, rows, mixes, grad_y, grad_q, before, last, vmem):
    first = before is None
    args = [table, rows, *mixes, *grad_y, *grad_q, *(() if first else (before,))]
    outs = [like((WIDTH, 2 * WIDTH), BF16 if last else F32)]
    return call(
        "expert_weights",
        functools.partial(expert_weights_kernel, first),
        outs,
        args,
        [pltpu.VMEM((2, HALF, WIDTH), BF16)],
        smem=(0,),
        flops=3 * 10**9,
        vmem=vmem,
    )[0]


def shared_weights_kernel(first, rows, grad_k, grad_v, *refs):
    after = refs[-1]
    for half, grad in enumerate((grad_k, grad_v)):
        at = slice(half * WIDTH, (half + 1) * WIDTH)
        value = tn(rows[...], grad[...])
        if not first:
            value = value + refs[0][:, at]
        after[:, at] = value.astype(after.dtype)


def shared_last_kernel(*refs):
    scal, far, outs = refs[0], refs[1:9], refs[9:11]
    held, (total, packed, in_sems, out_sems) = refs[11:19], refs[19:]
    rows_1, grad_k1, rows_0, grad_k0, before, grad_v1, grad_v0, tiny = held
    copies = [copy_in(far[n], held[n], in_sems.at[n]) for n in range(8)]
    for n in range(5):
        copies[n].wait()
    value = tn(rows_1[...], grad_k1[...]) + tn(rows_0[...], grad_k0[...])
    total[:, 0:WIDTH] = (value + before[:, 0:WIDTH]).astype(BF16)
    for n in range(5, 8):
        copies[n].wait()
    value = tn(rows_1[...], grad_v1[...]) + tn(rows_0[...], grad_v0[...])
    total[:, WIDTH : 2 * WIDTH] = (value + before[:, WIDTH : 2 * WIDTH]).astype(BF16)
    total[:, 2 * WIDTH :] = tiny[...].astype(BF16)
    row = iota((WIDTH, WIDTH), 0)
    side, hop, spot = row >> 8, (row >> 6) & 3, (row >> 2) & 15
    owner = ((scal[0, 9] + hop) & 3) * 2 + (side ^ scal[0, 10])
    source = spot * 32 + owner * 4 + (row & 3)
    pick = onehot(source == iota((WIDTH, WIDTH), 1))
    packed[...] = nn(pick, total[...]).astype(BF16).reshape(2, CHIPS, 64, SHARED)
    leaving = [copy_in(packed.at[n], outs[n], out_sems.at[n]) for n in range(2)]
    for copy in leaving:
        copy.wait()


def shared_last(table, step_1, step_0, before, tiny):
    (rows_1, grad_k1, grad_v1), (rows_0, grad_k0, grad_v0) = step_1, step_0
    args = [rows_1, grad_k1, rows_0, grad_k0, before, grad_v1, grad_v0, tiny]
    scratch = [pltpu.VMEM(a.shape, a.dtype) for a in args] + [
        pltpu.VMEM((WIDTH, SHARED), BF16),
        pltpu.VMEM((2, CHIPS, 64, SHARED), BF16),
        pltpu.SemaphoreType.DMA((8,)),
        pltpu.SemaphoreType.DMA((2,)),
    ]
    outs = [like((CHIPS, 64, SHARED), BF16)] * 2
    return call_any(
        "shared_last", shared_last_kernel, outs, [table, *args], scratch, 4 * 10**9, 60, (), ()
    )


def core_sum_kernel(mine, other, *outs):
    for hop in range(CHIPS):
        outs[hop][...] = (mine[hop].astype(F32) + other[hop].astype(F32)).astype(BF16)


def core_sum(mine, other):
    outs = [like((64, SHARED), BF16)] * CHIPS
    return call("core_sum", core_sum_kernel, outs, [mine, other], vmem=60)


def last_weights_kernel(*refs):
    scal, far, out = refs[0], refs[1:13], refs[13]
    held, (own, total, in_sems, out_sem) = refs[14:26], refs[26:]
    rows, q_0, q_1, expert_acc, mix_0, y_0, mix_1, y_1 = held[:8]
    parts = held[8:]
    copies = [copy_in(far[n], held[n], in_sems.at[n]) for n in range(12)]
    core = scal[0, 10]
    copies[0].wait()
    for side in range(2):
        for source in range(CHIPS):
            own[side, source * TOK : (source + 1) * TOK, :] = rows[
                rows_at(2 * source + (core if side == 0 else 1 - core)), :
            ]
    for n in range(1, 4):
        copies[n].wait()
    value = tn(own[0], q_0[...]) + tn(own[1], q_1[...]) + expert_acc[:, 0:WIDTH]
    total[:, 0:32, :] = value.astype(BF16).reshape(16, 32, WIDTH)
    for n in range(4, 8):
        copies[n].wait()
    value = tn(mix_0[...], y_0[...]) + tn(mix_1[...], y_1[...]) + expert_acc[:, WIDTH : 2 * WIDTH]
    total[:, 32:64, :] = value.astype(BF16).reshape(16, 32, WIDTH)
    for n in range(8, 12):
        copies[n].wait()
    summed = sum(p[...].astype(F32) for p in parts).astype(BF16)
    small = jnp.concatenate(
        [summed[:, 2 * WIDTH :], jnp.zeros((64, WIDTH - LANES), BF16)], 1
    )
    row, col = iota((256, 64), 0), iota((256, 64), 1)
    spread = jnp.zeros((256, WIDTH), F32)
    for n, value in enumerate((summed[:, 0:WIDTH], summed[:, WIDTH : 2 * WIDTH], small)):
        pick = onehot(((row >> 4) * 4 + (row & 15) - 4 * n == col) & (((row >> 2) & 3) == n))
        spread = spread + nn(pick, value)
    total[:, 64:80, :] = spread.astype(BF16).reshape(16, 16, WIDTH)
    copy_in(total, out, out_sem.at[0]).wait()


def last_weights(table, rows, mixes, grad_y, grad_q, expert_acc, parts):
    args = [rows, *grad_q, expert_acc, mixes[0], grad_y[0], mixes[1], grad_y[1], *parts]
    scratch = [pltpu.VMEM(a.shape, a.dtype) for a in args] + [
        pltpu.VMEM((2, HALF, WIDTH), BF16),
        pltpu.VMEM((16, 80, WIDTH), BF16),
        pltpu.SemaphoreType.DMA((12,)),
        pltpu.SemaphoreType.DMA((1,)),
    ]
    outs = [like((16, 80, WIDTH), BF16)]
    return call_any(
        "last_weights", last_weights_kernel, outs, [table, *args], scratch, 4 * 10**9, 60, (), ()
    )[0]


SHARED = 2 * WIDTH + LANES


def shared_weights(rows, grad_k, grad_v, before, vmem=20):
    first = before is None
    args = [rows, grad_k, grad_v, *(() if first else (before,))]
    outs = [like((WIDTH, 2 * WIDTH), F32)]
    kernel = functools.partial(shared_weights_kernel, first)
    return call("shared_weights", kernel, outs, args, flops=3 * 10**9, vmem=vmem)[0]


def slot_pick(shape, r, row_dim):
    row, col = iota(shape, row_dim), iota(shape, 1 - row_dim)
    skip = SLOTS * r
    for source in range(1, CHIPS):
        skip = skip + jnp.where(row >= SLOTS * source, SLOTS, 0)
    return onehot(col == row + skip)


ROWS = CHIPS * SLOTS
BLOCK = 2 * SLOTS


def gelu_parts(x):
    scale = 0.7978845608028654
    inner = scale * (x + 0.044715 * x * x * x)
    return jnp.tanh(inner), scale * (1.0 + 3.0 * 0.044715 * x * x)


def store_blocks(results, outs):
    full = sum(
        nn(slot_pick((2 * ROWS, ROWS), r, 1), results[r].astype(BF16)) for r in range(2)
    ).astype(BF16)
    for hop in range(CHIPS):
        outs[hop][...] = full[hop * BLOCK : (hop + 1) * BLOCK]


def hidden_at(step):
    return slice(step * PART, (step + 1) * PART)


def fetch_weights(win, wout, win_far, wout_far, sems):
    copies = []
    for step in range(FFN // PART):
        at = hidden_at(step)
        now = []
        for r in range(2):
            now.append((win_far[r].at[:, at], win.at[r, :, at]))
            now.append((wout_far[r].at[at, :], wout.at[r, at, :]))
        copies.append([copy_in(src, dst, sems.at[step, n]) for n, (src, dst) in enumerate(now)])
    return copies


def feed_kernel(*refs):
    blocks, win_far, wout_far = refs[0:4], refs[4:6], refs[6:8]
    outs, received_out = refs[8:12], refs[12:14]
    win, wout, received, weight_sems, out_sems = refs[14:]
    copies = fetch_weights(win, wout, win_far, wout_far, weight_sems)
    full = jnp.concatenate([b[...] for b in blocks], 0)
    leaving = []
    for r in range(2):
        received[r] = nn(slot_pick((ROWS, 2 * ROWS), r, 0), full).astype(BF16)
        leaving.append(copy_in(received.at[r], received_out[r], out_sems.at[r]))
    total = [jnp.zeros((ROWS, WIDTH), F32)] * 2
    for step in range(FFN // PART):
        at = hidden_at(step)
        for copy in copies[step]:
            copy.wait()
        for r in range(2):
            pre = nn(received[r], win[r, :, at])
            bend, _ = gelu_parts(pre)
            total[r] = total[r] + nn((0.5 * pre * (1.0 + bend)).astype(BF16), wout[r, at, :])
    store_blocks(total, outs)
    for copy in leaving:
        copy.wait()


NEAR = pl.BlockSpec(memory_space=pltpu.VMEM)


def feed(blocks, win, wout):
    return pl.pallas_call(
        feed_kernel,
        in_specs=[NEAR] * 4 + [FAR] * 4,
        out_specs=tuple([NEAR] * 4 + [FAR] * 2),
        out_shape=tuple([like((BLOCK, WIDTH), BF16)] * 4 + [like((ROWS, WIDTH), BF16)] * 2),
        scratch_shapes=[
            pltpu.VMEM((2, WIDTH, FFN), BF16),
            pltpu.VMEM((2, FFN, WIDTH), BF16),
            pltpu.VMEM((2, ROWS, WIDTH), BF16),
            pltpu.SemaphoreType.DMA((FFN // PART, 4)),
            pltpu.SemaphoreType.DMA((2,)),
        ],
        compiler_params=pltpu.CompilerParams(vmem_limit_bytes=24 * 2**20),
        cost_estimate=pl.CostEstimate(flops=2 * 10**9, bytes_accessed=10**7, transcendentals=10**6),
        name="feed",
    )(*blocks, *win, *wout)


def feed_back_kernel(*refs):
    blocks, received_far, win_far, wout_far = refs[0:4], refs[4:6], refs[6:8], refs[8:10]
    outs, rows_out, acts_out, pre_out = refs[10:14], refs[14:16], refs[16:18], refs[18:20]
    win, wout, received, grad_rows, acts, grad_pre = refs[20:26]
    weight_sems, in_sems, out_sems = refs[26:]
    arriving = [copy_in(received_far[r], received.at[r], in_sems.at[r]) for r in range(2)]
    copies = fetch_weights(win, wout, win_far, wout_far, weight_sems)
    full = jnp.concatenate([b[...] for b in blocks], 0)
    leaving = []
    for r in range(2):
        grad_rows[r] = nn(slot_pick((ROWS, 2 * ROWS), r, 0), full).astype(BF16)
        leaving.append(copy_in(grad_rows.at[r], rows_out[r], out_sems.at[r]))
    for copy in arriving:
        copy.wait()
    total = [jnp.zeros((ROWS, WIDTH), F32)] * 2
    for step in range(FFN // PART):
        at = hidden_at(step)
        for copy in copies[step]:
            copy.wait()
        for r in range(2):
            pre = nn(received[r], win[r, :, at])
            bend, slope = gelu_parts(pre)
            acts[r, :, at] = (0.5 * pre * (1.0 + bend)).astype(BF16)
            grad_act = nt(grad_rows[r], wout[r, at, :])
            inner = 0.5 * (1.0 + bend) + 0.5 * pre * (1.0 - bend * bend) * slope
            low = (grad_act * inner).astype(BF16)
            grad_pre[r, :, at] = low
            total[r] = total[r] + nt(low, win[r, :, at])
    for r in range(2):
        leaving.append(copy_in(acts.at[r], acts_out[r], out_sems.at[2 + r]))
        leaving.append(copy_in(grad_pre.at[r], pre_out[r], out_sems.at[4 + r]))
    store_blocks(total, outs)
    for copy in leaving:
        copy.wait()


def feed_back(blocks, received, win, wout):
    return pl.pallas_call(
        feed_back_kernel,
        in_specs=[NEAR] * 4 + [FAR] * 6,
        out_specs=tuple([NEAR] * 4 + [FAR] * 6),
        out_shape=tuple(
            [like((BLOCK, WIDTH), BF16)] * 4
            + [like((ROWS, WIDTH), BF16)] * 2
            + [like((ROWS, FFN), BF16)] * 4
        ),
        scratch_shapes=[
            pltpu.VMEM((2, WIDTH, FFN), BF16),
            pltpu.VMEM((2, FFN, WIDTH), BF16),
            pltpu.VMEM((2, ROWS, WIDTH), BF16),
            pltpu.VMEM((2, ROWS, WIDTH), BF16),
            pltpu.VMEM((2, ROWS, FFN), BF16),
            pltpu.VMEM((2, ROWS, FFN), BF16),
            pltpu.SemaphoreType.DMA((FFN // PART, 4)),
            pltpu.SemaphoreType.DMA((2,)),
            pltpu.SemaphoreType.DMA((6,)),
        ],
        compiler_params=pltpu.CompilerParams(vmem_limit_bytes=28 * 2**20),
        cost_estimate=pl.CostEstimate(flops=3 * 10**9, bytes_accessed=10**7, transcendentals=10**6),
        name="feed_back",
    )(*blocks, *received, *win, *wout)


def feed_weights_kernel(*refs):
    far, out = refs[0:24], refs[24]
    received, grad_rows, acts, grad_pre, total, in_sems, out_sem = refs[25:]
    held = (received, grad_pre, grad_rows, acts)
    copies = [
        [
            copy_in(far[6 * n + s], held[n].at[ROWS * s : ROWS * (s + 1)], in_sems.at[n, s])
            for s in range(6)
        ]
        for n in range(4)
    ]
    for copy in copies[0] + copies[1]:
        copy.wait()
    for step in range(FFN // PART):
        value = tn(received[...], grad_pre[:, hidden_at(step)]).astype(BF16)
        total[:, step * 32 : (step + 1) * 32, :] = value.reshape(16, 32, PART)
    for copy in copies[2] + copies[3]:
        copy.wait()
    for step in range(FFN // PART):
        value = tn(acts[:, hidden_at(step)], grad_rows[...]).astype(BF16)
        total[4 * step : 4 * step + 4, TOK : 2 * TOK, :] = value.reshape(4, TOK, WIDTH)
    leaving = copy_in(total, out, out_sem.at[0])
    leaving.wait()


def feed_weights(received, grad_rows, acts, grad_pre):
    return pl.pallas_call(
        feed_weights_kernel,
        in_specs=[FAR] * 24,
        out_specs=FAR,
        out_shape=like((16, 2 * TOK, WIDTH), BF16),
        scratch_shapes=[
            pltpu.VMEM((6 * ROWS, WIDTH), BF16),
            pltpu.VMEM((6 * ROWS, WIDTH), BF16),
            pltpu.VMEM((6 * ROWS, FFN), BF16),
            pltpu.VMEM((6 * ROWS, FFN), BF16),
            pltpu.VMEM((16, 2 * TOK, WIDTH), BF16),
            pltpu.SemaphoreType.DMA((4, 6)),
            pltpu.SemaphoreType.DMA((1,)),
        ],
        compiler_params=pltpu.CompilerParams(vmem_limit_bytes=60 * 2**20),
        cost_estimate=pl.CostEstimate(flops=8 * 10**9, bytes_accessed=2 * 10**7, transcendentals=0),
        name="feed_weights",
    )(*received, *grad_pre, *grad_rows, *acts)


def first_norm_kernel(block, gain, depth, wide, normed, payload, tail):
    value = block[...].astype(F32)
    wide[...] = value
    low = (norm_parts(value)[0] * gain[...]).astype(BF16)
    normed[...] = low
    payload[0:TOK, :] = low
    tail[...] = jnp.zeros_like(tail)
    tail[0:1, 0:TOK] = depth[...].astype(F32)
    payload[TOK : TOK + 16, :] = tail[...].astype(BF16)


def first_norm(block, gain, depth):
    outs = [
        like((TOK, WIDTH), F32),
        like((TOK, WIDTH), BF16),
        like((TOK + 16, WIDTH), BF16),
    ]
    scratch = [pltpu.VMEM((16, WIDTH), F32)]
    args = [block, gain, depth]
    return call("first_norm", first_norm_kernel, outs, args, scratch, near_out=(2,), vmem=60)


def attend_plan_kernel(steps, *refs):
    place, choices = refs[0], refs[1]
    blocks = refs[2:10] if 0 not in steps else ()
    outs = refs[2 + len(blocks) :]
    outs, (spots, named_all, depth_col, tails, sems) = outs[: 5 * len(steps)], outs[5 * len(steps) :]
    chip, core = place[0], place[1]
    dp_row, dp_col = place[2], place[3]
    token = iota((SEQ, LANES), 0)
    lanes = iota((SEQ, LANES), 1)
    held = ((token // TOK) % 2) == core
    if blocks:
        copies = [
            copy_in(ref.at[TOK : TOK + 16, 0:TOK], tails.at[n], sems.at[n])
            for n, ref in enumerate(blocks)
        ]
        for copy in copies:
            copy.wait()
        for hop in range(CHIPS):
            source = lax.rem(chip - hop + CHIPS, CHIPS)
            for side, n in ((core, hop), (1 - core, CHIPS + hop)):
                rows = tails[n].astype(F32)
                rows = jnp.concatenate([rows, jnp.zeros((TOK - 16, TOK), F32)], 0)
                depth_col[rows_at(source * 2 + side), :] = rows.T
    before = onehot(iota((SEQ, SEQ), 1) < iota((SEQ, SEQ), 0))
    for n, s in enumerate(steps):
        table, chosen_out, row_out, col_out, key_out = outs[5 * n : 5 * n + 5]
        turned = jnp.concatenate([choices[s].astype(F32), jnp.zeros((4, SEQ), F32)], 0).T
        named_here = named(turned.astype(I32), 4)
        named_all[...] = jnp.where(named_here, 1.0, 0.0)
        live = held[:, 0:1]
        if blocks:
            live = live & (depth_col[:, 0:1] > s + 0.5)
        live = jnp.where(live, 1.0, 0.0)
        hits = [
            row_sum(jnp.where(lanes == 2 * chip + side, named_all[...], 0.0)) * live
            for side in (core, 1 - core)
        ]
        count = hits[0] + hits[1]
        base = nn(before, jnp.broadcast_to(count, (SEQ, LANES)).astype(BF16))
        key_out[...] = base.astype(I32)
        spot = jnp.where(
            lanes == 0,
            jnp.where(hits[0] > 0, base, -1.0),
            jnp.where(hits[1] > 0, base + hits[0], -1.0),
        )
        spots[...] = jnp.where(lanes < 2, spot, -1.0)
        for source in range(CHIPS):
            at = slice(source * TOK, (source + 1) * TOK)
            chosen_out[at, :] = named_all[rows_at(2 * source + core), :]
            part = spots[rows_at(2 * source + core), :]
            col_out[at, :] = part.astype(I32)
            row_out[:, at] = part.T[:8].astype(I32)
        reach = jnp.sum(
            jnp.where(base <= (lanes * TOK + TOK - 1).astype(F32), 1.0, 0.0), 0, keepdims=True
        )
        total = jnp.sum(count, 0, keepdims=True).astype(I32)
        line = iota((8, LANES), 1)
        chunks = (reach.astype(I32) + (SPAN - 1)) // SPAN
        packed = (total + (TOK - 1)) // TOK
        short = (line == packed - 1) & (total - (packed - 1) * TOK <= TOK // 2)
        chunks = jnp.where(short, SMALL, chunks)
        table[...] = jnp.where(
            line < 8,
            chunks,
            packed,
        )
        for lane, value in ((9, chip), (10, core), (11, dp_row), (12, dp_col)):
            table[...] = jnp.where(line == lane, value, table[...])


def attend_plan(steps, place, choices, blocks):
    outs = [
        like((8, LANES), I32),
        like((HALF, LANES), F32),
        like((8, HALF), I32),
        like((HALF, LANES), I32),
        like((SEQ, LANES), I32),
    ] * len(steps)
    scratch = [pltpu.VMEM((SEQ, LANES), F32)] * 3
    scratch += [pltpu.VMEM((8, 16, TOK), BF16), pltpu.SemaphoreType.DMA((8,))]
    res = call(
        "attend_plan", functools.partial(attend_plan_kernel, steps), outs,
        [place, choices, *blocks], scratch, smem=(0,), raw=range(2, 10), flops=10**9, vmem=60,
    )
    names = ("table", "chosen", "pos_row", "pos_col", "key_pos")
    return [dict(zip(names, res[5 * n : 5 * n + 5])) for n in range(len(steps))]


def slot_plan_kernel(place, choices, depth, *outs):
    chip, core = place[0], place[1]
    depth_col = turned_row(depth[...])
    lanes = iota((TOK, LANES), 1)
    before = onehot(iota((TOK, TOK), 1) < iota((TOK, TOK), 0))
    hop = (lanes // 2 - chip + CHIPS) % CHIPS
    start = hop * BLOCK + jnp.where(lanes % 2 == core, 0, SLOTS)
    for s in range(3):
        turned = jnp.concatenate([choices[s].astype(F32), jnp.zeros((6, TOK), F32)], 0).T
        choice = turned.astype(I32)
        live = depth_col > s
        names = [lanes == choice[:, k : k + 1] for k in range(2)]
        hits = jnp.where((names[0] | names[1]) & live, 1.0, 0.0)
        spot = nn(before, hits.astype(BF16)) + start.astype(F32)
        table = jnp.full((TOK, LANES), -1.0, F32)
        for k in range(2):
            slot = jnp.where(live, row_sum(jnp.where(names[k], spot, 0.0)), -1.0)
            table = jnp.where(lanes == k, slot, table)
            table = jnp.where(lanes == 2 + k, choice[:, k : k + 1].astype(F32), table)
        outs[2 * s][...] = table.astype(I32)
        outs[2 * s + 1][...] = table.T[:8].astype(I32)


def slot_plan(place, choices, depth):
    outs = [like((TOK, LANES), I32), like((8, TOK), I32)] * 3
    res = call("slot_plan", slot_plan_kernel, outs, [place, choices, depth], smem=(0,))
    return list(res[0::2]), list(res[1::2])


def dispatch_kernel(*refs):
    state, parts = refs[0], refs[1:5]
    gain, router, slot_row, slot_col = refs[5:9]
    mixed_out, normed_out, gates_out = refs[9:12]
    sends = refs[12:16]
    mixed = state[...] + sum(p[...].astype(F32) for p in parts)
    mixed_out[...] = mixed
    normed = (norm_parts(mixed)[0] * gain[...]).astype(BF16)
    normed_out[...] = normed
    logits = nt(normed, router[...])
    picked = [column(logits, slot_col[:, 2 + k : 3 + k]) for k in range(2)]
    peak = jnp.maximum(picked[0], picked[1])
    weights = [jnp.exp(p - peak) for p in picked]
    total = weights[0] + weights[1]
    lanes = iota((TOK, LANES), 1)
    gates_out[...] = jnp.where(
        lanes == 0, weights[0] / total, jnp.where(lanes == 1, weights[1] / total, 0.0)
    )
    slots = iota((2 * ROWS, TOK), 0)
    hit = (slot_row[0:1, :] == slots) | (slot_row[1:2, :] == slots)
    full = nn(onehot(hit), normed).astype(BF16)
    for hop in range(CHIPS):
        sends[hop][...] = full[hop * BLOCK : (hop + 1) * BLOCK]


def dispatch(state, parts, gain, router, slot_row, slot_col):
    outs = [
        like((TOK, WIDTH), F32),
        like((TOK, WIDTH), BF16),
        like((TOK, LANES), F32),
    ] + [like((BLOCK, WIDTH), BF16)] * 4
    return call("dispatch", dispatch_kernel, outs, [state, *parts, gain, router, slot_row, slot_col], near=range(1, 5), near_out=range(3, 7))


def picked_rows(slot_col, returned):
    full = jnp.concatenate([b[...] for b in returned], 0)
    slots = iota((TOK, 2 * ROWS), 1)
    return [nn(onehot(slot_col[:, k : k + 1] == slots), full) for k in range(2)]


def next_state(mixed, state, gates, slot_col, rows):
    part = gates[:, 0:1] * rows[0] + gates[:, 1:2] * rows[1]
    return jnp.where(slot_col[:, 0:1] >= 0, mixed + part, state)


def advance_kernel(*refs):
    mixed, state, gates, slot_col = refs[0:4]
    returned, gain = refs[4:8], refs[8]
    state_out, normed_out = refs[9:11]
    rows = picked_rows(slot_col[...], returned)
    new = next_state(mixed[...], state[...], gates[...], slot_col[...], rows)
    state_out[...] = new
    normed_out[...] = (norm_parts(new)[0] * gain[...]).astype(BF16)


def advance(mixed, state, gates, slot_col, returned, gain):
    outs = [like((TOK, WIDTH), F32), like((TOK, WIDTH), BF16)]
    return call("advance", advance_kernel, outs, [mixed, state, gates, slot_col, *returned, gain], near=range(4, 8), near_out=(1,))


def send_grads(upstream, rows, gates, slot_row, slot_col, grad_z_out, gate_grads_out, sends):
    grad_z = jnp.where(slot_col[:, 0:1] >= 0, upstream, 0.0)
    grad_z_out[...] = grad_z
    lanes = iota((TOK, LANES), 1)
    gate_grads_out[...] = jnp.where(
        lanes == 0,
        row_sum(rows[0] * grad_z),
        jnp.where(lanes == 1, row_sum(rows[1] * grad_z), 0.0),
    )
    slots = iota((2 * ROWS, TOK), 0)
    full = sum(
        nn(onehot(slot_row[k : k + 1, :] == slots), (gates[:, k : k + 1] * grad_z).astype(BF16))
        for k in range(2)
    ).astype(BF16)
    for hop in range(CHIPS):
        sends[hop][...] = full[hop * BLOCK : (hop + 1) * BLOCK]


SEND_OUTS = [
    like((TOK, WIDTH), F32),
    like((TOK, LANES), F32),
] + [like((BLOCK, WIDTH), BF16)] * 4


def turn_kernel(*refs):
    mixed, state, gates, slot_col, slot_row = refs[0:5]
    returned = refs[5:9]
    first_state, halt, depth, cotangent = refs[9:13]
    output, coefs, tiny, upstream_out, grad_z, gate_grads = refs[13:19]
    sends = refs[19:23]
    rows = picked_rows(slot_col[...], returned)
    second = state[...]
    third = next_state(mixed[...], second, gates[...], slot_col[...], rows)
    first = first_state[...]
    vector = halt[...]
    grad = cotangent[...].astype(F32)
    p1 = jax.nn.sigmoid(row_sum(first * vector))
    p2 = jax.nn.sigmoid(row_sum(second * vector))
    a1, a2, a3 = row_sum(first * grad), row_sum(second * grad), row_sum(third * grad)
    steps = turned_row(depth[...])
    one, two, three = steps == 1, steps == 2, steps == 3
    c1 = jnp.where(one, 1.0, p1)
    c2 = jnp.where(one, 0.0, jnp.where(two, 1.0 - p1, p2 * (1.0 - p1)))
    c3 = jnp.where(three, (1.0 - p1) * (1.0 - p2), 0.0)
    output[...] = c1 * first + c2 * second + c3 * third
    d1 = jnp.where(
        two, a1 - a2, jnp.where(three, a1 - p2 * a2 - (1.0 - p2) * a3, 0.0)
    ) * (p1 * (1.0 - p1))
    d2 = jnp.where(three, (1.0 - p1) * (a2 - a3), 0.0) * (p2 * (1.0 - p2))
    tiny[...] = lane_of(jnp.sum(d1 * first + d2 * second, 0, keepdims=True), 25)
    lanes = iota((TOK, LANES), 1)
    table = jnp.zeros((TOK, LANES), F32)
    for lane, value in enumerate((c1, c2, c3, d1, d2)):
        table = jnp.where(lanes == lane, value, table)
    coefs[...] = table
    upstream = c3 * grad
    upstream_out[...] = upstream
    send_grads(upstream, rows, gates[...], slot_row[...], slot_col[...], grad_z, gate_grads, sends)


def turn(mixed, state, gates, slot_col, slot_row, returned, first_state, halt, depth, cotangent):
    outs = [
        like((TOK, WIDTH), F32),
        like((TOK, LANES), F32),
        like((WIDTH, LANES), F32),
        like((TOK, WIDTH), F32),
    ] + SEND_OUTS
    args = [mixed, state, gates, slot_col, slot_row, *returned, first_state, halt, depth, cotangent]
    return call("turn", turn_kernel, outs, args, near=range(5, 9), near_out=range(6, 10))


def moe_back_kernel(*refs):
    returned, slot_col, gates, gate_grads = refs[0:4], refs[4], refs[5], refs[6]
    normed, router, mixed, gain, grad_z, tiny = refs[7:13]
    grad_mixed, grad_low, tiny_out = refs[13:]
    full = jnp.concatenate([b[...] for b in returned], 0)
    slots = iota((TOK, 2 * ROWS), 1)
    hit = (slot_col[:, 0:1] == slots) | (slot_col[:, 1:2] == slots)
    grad_normed = nn(onehot(hit), full)
    weights, grads = gates[...], gate_grads[...]
    inner = row_sum(weights * grads)
    lanes = iota((TOK, LANES), 1)
    grad_logits = jnp.zeros((TOK, LANES), F32)
    for k in range(2):
        value = weights[:, k : k + 1] * (grads[:, k : k + 1] - inner)
        grad_logits = grad_logits + jnp.where(lanes == slot_col[:, 2 + k : 3 + k], value, 0.0)
    low = grad_logits.astype(BF16)
    grad_normed = grad_normed + nn(low, router[...])
    out, gain_part = norm_back(grad_normed, mixed[...], gain[...])
    out = out + grad_z[...]
    turned = jnp.concatenate([low[:, LANES - 16 :], low[:, : LANES - 16]], 1)
    tiny_out[...] = tiny[...] + tn(normed[...], turned) + lane_of(gain_part, 24)
    grad_mixed[...] = out
    grad_low[...] = out.astype(BF16)


def moe_back(returned, slot_col, gates, gate_grads, normed, router, mixed, gain, grad_z, tiny):
    outs = [
        like((TOK, WIDTH), F32),
        like((TOK, WIDTH), BF16),
        like((WIDTH, LANES), F32),
    ]
    args = [*returned, slot_col, gates, gate_grads, normed, router, mixed, gain, grad_z, tiny]
    return call("moe_back", moe_back_kernel, outs, args, near=range(4), near_out=(1,))


def retreat_kernel(step, *refs):
    parts = refs[0:4]
    state, gain, slot_col, upstream, grad_mixed = refs[4:9]
    rest = refs[9:]
    total = sum(p[...].astype(F32) for p in parts)
    out, _ = norm_back(total, state[...], gain[...])
    kept = jnp.where(slot_col[:, 0:1] >= 0, 0.0, upstream[...])
    carry = kept + grad_mixed[...] + out
    if step == 0:
        rest[0][...] = carry
        return
    cotangent, halt, coefs, gates, before_col, before_row = rest[0:6]
    returned = rest[6:10]
    upstream_out, grad_z, gate_grads_out = rest[10:13]
    sends = rest[13:17]
    table = coefs[...]
    carry = carry + column(table, step - 1) * cotangent[...].astype(F32)
    carry = carry + column(table, step + 2) * halt[...]
    upstream_out[...] = carry
    rows = picked_rows(before_col[...], returned)
    send_grads(
        carry, rows, gates[...], before_row[...], before_col[...], grad_z, gate_grads_out, sends
    )


def retreat(step, parts, args, extra):
    outs = [like((TOK, WIDTH), F32)] + (SEND_OUTS if step else [])
    return call(
        "retreat", functools.partial(retreat_kernel, step), outs, [*parts, *args, *extra],
        near=range(4), near_out=range(3, 7),
    )


def swap_core(rows):
    return lax.ppermute(rows, "expert", [(i, i ^ 1) for i in range(2 * CHIPS)])


def shift_chip(rows, hops):
    count = 2 * CHIPS
    return lax.ppermute(rows, "expert", [(i, (i + 2 * hops) % count) for i in range(count)])


def send_blocks(blocks):
    return [blocks[0]] + [shift_chip(blocks[d], d) for d in (1, 2, 3)]


def after(value, other):
    return lax.optimization_barrier((value, other))


def return_blocks(blocks):
    return [blocks[0]] + [shift_chip(blocks[d], CHIPS - d) for d in (1, 2, 3)]


def spread_rows(rows):
    return [rows] + [shift_chip(rows, d) for d in (1, 2, 3)]


def dp_move(blocks):
    return lax.all_to_all(blocks, "dp", split_axis=0, concat_axis=0, tiled=True)


def block_sum(blocks):
    return jnp.sum(blocks.astype(F32), 0)


def local(
    block_input,
    gain_one,
    gain_two,
    moa_router,
    key_proj,
    value_proj,
    query_proj,
    out_proj,
    moe_router,
    ffn_in,
    ffn_out,
    halt_weight,
    depths,
    moa_choice,
    moe_choice,
    cotangent,
):
    member = lax.axis_index("expert")
    spot = lax.axis_index("dp")
    place = jnp.stack([member // 2, member % 2, spot // 4, spot % 4]).astype(I32)
    gain_a, gain_b = gain_one[None, :], gain_two[None, :]
    halt = halt_weight[None, :]
    router_a = jnp.pad(moa_router.T, ((0, LANES - 8), (0, 0)))
    router_b = jnp.pad(moe_router.T, ((0, LANES - 8), (0, 0)))
    depth = depths[None, :]
    moa_rows, moe_rows = moa_choice.swapaxes(1, 2), moe_choice.swapaxes(1, 2)

    state, normed, payload = first_norm(block_input, gain_a, depth)
    same = spread_rows(payload)
    same[1], place_late = after(same[1], place)
    plan = attend_plan((0,), place_late, moa_rows, ())
    same[2], plan[0]["table"] = after(same[2], plan[0]["table"])
    query_w = [query_proj[0], swap_core(query_proj[0])]
    out_w = [out_proj[0], swap_core(out_proj[0])]
    other = [swap_core(rows) for rows in same]
    slot_cols = slot_rows = None
    win = wout = None

    kept = []
    states = [state]
    for s in range(3):
        if s:
            same = spread_rows(normed)
            other = [swap_core(rows) for rows in same]
        p = plan[s]
        res = attend(
            p["table"], same, other, key_proj, value_proj, query_w, out_w, router_a, p,
            60,
        )
        parts = send_blocks(res[:4])
        if s == 0:
            parts[1], place_late = after(parts[1], place)
            slot_cols, slot_rows = slot_plan(place_late, moe_rows, depth)
            parts[2], slot_cols[0] = after(parts[2], slot_cols[0])
            win = [ffn_in[0], swap_core(ffn_in[0])]
            wout = [ffn_out[0], swap_core(ffn_out[0])]
            tails = (*same, *other)
        mixed, normed_b, gates, *sends = dispatch(
            state, parts, gain_b, router_b, slot_rows[s], slot_cols[s]
        )
        *sends, mine, others = feed(send_blocks(sends), win, wout)
        returned = return_blocks(sends)
        if s < 2:
            returned[1], place_late = after(returned[1], place)
            plan = plan + attend_plan((s + 1,), place_late, moa_rows, tails)
            returned[2], plan[s + 1]["table"] = after(returned[2], plan[s + 1]["table"])
        *saved, spread_0, spread_1, lse, weights = res[4:]
        kept.append(
            dict(
                normed=normed, rows=saved[0], mixed=mixed, normed_b=normed_b, gates=gates,
                attend=(*saved[1:], spread_0, spread_1, lse, weights),
                mixes=(spread_0, swap_core(spread_1)),
                received=(mine, others), returned=returned, state=state,
                received_all=(mine, swap_core(others)),
            )
        )
        if s < 2:
            state, normed = advance(mixed, state, gates, slot_cols[s], returned, gain_a)
            states.append(state)

    output, coefs, tiny, upstream, grad_z, gate_grads, *sends = turn(
        mixed, state, gates, slot_cols[2], slot_rows[2], returned, states[1], halt, depth, cotangent
    )
    expert_acc = shared_acc = pending = None
    received, acts, grad_pres, grad_rows = [], [], [], []
    for s in (2, 1, 0):
        k, p = kept[s], plan[s]
        table = p["table"]
        *sends, rows_0, rows_1, act_0, act_1, pre_0, pre_1 = feed_back(
            send_blocks(sends), k["received"], win, wout
        )
        back = return_blocks(sends)
        if pending and s:
            back[1], grad_k = after(back[1], pending[1])
            shared_acc = shared_weights(pending[0], grad_k, pending[2], shared_acc)
            back[2], shared_acc = after(back[2], shared_acc)
        received += k["received_all"]
        acts += [act_0, swap_core(act_1)]
        grad_pres += [pre_0, swap_core(pre_1)]
        grad_rows += [rows_0, swap_core(rows_1)]
        if s == 0:
            feed_grads = feed_weights(received, grad_rows, acts, grad_pres)
            back[2], feed_grads = after(back[2], feed_grads)
            feed_grads = dp_move(feed_grads)
        grad_mixed, grad_low, tiny = moe_back(
            back, slot_cols[s], k["gates"], gate_grads, k["normed_b"], router_b, k["mixed"],
            gain_b, grad_z, tiny,
        )
        limit = 20 if s else 60
        arrived = spread_rows(grad_low)
        *same, other, y_0, y_1, q_0, q_1, grad_k, grad_v, tiny = attend_back(
            table, arrived, k["attend"], key_proj, value_proj, query_w, out_w, p,
            (k["rows"], router_a, gain_a, tiny), 36 if s else 60,
        )
        other = swap_core(other)
        if s:
            parts = send_blocks(pair_sum(same, other, limit))
            parts[1], q_0 = after(parts[1], q_0)
        if s:
            expert_acc = expert_weights(
                table, k["rows"], k["mixes"], (y_0, swap_core(y_1)), (q_0, swap_core(q_1)),
                expert_acc, False, 20,
            )
            parts[2], expert_acc = after(parts[2], expert_acc)
            pending = (k["rows"], grad_k, grad_v)
        else:
            mine, others = shared_last(
                table, pending, (k["rows"], grad_k, grad_v), shared_acc, tiny
            )
            shared = send_blocks(core_sum(mine, swap_core(others)))
            parts = send_blocks(pair_sum(same, other, limit))
            weights_last = last_weights(
                table, k["rows"], k["mixes"], (y_0, swap_core(y_1)), (q_0, swap_core(q_1)),
                expert_acc, shared,
            )
            weights_last, feed_grads, *parts = lax.optimization_barrier(
                (weights_last, feed_grads, *parts)
            )
            moved = dp_move(weights_last)
        args = (k["state"], gain_a, slot_cols[s], upstream, grad_mixed)
        if s:
            b = kept[s - 1]
            extra = (
                cotangent, halt, coefs, b["gates"], slot_cols[s - 1], slot_rows[s - 1],
                *b["returned"],
            )
            upstream, grad_z, gate_grads, *sends = retreat(s, parts, args, extra)
        else:
            (grad_input,) = retreat(s, parts, args, ())

    summed = block_sum(moved)
    tiny = summed[72:76]
    feed_grads = block_sum(feed_grads)
    grad_in = feed_grads[:TOK].reshape(4, 32, PART).swapaxes(0, 1).reshape(32, FFN)
    grad_out = feed_grads[TOK:]
    return (
        output,
        grad_input,
        tiny[:, 8],
        tiny[:, 24],
        tiny[:, :8],
        summed[64:68],
        summed[68:72],
        summed[0:32][None],
        summed[32:64][None],
        tiny[:, 16:24],
        grad_in[None],
        grad_out[None],
        tiny[:, 25],
    )


def solution(mesh):
    in_specs = (
        P(("dp", "expert"), None),
        P(),
        P(),
        P(),
        P(),
        P(),
        P("expert", None, None),
        P("expert", None, None),
        P(),
        P("expert", None, None),
        P("expert", None, None),
        P(),
        P(("dp", "expert")),
        P(None, "dp", None),
        P(None, ("dp", "expert"), None),
        P(("dp", "expert"), None),
    )
    out_specs = (
        P(("dp", "expert"), None),
        P(("dp", "expert"), None),
        P(("dp", "expert")),
        P(("dp", "expert")),
        P(("dp", "expert"), None),
        P(("dp", "expert"), None),
        P(("dp", "expert"), None),
        P("expert", "dp", None),
        P("expert", "dp", None),
        P(("dp", "expert"), None),
        P("expert", "dp", None),
        P("expert", "dp", None),
        P(("dp", "expert")),
    )
    return jax.shard_map(local, mesh=mesh, in_specs=in_specs, out_specs=out_specs, check_vma=False)
```
